256 devices in a mesh: section: 2 (over core), tensor: 8 (over z), shard: 16 (over y, x).
Axes of the slice: x: 4, y: 4, z: 8, core: 2. Of those that a mesh axis runs over, the one named last changes fastest.
Arguments:
- embeds: bfloat16 [16, 256, 4096], P('shard', 'tensor'), may hold values from -6 to 6
- segments: int32 [16, 256], P('shard'), may hold values from 0 to 7, never falling along the last dimension, each value on 1 to 64 neighbouring positions
- rel_table: float32 [32, 32], P(None, 'tensor'), may hold values from -320 to 320
- attn_gain: float32 [2, 4096], P('section'), may hold values from 0.25 to 1.75
- w_query: bfloat16 [2, 4096, 2048], P('section', None, 'tensor'), may hold values from -0.01171875 to 0.01171875
- w_key: bfloat16 [2, 4096, 2048], P('section', None, 'tensor'), may hold values from -0.09375 to 0.09375
- w_value: bfloat16 [2, 4096, 2048], P('section', None, 'tensor'), may hold values from -0.09375 to 0.09375
- w_out: bfloat16 [2, 2048, 4096], P('section', 'tensor'), may hold values from -0.125 to 0.125
- ffn_gain: float32 [2, 4096], P('section'), may hold values from 0.25 to 1.75
- w_gate: bfloat16 [2, 4096, 5120], P('section', 'shard', 'tensor'), may hold values from -0.09375 to 0.09375
- w_up: bfloat16 [2, 4096, 5120], P('section', 'shard', 'tensor'), may hold values from -0.09375 to 0.09375
- w_down: bfloat16 [2, 5120, 4096], P('section', 'tensor', 'shard'), may hold values from -0.078125 to 0.078125
- final_gain: float32 [4096], replicated, may hold values from 0.25 to 1.75
- w_proj: bfloat16 [4096, 768], P('tensor'), may hold values from -0.09375 to 0.09375
- dest_shard: int32 [16, 8], P('shard'), may hold values from 0 to 31, as said below
- dest_slot: int32 [16, 8], P('shard'), may hold values from 0 to 3
Outputs:
- index: bfloat16 [128, 768], P(('section', 'shard'))
The draws below stay inside these ranges and needn't reach their ends.
Inputs may be any that keep to these rules, and one draw needn't show every extreme that they name: `segments`: within a pack the passage number never falls, and each of the 8 passages has 1 to 64 tokens. `dest_shard`: together with dest_slot, each of the 128 index slots receives exactly one passage.
All inputs are finite; a program needn't handle non-finite values.
Results may differ from the reference program's by a relative error of at most 0.033.
Values may be sent and summed in bfloat16 or wider, within the bound.
A program may use at most 128 MiB of HBM per device.

```python
import math
import jax
import jax.numpy as jnp
import numpy as np
from jax import lax

D = 4096
HEADS = 32
HD = 64
FF = 5120
E = 768
SEQ = 256
PPM = 8
LMAX = 64
BUCKETS = 32
BATCHES = 16
OWNERS = 32
SLOTS = 4
N_SECTION = 2
N_TENSOR = 8


def routing(key):
    ordering = jax.random.permutation(key, BATCHES * PPM)
    return ordering.reshape(BATCHES, PPM).astype(jnp.int32)


def draw_dest_shard(key, part):
    ordering = routing(key)
    return ordering // SLOTS


def draw_dest_slot(key, part):
    ordering = routing(key)
    return ordering % SLOTS


def draw_rel_table(key, part):
    key = jax.random.fold_in(key, 7)
    base_key = jax.random.fold_in(key, 0)
    return 2.0 * jax.random.truncated_normal(base_key, -4.0, 4.0, (BUCKETS, HEADS), jnp.float32)


def block_levels(own_key, shape, shards, least, top_value):
    gain = 1.0
    for axis_at, parts in shards:
        steps = jax.random.uniform(jax.random.fold_in(jax.random.fold_in(own_key, 6), axis_at), (parts,), jnp.float32, least / len(shards), top_value / len(shards))
        gain = gain * jnp.repeat(jnp.exp(steps), shape[axis_at] // parts).reshape((-1,) + (1,) * (len(shape) - 1 - axis_at))
    return gain


def split_up(amount, total, bound, skew):
    portions = [(1 << 20) // math.isqrt(rank ** skew) + 1 for rank in range(2, amount + 1)]
    spare, given = total - bound - (amount - 1), [1] * (amount - 1)
    while spare > 0:
        movable = [i for i in range(amount - 1) if given[i] < bound]
        mass, budget = sum([portions[i] for i in movable]), spare
        for i in movable:
            more = min(bound - given[i], max(1, budget * portions[i] // mass), spare)
            given[i] = given[i] + more
            spare = spare - more
    return np.array([bound] + given)


def uneven_parts(stream_key, number_of, total, reach, slope):
    if number_of == 2:
        one = jax.random.randint(stream_key, (), max(1, total - reach), min(reach, total - 1) + 1)
        return jnp.stack([one, total - one])
    tallies = jnp.asarray(split_up(number_of, total, reach, slope), jnp.int32)
    twos = (number_of - 1) // 2
    source_of, taker = tallies[1:1 + 2 * twos:2], tallies[2:2 + 2 * twos:2]
    margin = jnp.minimum(source_of - 1, reach - taker)
    moved = jax.random.randint(jax.random.fold_in(stream_key, 1), (twos,), 0, 1 << 20) % (margin + 1)
    tallies = tallies.at[1:1 + 2 * twos:2].set(source_of - moved).at[2:2 + 2 * twos:2].set(taker + moved)
    return tallies[jax.random.permutation(jax.random.fold_in(stream_key, 2), number_of)]


def normal_values(stream_key, shape, scale, reach, cuts=(), kind=jnp.bfloat16):
    drawn = scale * jax.random.normal(stream_key, shape, jnp.float32)
    if cuts:
        drawn = drawn * block_levels(stream_key, shape, cuts, -0.22, 0.18)
    return jnp.clip(drawn, -reach, reach).astype(kind)


def setup_inputs(seed: int = 0) -> dict:
    keys = jax.random.split(jax.random.key(seed), 17)
    embeds = normal_values(keys[0], (BATCHES, SEQ, D), 1.0, 6.0, ((0, 16), (1, 8)))
    segments = jax.vmap(lambda own: jnp.searchsorted(jnp.cumsum(uneven_parts(own, PPM, SEQ, LMAX, 2)), jnp.arange(SEQ), side="right"))(jax.random.split(keys[1], BATCHES)).reshape((BATCHES, SEQ)).astype(jnp.int32)
    rel_table = draw_rel_table(jax.random.fold_in(keys[16], 71), 0)
    attn_gain = jnp.clip(1.0 + 0.15 * jax.random.normal(keys[3], (N_SECTION, D), jnp.float32), 0.25, 1.75)
    w_query = normal_values(keys[4], (N_SECTION, D, HEADS * HD), (D * HD) ** -0.5, 0.01171875, ((0, 2), (2, 8)))
    w_key = normal_values(keys[5], (N_SECTION, D, HEADS * HD), D ** -0.5, 0.09375, ((0, 2), (2, 8)))
    w_value = normal_values(keys[6], (N_SECTION, D, HEADS * HD), D ** -0.5, 0.09375, ((0, 2), (2, 8)))
    w_out = normal_values(keys[7], (N_SECTION, HEADS * HD, D), (HEADS * HD) ** -0.5, 0.125, ((0, 2), (1, 8)))
    ffn_gain = jnp.clip(1.0 + 0.15 * jax.random.normal(keys[8], (N_SECTION, D), jnp.float32), 0.25, 1.75)
    w_gate = normal_values(keys[9], (N_SECTION, D, FF), D ** -0.5, 0.09375, ((0, 2), (1, 16), (2, 8)))
    w_up = normal_values(keys[10], (N_SECTION, D, FF), D ** -0.5, 0.09375, ((0, 2), (1, 16), (2, 8)))
    w_down = normal_values(keys[11], (N_SECTION, FF, D), FF ** -0.5, 0.078125, ((0, 2), (1, 8), (2, 16)))
    final_gain = jnp.clip(1.0 + 0.15 * jax.random.normal(keys[12], (D,), jnp.float32), 0.25, 1.75)
    w_proj = normal_values(keys[13], (D, E), D ** -0.5, 0.09375, ((0, 8),))
    dest_shard = draw_dest_shard(jax.random.fold_in(keys[16], 71), 0)
    dest_slot = draw_dest_slot(jax.random.fold_in(keys[16], 71), 0)
    return {"embeds": embeds, "segments": segments, "rel_table": rel_table, "attn_gain": attn_gain, "w_query": w_query, "w_key": w_key, "w_value": w_value, "w_out": w_out, "ffn_gain": ffn_gain, "w_gate": w_gate, "w_up": w_up, "w_down": w_down, "final_gain": final_gain, "w_proj": w_proj, "dest_shard": dest_shard, "dest_slot": dest_slot}


bucket_edges = (12, 16, 23, 32, 46, 64, 91)

def buckets(length):
    position = jnp.arange(length, dtype=jnp.int32)
    relative = position[None, :] - position[:, None]
    forward = (relative > 0).astype(jnp.int32) * 16
    distance = jnp.abs(relative)
    far_code = 8 + sum(((distance >= boundary).astype(jnp.int32) for boundary in bucket_edges))
    return forward + jnp.where(distance < 8, distance, far_code)

def rms_scale(source, norm_gain):
    floats = source.astype(jnp.float32)
    mean_square = lax.optimization_barrier(jnp.mean(floats * floats, axis=-1, keepdims=True))
    return floats * lax.rsqrt(mean_square + 1e-06) * norm_gain

def grouped_sum(inputs, weights, groups):
    batch_count, length, inner = inputs.shape
    split_inputs = inputs.astype(jnp.float32).reshape(batch_count, length, groups, inner // groups)
    split_weights = weights.astype(jnp.float32).reshape(groups, inner // groups, weights.shape[1])
    partial_value = jnp.einsum('bsgi,gid->bgsd', split_inputs, split_weights)
    rounded = lax.optimization_barrier(partial_value.astype(jnp.bfloat16))
    return lax.optimization_barrier(jnp.sum(rounded.astype(jnp.float32), axis=1))

def reference(embeds, segments, rel_table, attn_gain, w_query, w_key, w_value, w_out, ffn_gain, w_gate, w_up, w_down, final_gain, w_proj, dest_shard, dest_slot):
    hidden = embeds
    position_bias = jnp.transpose(rel_table[buckets(SEQ)], (2, 0, 1))
    same_passage = segments[:, :, None] == segments[:, None, :]
    batch_count = embeds.shape[0]
    for layer_index in range(N_SECTION):
        normed = rms_scale(hidden, attn_gain[layer_index]).astype(jnp.bfloat16)
        normed_f = normed.astype(jnp.float32)
        queries = jnp.einsum('bsd,de->bse', normed_f, w_query[layer_index].astype(jnp.float32)).astype(jnp.bfloat16)
        keys_all = jnp.einsum('bsd,de->bse', normed_f, w_key[layer_index].astype(jnp.float32)).astype(jnp.bfloat16)
        values = jnp.einsum('bsd,de->bse', normed_f, w_value[layer_index].astype(jnp.float32)).astype(jnp.bfloat16)
        queries = queries.reshape(batch_count, SEQ, HEADS, HD).astype(jnp.float32)
        keys_all = keys_all.reshape(batch_count, SEQ, HEADS, HD).astype(jnp.float32)
        values = values.reshape(batch_count, SEQ, HEADS, HD).astype(jnp.float32)
        scores = jnp.einsum('bqhd,bkhd->bhqk', queries, keys_all) + position_bias[None]
        scores = jnp.where(same_passage[:, None], scores, -1e+30)
        row_max = lax.optimization_barrier(jnp.max(scores, axis=-1, keepdims=True))
        weights = jnp.exp(scores - row_max)
        probabilities = (weights / lax.optimization_barrier(jnp.sum(weights, axis=-1, keepdims=True))).astype(jnp.bfloat16)
        context = jnp.einsum('bhqk,bkhd->bqhd', probabilities.astype(jnp.float32), values)
        context = context.astype(jnp.bfloat16).reshape(batch_count, SEQ, HEADS * HD)
        attended = grouped_sum(context, w_out[layer_index], N_TENSOR)
        hidden = (hidden.astype(jnp.float32) + attended).astype(jnp.bfloat16)
        normed2 = rms_scale(hidden, ffn_gain[layer_index]).astype(jnp.bfloat16).astype(jnp.float32)
        gate_part = jnp.einsum('bsd,df->bsf', normed2, w_gate[layer_index].astype(jnp.float32))
        up_part = jnp.einsum('bsd,df->bsf', normed2, w_up[layer_index].astype(jnp.float32))
        activation = (jax.nn.gelu(gate_part, approximate=True) * up_part).astype(jnp.bfloat16)
        fed = grouped_sum(activation, w_down[layer_index], N_TENSOR)
        hidden = (hidden.astype(jnp.float32) + fed).astype(jnp.bfloat16)
    finished = rms_scale(hidden, final_gain)
    member = (segments[:, None, :] == jnp.arange(PPM, dtype=jnp.int32)[None, :, None]).astype(jnp.float32)
    sums = jnp.einsum('bps,bsd->bpd', member, finished, precision=lax.Precision.HIGHEST)
    counts = lax.optimization_barrier(jnp.sum(member, axis=-1))[..., None]
    pooled = (sums / counts).astype(jnp.bfloat16).reshape(batch_count * PPM, D)
    projected = jnp.dot(pooled, w_proj, preferred_element_type=jnp.float32)
    unit = projected * lax.rsqrt(lax.optimization_barrier(jnp.mean(projected * projected, axis=-1, keepdims=True)) + 1e-06)
    target = (dest_shard * SLOTS + dest_slot).reshape(-1).astype(jnp.int32)
    index = jnp.zeros((OWNERS * SLOTS, E), jnp.float32).at[target].set(unit)
    return index.astype(jnp.bfloat16)
```

```python
import functools

import jax
import jax.numpy as jnp
from jax import lax
from jax.experimental import pallas as pl
from jax.experimental.pallas import tpu as pltpu
from jax.sharding import PartitionSpec as P

MESH = pl.DeviceIdType.MESH
F32 = jnp.float32
BF16 = jnp.bfloat16
HIGHEST = lax.Precision.HIGHEST

ROWS = 32
CHUNK = 16
RINGZ = 8
SIDE = 4
SHARDS = SIDE * SIDE
WIDTH = 4096
SEQ = 256
HEADS = 4
PPM = 8
DK = 256
HID = 640
EMB = 768
HALF = EMB // 2
PCOLS = WIDTH // RINGZ
EPS = 1e-06

lowest = (0, 1, 2, 3, 4, 5, 6, 7, 8, 12, 16, 23, 32, 46, 64, 91)


def copy_to(src, dst, send, recv, device):
    return pltpu.make_async_remote_copy(
        src_ref=src,
        dst_ref=dst,
        send_sem=send,
        recv_sem=recv,
        device_id=device,
        device_id_type=MESH,
    )


def normed(rows, gain):
    mean_square = jnp.mean(rows * rows, axis=-1, keepdims=True)
    return rows * lax.rsqrt(mean_square + EPS) * gain


def gather_rows(z, blocks, send, recv):
    right, left = lax.rem(z + 1, RINGZ), lax.rem(z + RINGZ - 1, RINGZ)

    def going(way, step, c):
        back = step - 1
        owner = lax.rem(z + RINGZ - back, RINGZ) if way == 0 else lax.rem(z + back, RINGZ)
        at = (way * 4 + step - 1) * 2 + c
        ref = blocks.at[2 * owner + c]
        return copy_to(ref, ref, send.at[at], recv.at[at], {"tensor": right if way == 0 else left})

    def coming(way, step, c):
        owner = lax.rem(z + RINGZ - step, RINGZ) if way == 0 else lax.rem(z + step, RINGZ)
        at = (way * 4 + step - 1) * 2 + c
        ref = blocks.at[2 * owner + c]
        return copy_to(ref, ref, send.at[at], recv.at[at], {"tensor": right if way == 0 else left})

    sent = []
    for step in (1, 2, 3):
        for c in (0, 1):
            for way in (0, 1):
                if step > 1:
                    coming(way, step - 1, c).wait_recv()
                moving = going(way, step, c)
                moving.start()
                sent.append(moving)
    for way in (0, 1):
        coming(way, 3, way).wait_recv()
        moving = going(way, 4, way)
        moving.start()
        sent.append(moving)
    for way in (0, 1):
        coming(way, 3, 1 - way).wait_recv()
    for way in (0, 1):
        coming(way, 4, way).wait_recv()
    return sent


def sum_rows(z, parts, landed, send, recv):
    right, left = lax.rem(z + 1, RINGZ), lax.rem(z + RINGZ - 1, RINGZ)

    def place(way, step, c):
        return way * 8 + (step - 1) * 2 + c

    def going(way, step, c):
        ahead = 5 - step
        owner = lax.rem(z + ahead, RINGZ) if way == 0 else lax.rem(z + RINGZ - ahead, RINGZ)
        at = place(way, step, c)
        index = 2 * owner + c
        return index, copy_to(
            parts.at[index],
            landed.at[at],
            send.at[at],
            recv.at[at],
            {"tensor": right if way == 0 else left},
        )

    def arrived(way, step, c):
        going(way, step, c)[1].wait_recv()
        return landed[place(way, step, c)].astype(F32)

    sent = []

    def forward(way, step, c, adds):
        index, moving = going(way, step, c)
        if adds:
            total = parts[index].astype(F32) + arrived(way, step - 1, c)
            parts[index] = total.astype(BF16)
        moving.start()
        sent.append(moving)

    for way in (0, 1):
        forward(way, 1, way, False)
    for way in (0, 1):
        forward(way, 2, 1 - way, False)
    for way in (0, 1):
        forward(way, 2, way, True)
    for step in (3, 4):
        for first in (1, 0):
            for way in (0, 1):
                forward(way, step, way if first == 0 else 1 - way, True)

    def total(c):
        own = parts[2 * z + c].astype(F32)
        return own + arrived(0, 4, c) + arrived(1, 4, c)

    return sent, total


def gather_weights(y, x, gate, up, down, send, recv):
    def neighbour(axis, sign):
        step = 1 if sign == 0 else SIDE - 1
        if axis == 0:
            return {"shard": y * SIDE + lax.rem(x + step, SIDE)}
        return {"shard": lax.rem(y + step, SIDE) * SIDE + x}

    def behind(axis, sign):
        step = SIDE - 1 if sign == 0 else 1
        return lax.rem((x if axis == 0 else y) + step, SIDE)

    halves = {0: (0, DK // 2), 1: (DK // 2, DK // 2)}
    part = HID // 2
    quarter = HID // 4

    def pieces(array, at_y, at_x, sign):
        if array == 0:
            lead = gate.at[at_y] if at_x is None else gate.at[at_y, at_x]
            start, size = (0, DK) if sign is None else halves[sign]
        elif array == 1:
            lead = up.at[:, at_x] if at_y is None else up.at[at_y, at_x]
            start, size = (0, DK) if sign is None else halves[sign]
        else:
            if at_x is None:
                lead = down.at[at_y]
            elif at_y is None:
                lead = down.at[:, at_x]
            else:
                lead = down.at[at_y, at_x]
            base = 0 if array == 2 else part
            start, size = (base, part) if sign is None else (base + sign * quarter, quarter)
        rows = pl.ds(start, size)
        return lead.at[rows] if at_x is not None and at_y is not None else lead.at[:, rows]

    sent = []
    first_axis = {0: 0, 2: 0, 1: 1, 3: 1}

    def where(array, axis, coordinate, stage):
        if axis == 0:
            return (y if stage == 0 else None, coordinate)
        return (coordinate, x if stage == 0 else None)

    def move(stage, hop, array, sign):
        axis = first_axis[array] if stage == 0 else 1 - first_axis[array]
        at = ((stage * 2 + hop) * 4 + array) * 2 + sign
        own = x if axis == 0 else y
        coordinate = own if hop == 0 else behind(axis, sign)
        ref = pieces(array, *where(array, axis, coordinate, stage), None if hop == 0 else sign)
        return copy_to(ref, ref, send.at[at], recv.at[at], neighbour(axis, sign))

    def landing(stage, hop, array, sign):
        axis = first_axis[array] if stage == 0 else 1 - first_axis[array]
        at = ((stage * 2 + hop) * 4 + array) * 2 + sign
        own = x if axis == 0 else y
        coordinate = behind(axis, sign) if hop == 0 else lax.rem(own + 2, SIDE)
        ref = pieces(array, *where(array, axis, coordinate, stage), None if hop == 0 else sign)
        return copy_to(ref, ref, send.at[at], recv.at[at], neighbour(axis, sign))

    for stage in (0, 1):
        for hop in (0, 1):
            for array in range(4):
                for sign in (0, 1):
                    if hop == 1:
                        landing(stage, 0, array, sign).wait_recv()
                    moving = move(stage, hop, array, sign)
                    moving.start()
                    sent.append(moving)
        for array in range(4):
            for sign in (0, 1):
                landing(stage, 1, array, sign).wait_recv()
    for moving in sent:
        moving.wait_send()


def kernel(
    embeds,
    segments,
    segments_s,
    rel_s,
    attn_gain,
    w_query,
    w_key,
    w_value,
    w_out,
    ffn_gain,
    w_gate,
    w_up,
    w_down,
    final_gain,
    w_proj,
    dest_shard,
    dest_slot,
    index,
    query_w,
    key_w,
    value_w,
    out_w,
    proj_w,
    gate_w,
    up_w,
    down_w,
    bias,
    member_here,
    attn_rows,
    attn_parts,
    attn_landed,
    ffn_rows,
    ffn_parts,
    ffn_landed,
    attn_in,
    handed,
    ffn_in,
    gain_in,
    queries,
    keys,
    values,
    context,
    sums,
    hidden,
    pooled,
    pooled_in,
    shares,
    placed,
    placed_in,
    load_sem,
    swap_send,
    swap_recv,
    hand_send,
    hand_recv,
    ag_send,
    ag_recv,
    rs_send,
    rs_recv,
    w_send,
    w_recv,
    pool_send,
    pool_recv,
    share_send,
    share_recv,
    place_send,
    place_recv,
):
    section = lax.axis_index("section")
    z = lax.axis_index("tensor")
    shard = lax.axis_index("shard")
    y, x = shard // SIDE, lax.rem(shard, SIDE)
    other = 1 - section

    barrier = pltpu.get_barrier_semaphore()

    def greet(device):
        pl.semaphore_signal(barrier, inc=1, device_id=device, device_id_type=MESH)

    @pl.loop(1, RINGZ)
    def _(k):
        greet({"tensor": lax.rem(z + k, RINGZ)})

    @pl.loop(1, SHARDS)
    def _(k):
        greet({"shard": lax.rem(shard + k, SHARDS)})

    @pl.loop(0, SHARDS)
    def _(k):
        greet({"section": other, "shard": lax.rem(shard + k, SHARDS)})

    loads = [
        pltpu.make_async_copy(src, dst, load_sem.at[i])
        for i, (src, dst) in enumerate(
            (
                (w_query.at[0], query_w),
                (w_key.at[0], key_w),
                (w_value.at[0], value_w),
                (w_out.at[0], out_w),
                (w_proj, proj_w),
            )
        )
    ]
    for load in loads:
        load.start()

    passage = lax.broadcasted_iota(jnp.int32, (PPM, SEQ), 0)
    member = (passage == segments[...]).astype(F32)
    same = lax.dot_general(
        member.astype(BF16),
        member.astype(BF16),
        (((0,), (0,)), ((), ())),
        preferred_element_type=F32,
    )
    counts = jnp.sum(member, axis=-1, keepdims=True)
    bias[0] = same

    here_row = lax.broadcasted_iota(jnp.int32, (PPM, ROWS), 0)
    here_col = lax.broadcasted_iota(jnp.int32, (PPM, ROWS), 1)
    here = jnp.zeros((PPM, ROWS), F32)
    for r in range(ROWS):
        here = jnp.where((here_col == r) & (here_row == segments_s[0, z * ROWS + r]), 1.0, here)
    member_here[...] = here

    @pl.loop(0, SEQ // ROWS)
    def _(block):
        rows = pl.ds(pl.multiple_of(block * ROWS, ROWS), ROWS)
        inside = bias[0, rows, :] > 0.5
        i = lax.broadcasted_iota(jnp.int32, (ROWS, SEQ), 0) + block * ROWS
        k = lax.broadcasted_iota(jnp.int32, (ROWS, SEQ), 1)
        ahead = k - i
        distance = jnp.abs(ahead)
        for head in range(HEADS):
            before = jnp.full((ROWS, SEQ), rel_s[0, head], F32)
            after = jnp.full((ROWS, SEQ), rel_s[16, head], F32)
            for code in range(1, 16):
                reached = distance >= lowest[code]
                before = jnp.where(reached, rel_s[code, head], before)
                after = jnp.where(reached, rel_s[16 + code, head], after)
            value = jnp.where(ahead > 0, after, before)
            bias[head, rows, :] = jnp.where(inside, value, -1e30)

    pl.semaphore_wait(barrier, RINGZ - 1 + SHARDS - 1 + SHARDS)

    swaps = [
        copy_to(src, dst.at[y, x], swap_send.at[i], swap_recv.at[i], {"section": other})
        for i, (src, dst) in enumerate(
            ((w_gate.at[0], gate_w), (w_up.at[0], up_w), (w_down.at[0], down_w))
        )
    ]
    swaps.append(copy_to(ffn_gain, gain_in, swap_send.at[3], swap_recv.at[3], {"section": other}))
    for swap in swaps:
        swap.start()

    hand = copy_to(handed, ffn_in, hand_send.at[0], hand_recv.at[0], {"section": other})

    def put_normed(rows_ref, gain, blocks):
        for c in range(2):
            value = normed(rows_ref[c].astype(F32), gain[...])
            blocks[2 * z + c] = value.astype(BF16)

    def attention():
        put_normed(attn_in, attn_gain, attn_rows)
        sent = gather_rows(z, attn_rows, ag_send, ag_recv)
        for load in loads[:3]:
            load.wait()

        @pl.loop(0, 4)
        def _(step):
            span = pl.ds(pl.multiple_of(step * 1024, 1024), 1024)
            rows = attn_rows[:, :, span].reshape(SEQ, 1024)
            for n, weight in enumerate((query_w, key_w, value_w)):
                cols = slice(n * 256, (n + 1) * 256)
                product = jnp.dot(rows, weight[span, :], preferred_element_type=F32)
                sums[:, cols] = jnp.where(step == 0, 0.0, sums[:, cols]) + product

        queries[...] = sums[:, 0:256].astype(BF16)
        keys[...] = sums[:, 256:512].astype(BF16)
        values[...] = sums[:, 512:768].astype(BF16)

        lane = lax.broadcasted_iota(jnp.int32, (SEQ, 128), 1)

        @pl.loop(0, HEADS // 2)
        def _(pair):
            cols = pl.ds(pl.multiple_of(pair * 128, 128), 128)
            query_pair, key_pair, value_pair = queries[:, cols], keys[:, cols], values[:, cols]
            results = []
            for sub in range(2):
                mine = (lane >= 64) if sub else (lane < 64)
                one = jnp.where(mine, query_pair.astype(F32), 0.0).astype(BF16)
                scores = lax.dot_general(
                    one, key_pair, (((1,), (1,)), ((), ())), preferred_element_type=F32
                )
                scores = scores + bias[pair * 2 + sub]
                weights = jnp.exp(scores - jnp.max(scores, axis=-1, keepdims=True))
                probabilities = (weights / jnp.sum(weights, axis=-1, keepdims=True)).astype(BF16)
                results.append(jnp.dot(probabilities, value_pair, preferred_element_type=F32))
            context[:, cols] = jnp.where(lane < 64, results[0], results[1]).astype(BF16)

        loads[3].wait()

        @pl.loop(0, 4)
        def _(step):
            span = pl.ds(pl.multiple_of(step * 1024, 1024), 1024)
            product = jnp.dot(context[...], out_w[:, span], preferred_element_type=F32)
            attn_parts[:, :, span] = product.astype(BF16).reshape(2 * RINGZ, CHUNK, 1024)

        more, total = sum_rows(z, attn_parts, attn_landed, rs_send, rs_recv)
        for c in range(2):
            handed[c] = (attn_in[c].astype(F32) + total(c)).astype(BF16)
        hand.start()
        for moving in sent + more:
            moving.wait_send()
        hand.wait_send()

    def feed():
        hand.wait_recv()
        put_normed(ffn_in, gain_in, ffn_rows)
        sent = gather_rows(z, ffn_rows, ag_send.at[pl.ds(16, 16)], ag_recv.at[pl.ds(16, 16)])

        @pl.loop(0, SIDE)
        def _(step):
            span = pl.ds(pl.multiple_of(step * 1024, 1024), 1024)
            rows = ffn_rows[:, :, span].reshape(SEQ, 1024)
            for n, weight in enumerate((gate_w, up_w)):
                cols = slice(n * HID, (n + 1) * HID)
                product = jnp.dot(
                    rows, weight[step].reshape(SIDE * DK, HID), preferred_element_type=F32
                )
                sums[:, cols] = jnp.where(step == 0, 0.0, sums[:, cols]) + product

        gate = sums[:, 0:HID]
        curve = jnp.tanh(0.7978845608 * (gate + 0.044715 * gate * gate * gate))
        hidden[...] = (0.5 * gate * (1.0 + curve) * sums[:, HID : 2 * HID]).astype(BF16)

        @pl.loop(0, SHARDS)
        def _(step):
            span = pl.ds(pl.multiple_of(step * DK, DK), DK)
            product = jnp.dot(
                hidden[...],
                down_w[step // SIDE, lax.rem(step, SIDE)],
                preferred_element_type=F32,
            )
            ffn_parts[:, :, span] = product.astype(BF16).reshape(2 * RINGZ, CHUNK, DK)

        more, total = sum_rows(
            z, ffn_parts, ffn_landed, rs_send.at[pl.ds(16, 16)], rs_recv.at[pl.ds(16, 16)]
        )
        for c in range(2):
            value = (ffn_in[c].astype(F32) + total(c)).astype(BF16)
            attn_in[c] = value
        for moving in sent + more:
            moving.wait_send()

    @pl.when(section == 0)
    def _():
        attn_in[...] = embeds[0].reshape(2, CHUNK, WIDTH)

    @pl.loop(0, 3)
    def _(turn):
        role = lax.rem(turn + section, 3)

        @pl.when(role == 0)
        def _():
            attention()

        @pl.when(role == 1)
        def _():
            for swap in swaps:
                swap.wait_recv()
            gather_weights(y, x, gate_w, up_w, down_w, w_send, w_recv)

        @pl.when(role == 2)
        def _():
            feed()

    for swap in swaps:
        swap.wait_send()
    loads[4].wait()

    @pl.when(section == 0)
    def _():
        finished = normed(attn_in[...].reshape(ROWS, WIDTH).astype(F32), final_gain[...])
        part = jnp.dot(member_here[...], finished, precision=HIGHEST, preferred_element_type=F32)
        for d in range(RINGZ):
            pooled[d] = part[:, d * PCOLS : (d + 1) * PCOLS]
        pooled_in[z] = pooled[z]

        def pool_copy(k):
            to = lax.rem(z + k, RINGZ)
            return copy_to(
                pooled.at[to], pooled_in.at[z], pool_send.at[k], pool_recv.at[k], {"tensor": to}
            )

        for k in range(1, RINGZ):
            pool_copy(k).start()
        for k in range(1, RINGZ):
            pool_copy(k).wait_recv()
        means = (jnp.sum(pooled_in[...], axis=0) / counts).astype(BF16)
        shares[z] = jnp.dot(means, proj_w[...], preferred_element_type=F32)

        def share_copy(k):
            to = lax.rem(z + k, RINGZ)
            return copy_to(
                shares.at[z], shares.at[z], share_send.at[k], share_recv.at[k], {"tensor": to}
            )

        for k in range(1, RINGZ):
            share_copy(k).start()
        for k in range(1, RINGZ):
            share_copy(k).wait_recv()
        projected = shares[0]
        for d in range(1, RINGZ):
            projected = projected + shares[d]
        mean_square = jnp.mean(projected * projected, axis=-1, keepdims=True)
        unit = (projected * lax.rsqrt(mean_square + EPS)).astype(BF16).astype(F32)
        row = lax.broadcasted_iota(jnp.int32, (2 * SHARDS * 8, PPM), 0)
        chosen = (dest_shard[...] == (row >> 3)) & (dest_slot[...] == (row & 3))
        chosen = chosen.astype(F32)
        lower = jnp.dot(chosen, unit[:, :HALF], preferred_element_type=F32)
        upper = jnp.dot(chosen, unit[:, HALF:], preferred_element_type=F32)
        row = lax.broadcasted_iota(jnp.int32, (2 * SHARDS * 8, HALF), 0)
        blocks = jnp.where((row & 7) < 4, lower, upper)
        placed[...] = blocks.reshape(2 * SHARDS, 8, HALF)
        placed_in[shard] = placed[shard]

        @pl.loop(1, SHARDS)
        def _(k):
            to = lax.rem(shard + k, SHARDS)
            copy_to(
                placed.at[to], placed_in.at[shard], place_send.at[k], place_recv.at[k], {"shard": to}
            ).start()

        @pl.loop(0, SHARDS)
        def _(k):
            to = lax.rem(shard + k, SHARDS)
            copy_to(
                placed.at[SHARDS + to],
                placed_in.at[shard],
                place_send.at[SHARDS + k],
                place_recv.at[k],
                {"section": other, "shard": to},
            ).start()

        for k in range(1, RINGZ):
            pool_copy(k).wait_send()
            share_copy(k).wait_send()

        @pl.loop(1, SHARDS)
        def _(k):
            copy_to(
                placed.at[0], placed_in.at[0], place_send.at[k], place_recv.at[k], {"shard": shard}
            ).wait_recv()

        @pl.loop(1, 2 * SHARDS)
        def _(k):
            copy_to(
                placed.at[0], placed_in.at[0], place_send.at[k], place_recv.at[0], {"shard": shard}
            ).wait_send()

    @pl.when(section == 1)
    def _():
        @pl.loop(0, SHARDS)
        def _(k):
            copy_to(
                placed.at[0], placed_in.at[0], place_send.at[k], place_recv.at[k], {"shard": shard}
            ).wait_recv()

    rows = jnp.sum(placed_in[...], axis=0)
    index[:, 0:HALF] = rows[0:4].astype(BF16)
    index[:, HALF:EMB] = rows[4:8].astype(BF16)


def on_device(
    embeds,
    segments,
    rel_table,
    attn_gain,
    w_query,
    w_key,
    w_value,
    w_out,
    ffn_gain,
    w_gate,
    w_up,
    w_down,
    final_gain,
    w_proj,
    dest_shard,
    dest_slot,
):
    vmem = pl.BlockSpec(memory_space=pltpu.VMEM)
    smem = pl.BlockSpec(memory_space=pltpu.SMEM)
    anywhere = pl.BlockSpec(memory_space=pl.ANY)
    dma = pltpu.SemaphoreType.DMA
    scratch = [
        pltpu.VMEM((WIDTH, 256), BF16),
        pltpu.VMEM((WIDTH, 256), BF16),
        pltpu.VMEM((WIDTH, 256), BF16),
        pltpu.VMEM((256, WIDTH), BF16),
        pltpu.VMEM((PCOLS, EMB), BF16),
        pltpu.VMEM((SIDE, SIDE, DK, HID), BF16),
        pltpu.VMEM((SIDE, SIDE, DK, HID), BF16),
        pltpu.VMEM((SIDE, SIDE, HID, DK), BF16),
        pltpu.VMEM((HEADS, SEQ, SEQ), F32),
        pltpu.VMEM((PPM, ROWS), F32),
        pltpu.VMEM((2 * RINGZ, CHUNK, WIDTH), BF16),
        pltpu.VMEM((2 * RINGZ, CHUNK, WIDTH), BF16),
        pltpu.VMEM((2 * RINGZ, CHUNK, WIDTH), BF16),
        pltpu.VMEM((2 * RINGZ, CHUNK, WIDTH), BF16),
        pltpu.VMEM((2 * RINGZ, CHUNK, WIDTH), BF16),
        pltpu.VMEM((2 * RINGZ, CHUNK, WIDTH), BF16),
        pltpu.VMEM((2, CHUNK, WIDTH), BF16),
        pltpu.VMEM((2, CHUNK, WIDTH), BF16),
        pltpu.VMEM((2, CHUNK, WIDTH), BF16),
        pltpu.VMEM((1, WIDTH), F32),
        pltpu.VMEM((SEQ, 256), BF16),
        pltpu.VMEM((SEQ, 256), BF16),
        pltpu.VMEM((SEQ, 256), BF16),
        pltpu.VMEM((SEQ, 256), BF16),
        pltpu.VMEM((SEQ, 2 * HID), F32),
        pltpu.VMEM((SEQ, HID), BF16),
        pltpu.VMEM((RINGZ, PPM, PCOLS), F32),
        pltpu.VMEM((RINGZ, PPM, PCOLS), F32),
        pltpu.VMEM((RINGZ, PPM, EMB), F32),
        pltpu.VMEM((2 * SHARDS, 8, HALF), F32),
        pltpu.VMEM((SHARDS, 8, HALF), F32),
        dma((5,)),
        dma((4,)),
        dma((4,)),
        dma((1,)),
        dma((1,)),
        dma((32,)),
        dma((32,)),
        dma((32,)),
        dma((32,)),
        dma((32,)),
        dma((32,)),
        dma((RINGZ,)),
        dma((RINGZ,)),
        dma((RINGZ,)),
        dma((RINGZ,)),
        dma((2 * SHARDS,)),
        dma((SHARDS,)),
    ]
    return pl.pallas_call(
        kernel,
        out_shape=jax.ShapeDtypeStruct((4, EMB), BF16),
        in_specs=[
            vmem,
            vmem,
            smem,
            smem,
            vmem,
            anywhere,
            anywhere,
            anywhere,
            anywhere,
            vmem,
            anywhere,
            anywhere,
            anywhere,
            vmem,
            anywhere,
            vmem,
            vmem,
        ],
        out_specs=vmem,
        scratch_shapes=scratch,
        compiler_params=pltpu.CompilerParams(
            collective_id=0, has_side_effects=True, vmem_limit_bytes=58 * 1024 * 1024
        ),
    )(
        embeds,
        segments,
        segments,
        rel_table,
        attn_gain,
        w_query,
        w_key,
        w_value,
        w_out,
        ffn_gain,
        w_gate,
        w_up,
        w_down,
        final_gain.reshape(1, -1),
        w_proj,
        dest_shard,
        dest_slot,
    )


def solution(mesh):
    in_specs = (
        P("shard", "tensor", None),
        P("shard", None),
        P(None, "tensor"),
        P("section", None),
        P("section", None, "tensor"),
        P("section", None, "tensor"),
        P("section", None, "tensor"),
        P("section", "tensor", None),
        P("section", None),
        P("section", "shard", "tensor"),
        P("section", "shard", "tensor"),
        P("section", "tensor", "shard"),
        P(),
        P("tensor", None),
        P("shard", None),
        P("shard", None),
    )
    out_specs = P(("section", "shard"), None)
    return jax.shard_map(
        on_device, mesh=mesh, in_specs=in_specs, out_specs=out_specs, check_vma=False
    )
```

```python
import jax
import jax.numpy as jnp
from jax import lax
from jax.experimental import pallas as pl
from jax.experimental.pallas import tpu as pltpu
from jax.sharding import PartitionSpec as P

MESH = pl.DeviceIdType.MESH
F32 = jnp.float32
BF16 = jnp.bfloat16
HIGHEST = lax.Precision.HIGHEST

ROWS = 32
CHUNK = 16
RINGZ = 8
SIDE = 4
SHARDS = SIDE * SIDE
WIDTH = 4096
GROUPS = 8
COLS = WIDTH // GROUPS
SEQ = 256
MID = SEQ // 2
HEADS = 4
PPM = 8
DK = 256
HID = 640
EMB = 768
HALF = EMB // 2
EPS = 1e-06

ORDER = (0, 1, 7, 2, 6, 3, 5, 4)
PLACE = tuple(ORDER.index(slot) for slot in range(RINGZ))
lowest = (0, 1, 2, 3, 4, 5, 6, 7, 8, 12, 16, 23, 32, 46, 64, 91)


def copy_to(src, dst, send, recv, device):
    return pltpu.make_async_remote_copy(
        src_ref=src,
        dst_ref=dst,
        send_sem=send,
        recv_sem=recv,
        device_id=device,
        device_id_type=MESH,
    )


def part_rows(half):
    return pl.ds(half * CHUNK, CHUNK)


def group_cols(g):
    return pl.ds(pl.multiple_of(g * COLS, COLS), COLS)


class Spread:
    def __init__(self, z, rows, send, recv):
        self.beside = (lax.rem(z + 1, RINGZ), lax.rem(z + RINGZ - 1, RINGZ))
        self.rows, self.send, self.recv = rows, send, recv

    def move(self, way, hop, g, src=None, section=None):
        source, target = (RINGZ - hop + 1, RINGZ - hop) if way == 0 else (hop - 1, hop)
        rows = pl.ds(0, ROWS) if hop < 4 else part_rows(way)
        if src is None:
            src = self.rows.at[g, PLACE[source % RINGZ], rows]
        device = {"tensor": self.beside[way]}
        if section is not None:
            device["section"] = section
        at = way * 4 + hop - 1
        return copy_to(
            src,
            self.rows.at[g, PLACE[target % RINGZ], rows],
            self.send.at[at, g],
            self.recv.at[at, g],
            device,
        )

    def step(self, hop, g):
        for way in (0, 1):
            if hop > 1:
                self.move(way, hop - 1, g).wait_recv()
            self.move(way, hop, g).start()

    def land(self, g):
        for way in (0, 1):
            self.move(way, 4, g).wait_recv()

    def sent(self, g, hops):
        for way in (0, 1):
            for hop in hops:
                self.move(way, hop, g).wait_send()


class Chains:
    def __init__(self, z, parts, landed, send, recv):
        self.beside = (lax.rem(z + 1, RINGZ), lax.rem(z + RINGZ - 1, RINGZ))
        self.parts, self.landed, self.send, self.recv = parts, landed, send, recv

    def move(self, way, hop, g, half):
        ahead = 5 - hop
        place = PLACE[ahead if way == 0 else RINGZ - ahead]
        at = way * 8 + (hop - 1) * 2 + half
        rows = part_rows(half)
        return copy_to(
            self.parts.at[g, place, rows],
            self.landed.at[way, hop - 1, g, rows],
            self.send.at[at, g],
            self.recv.at[at, g],
            {"tensor": self.beside[way]},
        )

    def forward(self, hop, g, late):
        for way in (0, 1):
            half = way if late else 1 - way
            if hop > (1 if late else 2):
                self.move(way, hop - 1, g, half).wait_recv()
                place = PLACE[5 - hop if way == 0 else RINGZ - 5 + hop]
                rows = part_rows(half)
                total = self.parts[g, place, rows].astype(F32) + self.landed[
                    way, hop - 2, g, rows
                ].astype(F32)
                self.parts[g, place, rows] = total.astype(BF16)
            self.move(way, hop, g, half).start()

    def total(self, g):
        for way in (0, 1):
            for half in (0, 1):
                self.move(way, 4, g, half).wait_recv()
        own = self.parts[g, 0].astype(F32)
        return own + self.landed[0, 3, g].astype(F32) + self.landed[1, 3, g].astype(F32)

    def sent(self, g):
        for way in (0, 1):
            self.move(way, 1, g, way).wait_send()
            for hop in (2, 3, 4):
                for half in (0, 1):
                    self.move(way, hop, g, half).wait_send()


class Weights:
    def __init__(self, y, x, gate, up, down, send, recv):
        self.y, self.x = y, x
        self.arrays = ((gate, 0, DK), (up, 0, DK), (down, 0, HID // 2), (down, HID // 2, HID // 2))
        self.send, self.recv = send, recv

    def piece(self, array, first, second, sign):
        ref, start, size = self.arrays[array]
        if sign is not None:
            size = size // 2
            start = start + sign * size
        along_x, along_y = (first, second) if array % 2 == 0 else (second, first)
        at_x, at_y = lax.rem(self.x + along_x, SIDE), lax.rem(self.y + along_y, SIDE)
        return ref.at[at_y, at_x, pl.ds(start, size)]

    def copy(self, array, stage, hop, line, sign, landing):
        step = 1 if sign == 0 else SIDE - 1
        back = SIDE - step
        away = (back if hop == 1 else 0) + (back if landing else 0)
        if stage == 0:
            ref = self.piece(array, away % SIDE, 0, None if hop == 0 else sign)
            at = hop * 2 + sign
        else:
            ref = self.piece(array, line, away % SIDE, None if hop == 0 else sign)
            at = 4 + (line * 2 + hop) * 2 + sign
        on_x = (array % 2 == 0) == (stage == 0)
        if on_x:
            shard = self.y * SIDE + lax.rem(self.x + step, SIDE)
        else:
            shard = lax.rem(self.y + step, SIDE) * SIDE + self.x
        return copy_to(ref, ref, self.send.at[array, at], self.recv.at[array, at], {"shard": shard})

    def go(self, array, stage, hop, line, sign):
        self.copy(array, stage, hop, line, sign, False).start()

    def wait(self, array, stage, hop, line, sign):
        self.copy(array, stage, hop, line, sign, True).wait_recv()

    def run(self, ready):
        both = (0, 1)
        for array in range(4):
            ready(array)
            for sign in both:
                self.go(array, 0, 0, 0, sign)
                self.go(array, 1, 0, 0, sign)
        for array in range(4):
            for sign in both:
                self.wait(array, 0, 0, 0, sign)
                self.go(array, 0, 1, 0, sign)
                line = SIDE - 1 if sign == 0 else 1
                for other in both:
                    self.go(array, 1, 0, line, other)
        for array in range(4):
            for sign in both:
                self.wait(array, 0, 1, 0, sign)
            for sign in both:
                self.go(array, 1, 0, 2, sign)
        for array in range(4):
            for line in (0, 1, 3, 2):
                for sign in both:
                    self.wait(array, 1, 0, line, sign)
                    self.go(array, 1, 1, line, sign)

    def land(self, arrays):
        for array in arrays:
            for line in range(SIDE):
                for sign in (0, 1):
                    self.wait(array, 1, 1, line, sign)

    def sent(self):
        for array in range(4):
            for sign in (0, 1):
                for hop in (0, 1):
                    self.copy(array, 0, hop, 0, sign, False).wait_send()
                    for line in range(SIDE):
                        self.copy(array, 1, hop, line, sign, False).wait_send()


def kernel(
    embeds,
    segments,
    rel_table,
    attn_gain,
    w_query,
    w_key,
    w_value,
    w_out,
    ffn_gain,
    w_gate,
    w_up,
    w_down,
    final_gain,
    w_proj,
    dest_shard,
    dest_slot,
    index,
    query_w,
    key_w,
    value_w,
    out_w,
    proj_w,
    gate_w,
    up_w,
    down_w,
    bias,
    member_here,
    attn_rows,
    attn_parts,
    attn_landed,
    ffn_rows,
    ffn_parts,
    ffn_landed,
    attn_in,
    handed,
    ffn_in,
    staged,
    queries,
    keys,
    values,
    context,
    sums,
    hidden,
    pooled,
    pooled_in,
    shares,
    placed,
    placed_in,
    load_sem,
    swap_send,
    swap_recv,
    hand_send,
    hand_recv,
    near_send,
    near_recv,
    ag_send,
    ag_recv,
    rs_send,
    rs_recv,
    w_send,
    w_recv,
    pool_send,
    pool_recv,
    share_send,
    share_recv,
    place_send,
    place_recv,
    free_sem,
):
    section = lax.axis_index("section")
    z = lax.axis_index("tensor")
    shard = lax.axis_index("shard")
    y, x = shard // SIDE, lax.rem(shard, SIDE)
    other = 1 - section

    barrier = pltpu.get_barrier_semaphore()

    def greet(device):
        pl.semaphore_signal(barrier, inc=1, device_id=device, device_id_type=MESH)

    @pl.loop(1, SHARDS)
    def _(k):
        greet({"shard": lax.rem(shard + k, SHARDS)})

    @pl.loop(0, SHARDS)
    def _(k):
        greet({"section": other, "shard": lax.rem(shard + k, SHARDS)})

    @pl.loop(1, RINGZ)
    def _(k):
        greet({"tensor": lax.rem(z + k, RINGZ)})

    for k in (1, RINGZ - 1):
        greet({"section": other, "tensor": lax.rem(z + k, RINGZ)})

    loads = [
        pltpu.make_async_copy(src, dst, load_sem.at[i])
        for i, (src, dst) in enumerate(
            (
                (w_query.at[0], query_w),
                (w_key.at[0], key_w),
                (w_value.at[0], value_w),
                (w_out.at[0], out_w),
                (w_proj, proj_w),
            )
        )
    ]
    for load in loads:
        load.start()

    passage = lax.broadcasted_iota(jnp.int32, (PPM, SEQ), 0)
    counts = jnp.sum((segments[...] == passage).astype(F32), axis=-1, keepdims=True)
    first = jnp.sum((segments[...] < passage).astype(F32), axis=-1, keepdims=True)

    def members(token):
        at = token.astype(F32)
        return ((at >= first) & (at < first + counts)).astype(F32)

    lane = lax.broadcasted_iota(jnp.int32, (PPM, ROWS), 1)
    member_here[...] = members(lane + z * ROWS)

    def slots(place):
        slot = jnp.full_like(place, ORDER[0])
        for at in range(1, RINGZ):
            slot = jnp.where(place == at, ORDER[at], slot)
        return slot

    def tokens(position):
        return (((slots(position >> 5) + z) & 7) << 5) + (position & 31)

    lane = lax.broadcasted_iota(jnp.int32, (PPM, SEQ), 1)
    member = members(tokens(lane)).astype(BF16)
    bias[0] = lax.dot_general(
        member, member, (((0,), (0,)), ((), ())), preferred_element_type=F32
    )

    @pl.loop(0, RINGZ)
    def _(block):
        rows = pl.ds(pl.multiple_of(block * ROWS, ROWS), ROWS)
        inside = bias[0, rows, :] > 0.5
        i = tokens(lax.broadcasted_iota(jnp.int32, (ROWS, SEQ), 0) + block * ROWS)
        k = tokens(lax.broadcasted_iota(jnp.int32, (ROWS, SEQ), 1))
        ahead = k - i
        distance = jnp.abs(ahead)
        for head in range(HEADS):
            before = jnp.broadcast_to(rel_table[0:1, head : head + 1], (ROWS, SEQ))
            after = jnp.broadcast_to(rel_table[16:17, head : head + 1], (ROWS, SEQ))
            for code in range(1, 16):
                reached = distance >= lowest[code]
                before = jnp.where(reached, rel_table[code : code + 1, head : head + 1], before)
                after = jnp.where(
                    reached, rel_table[16 + code : 17 + code, head : head + 1], after
                )
            value = jnp.where(ahead > 0, after, before)
            bias[head, rows, :] = jnp.where(inside, value, -1e30)

    @pl.when(section == 0)
    def _():
        for g in range(GROUPS):
            attn_in[g] = embeds[0, :, g * COLS : (g + 1) * COLS]

    pl.semaphore_wait(barrier, RINGZ - 1 + SHARDS - 1 + SHARDS + 2)

    swaps = [
        copy_to(src, dst, swap_send.at[i], swap_recv.at[i], {"section": other})
        for i, (src, dst) in enumerate(
            (
                (w_gate.at[0], gate_w.at[y, x]),
                (w_up.at[0], up_w.at[y, x]),
                (w_down.at[0], down_w.at[y, x]),
            )
        )
    ]
    for swap in swaps:
        swap.start()

    attn_spread = Spread(z, attn_rows, ag_send.at[0], ag_recv.at[0])
    ffn_spread = Spread(z, ffn_rows, ag_send.at[1], ag_recv.at[1])
    attn_chains = Chains(z, attn_parts, attn_landed, rs_send.at[0], rs_recv.at[0])
    ffn_chains = Chains(z, ffn_parts, ffn_landed, rs_send.at[1], rs_recv.at[1])
    weights = Weights(y, x, gate_w, up_w, down_w, w_send, w_recv)
    hand = copy_to(handed, ffn_in, hand_send.at[0], hand_recv.at[0], {"section": other})

    def near(g):
        return copy_to(
            staged.at[g], ffn_rows.at[g, 0], near_send.at[g], near_recv.at[g], {"section": other}
        )

    def squares(value):
        return jnp.sum(value * value, axis=-1, keepdims=True)

    def scale_of(total):
        return lax.rsqrt(total * (1.0 / WIDTH) + EPS)

    no_squares = jnp.zeros((ROWS, 1), F32)

    def run_spread(spread, multiply):
        @pl.loop(0, GROUPS)
        def _(g):
            spread.step(2, g)

        @pl.loop(0, GROUPS)
        def _(g):
            spread.step(3, g)

        @pl.loop(0, GROUPS // 2)
        def _(pair):
            multiply(pair, 0)
            for g in (2 * pair, 2 * pair + 1):
                spread.step(4, g)

    def run_chains(chains, far, between, close):
        @pl.loop(0, GROUPS)
        def _(g):
            far(g)
            chains.forward(1, g, True)
            chains.forward(2, g, False)

        between()

        @pl.loop(0, GROUPS)
        def _(g):
            close(g)
            chains.forward(2, g, True)
            chains.forward(3, g, False)

        @pl.loop(0, GROUPS)
        def _(g):
            chains.forward(3, g, True)
            chains.forward(4, g, False)

        @pl.loop(0, GROUPS)
        def _(g):
            chains.forward(4, g, True)

    def finish(chains, before, after):
        def add(g, total):
            value = (before[g].astype(F32) + chains.total(g)).astype(BF16)
            after[g] = value
            return total + squares(value.astype(F32))

        return lax.fori_loop(0, GROUPS, add, no_squares)

    def half(place):
        return pl.ds(place * 4, 4), slice(place * MID, (place + 1) * MID)

    def attention():
        total = lax.fori_loop(
            0, GROUPS, lambda g, t: t + squares(attn_in[g].astype(F32)), no_squares
        )
        scale = scale_of(total)

        @pl.loop(0, GROUPS)
        def _(g):
            value = attn_in[g].astype(F32) * scale * attn_gain[:, group_cols(g)]
            attn_rows[g, 0] = value.astype(BF16)
            attn_spread.step(1, g)

        for load in loads[:3]:
            load.wait()

        def multiply(pair, place):
            blocks, rows = half(place)
            for n, weight in enumerate((query_w, key_w, value_w)):
                cols = slice(n * 256, (n + 1) * 256)
                product = jnp.where(pair == 0, 0.0, sums[rows, cols])
                for g in (2 * pair, 2 * pair + 1):
                    product = product + jnp.dot(
                        attn_rows[g, blocks].reshape(MID, COLS),
                        weight[group_cols(g), :],
                        preferred_element_type=F32,
                    )
                sums[rows, cols] = product

        run_spread(attn_spread, multiply)

        @pl.loop(0, GROUPS)
        def _(g):
            attn_spread.land(g)

        @pl.loop(0, GROUPS // 2)
        def _(pair):
            multiply(pair, 1)

        queries[...] = sums[:, 0:256].astype(BF16)
        keys[...] = sums[:, 256:512].astype(BF16)
        values[...] = sums[:, 512:768].astype(BF16)

        def attend(place):
            _, rows = half(place)
            head_lane = lax.broadcasted_iota(jnp.int32, (MID, 128), 1)

            @pl.loop(0, HEADS // 2)
            def _(pair):
                cols = pl.ds(pl.multiple_of(pair * 128, 128), 128)
                query_pair, key_pair, value_pair = queries[rows, cols], keys[:, cols], values[:, cols]
                results = []
                for sub in range(2):
                    mine = (head_lane >= 64) if sub else (head_lane < 64)
                    one = jnp.where(mine, query_pair.astype(F32), 0.0).astype(BF16)
                    scores = lax.dot_general(
                        one, key_pair, (((1,), (1,)), ((), ())), preferred_element_type=F32
                    )
                    scores = scores + bias[pair * 2 + sub, rows, :]
                    powers = jnp.exp(scores - jnp.max(scores, axis=-1, keepdims=True))
                    shares_of = powers / jnp.sum(powers, axis=-1, keepdims=True)
                    results.append(
                        jnp.dot(shares_of.astype(BF16), value_pair, preferred_element_type=F32)
                    )
                context[rows, cols] = jnp.where(head_lane < 64, results[0], results[1]).astype(BF16)

        def project(g, place):
            blocks, rows = half(place)
            product = jnp.dot(
                context[rows, :], out_w[:, group_cols(g)], preferred_element_type=F32
            )
            attn_parts[g, blocks] = product.astype(BF16).reshape(4, ROWS, COLS)

        attend(1)
        loads[3].wait()
        run_chains(
            attn_chains, lambda g: project(g, 1), lambda: attend(0), lambda g: project(g, 0)
        )
        scale = scale_of(finish(attn_chains, attn_in, handed))

        @pl.loop(0, GROUPS)
        def _(g):
            value = handed[g].astype(F32) * scale * ffn_gain[:, group_cols(g)]
            staged[g] = value.astype(BF16)
            for way in (0, 1):
                ffn_spread.move(way, 1, g, staged.at[g], other).start()
            near(g).start()

        hand.start()

    def feed():
        def multiply(pair, place):
            blocks, rows = half(place)
            for n, weight in enumerate((gate_w, up_w)):
                cols = slice(n * HID, (n + 1) * HID)
                product = jnp.where(pair == 0, 0.0, sums[rows, cols])
                for j in range(2):
                    product = product + jnp.dot(
                        ffn_rows[2 * pair + j, blocks].reshape(MID, COLS),
                        weight[pair, 2 * j : 2 * j + 2].reshape(COLS, HID),
                        preferred_element_type=F32,
                    )
                sums[rows, cols] = product

        def activate(place):
            _, rows = half(place)
            gate = sums[rows, 0:HID]
            curve = jnp.tanh(0.7978845608 * (gate + 0.044715 * gate * gate * gate))
            hidden[rows, :] = (0.5 * gate * (1.0 + curve) * sums[rows, HID : 2 * HID]).astype(BF16)

        def first_multiply(pair, place):
            @pl.when(pair == 0)
            def _():
                @pl.loop(0, GROUPS)
                def _(g):
                    near(g).wait_recv()

                weights.land((0, 1))

            multiply(pair, place)

        run_spread(ffn_spread, first_multiply)
        activate(0)

        @pl.loop(0, GROUPS)
        def _(g):
            ffn_spread.land(g)

        @pl.loop(0, GROUPS // 2)
        def _(pair):
            multiply(pair, 1)

        activate(1)
        weights.land((2, 3))

        def project(g, place):
            blocks, rows = half(place)
            for j in range(2):
                product = jnp.dot(
                    hidden[rows, :],
                    down_w[g // 2, 2 * lax.rem(g, 2) + j],
                    preferred_element_type=F32,
                )
                ffn_parts[g, blocks, :, j * DK : (j + 1) * DK] = product.astype(BF16).reshape(
                    4, ROWS, DK
                )

        run_chains(ffn_chains, lambda g: project(g, 1), lambda: None, lambda g: project(g, 0))
        hand.wait_recv()
        finish(ffn_chains, ffn_in, attn_in)

    @pl.loop(0, 3)
    def _(turn):
        role = lax.rem(turn + section, 3)

        @pl.when(role == 0)
        def _():
            attention()

        @pl.when(role == 1)
        def _():
            @pl.when(section == 0)
            def _():
                pl.semaphore_wait(free_sem, 1)

            def ready(array):
                if array < 3:
                    swaps[array].wait_recv()

            weights.run(ready)

            @pl.when(section == 1)
            def _():
                pl.semaphore_signal(
                    free_sem, inc=1, device_id={"section": other}, device_id_type=MESH
                )

        @pl.when(role == 2)
        def _():
            feed()

    loads[4].wait()

    @pl.when(section == 0)
    def _():
        total = lax.fori_loop(
            0, GROUPS, lambda g, t: t + squares(attn_in[g].astype(F32)), no_squares
        )
        scale = scale_of(total)

        def pool_copy(k):
            to = lax.rem(z + k, RINGZ)
            return copy_to(
                pooled.at[to], pooled_in.at[z], pool_send.at[k], pool_recv.at[k], {"tensor": to}
            )

        def share_copy(k):
            to = lax.rem(z + k, RINGZ)
            return copy_to(
                shares.at[z], shares.at[z], share_send.at[k], share_recv.at[k], {"tensor": to}
            )

        def pool(g):
            finished = attn_in[g].astype(F32) * scale * final_gain[:, group_cols(g)]
            return jnp.dot(
                member_here[...], finished, precision=HIGHEST, preferred_element_type=F32
            )

        for k in (4, 3, 5, 2, 6, 1, 7):
            to = lax.rem(z + k, RINGZ)
            pooled[to] = pool(to)
            pool_copy(k).start()
        pooled_in[z] = pool(z)
        for k in range(1, RINGZ):
            pool_copy(k).wait_recv()
        means = (jnp.sum(pooled_in[...], axis=0) / counts).astype(BF16)
        shares[z] = jnp.dot(means, proj_w[...], preferred_element_type=F32)
        for k in (4, 3, 5, 2, 6, 1, 7):
            share_copy(k).start()
        row = lax.broadcasted_iota(jnp.int32, (2 * SHARDS * 8, PPM), 0)
        chosen = (dest_shard[...] == (row >> 3)) & (dest_slot[...] == (row & 3))
        chosen = chosen.astype(F32)
        for k in range(1, RINGZ):
            share_copy(k).wait_recv()
        projected = shares[0]
        for d in range(1, RINGZ):
            projected = projected + shares[d]
        mean_square = jnp.mean(projected * projected, axis=-1, keepdims=True)
        unit = (projected * lax.rsqrt(mean_square + EPS)).astype(BF16).astype(F32)
        lower = jnp.dot(chosen, unit[:, :HALF], preferred_element_type=F32)
        upper = jnp.dot(chosen, unit[:, HALF:], preferred_element_type=F32)
        row = lax.broadcasted_iota(jnp.int32, (2 * SHARDS * 8, HALF), 0)
        blocks = jnp.where((row & 7) < 4, lower, upper)
        placed[...] = blocks.reshape(2 * SHARDS, 8, HALF)
        placed_in[shard] = placed[shard]

        @pl.loop(1, SHARDS)
        def _(k):
            to = lax.rem(shard + k, SHARDS)
            copy_to(
                placed.at[to], placed_in.at[shard], place_send.at[k], place_recv.at[k], {"shard": to}
            ).start()

        @pl.loop(0, SHARDS)
        def _(k):
            to = lax.rem(shard + k, SHARDS)
            copy_to(
                placed.at[SHARDS + to],
                placed_in.at[shard],
                place_send.at[SHARDS + k],
                place_recv.at[k],
                {"section": other, "shard": to},
            ).start()

    for swap in swaps:
        swap.wait_send()
    weights.sent()
    hand.wait_send()

    @pl.loop(0, GROUPS)
    def _(g):
        attn_spread.sent(g, (1, 2, 3, 4))
        for way in (0, 1):
            ffn_spread.move(way, 1, g, staged.at[g], other).wait_send()
        ffn_spread.sent(g, (2, 3, 4))
        near(g).wait_send()
        attn_chains.sent(g)
        ffn_chains.sent(g)

    def place_wait(k):
        return copy_to(
            placed.at[0], placed_in.at[0], place_send.at[k], place_recv.at[k], {"shard": shard}
        )

    @pl.when(section == 0)
    def _():
        for k in range(1, RINGZ):
            pool_wait = copy_to(
                pooled.at[0], pooled_in.at[0], pool_send.at[k], pool_recv.at[k], {"tensor": z}
            )
            pool_wait.wait_send()
            share_wait = copy_to(
                shares.at[0], shares.at[0], share_send.at[k], share_recv.at[k], {"tensor": z}
            )
            share_wait.wait_send()

        @pl.loop(1, SHARDS)
        def _(k):
            place_wait(k).wait_recv()
            place_wait(k).wait_send()

        @pl.loop(SHARDS, 2 * SHARDS)
        def _(k):
            copy_to(
                placed.at[0], placed_in.at[0], place_send.at[k], place_recv.at[0], {"shard": shard}
            ).wait_send()

    @pl.when(section == 1)
    def _():
        @pl.loop(0, SHARDS)
        def _(k):
            place_wait(k).wait_recv()

    rows = jnp.sum(placed_in[...], axis=0)
    index[:, 0:HALF] = rows[0:4].astype(BF16)
    index[:, HALF:EMB] = rows[4:8].astype(BF16)


def on_device(
    embeds,
    segments,
    rel_table,
    attn_gain,
    w_query,
    w_key,
    w_value,
    w_out,
    ffn_gain,
    w_gate,
    w_up,
    w_down,
    final_gain,
    w_proj,
    dest_shard,
    dest_slot,
):
    vmem = pl.BlockSpec(memory_space=pltpu.VMEM)
    anywhere = pl.BlockSpec(memory_space=pl.ANY)
    dma = pltpu.SemaphoreType.DMA
    rows = pltpu.VMEM((GROUPS, RINGZ, ROWS, COLS), BF16)
    landed = pltpu.VMEM((2, 4, GROUPS, ROWS, COLS), BF16)
    own = pltpu.VMEM((GROUPS, ROWS, COLS), BF16)
    heads = pltpu.VMEM((SEQ, 256), BF16)
    scratch = [
        pltpu.VMEM((WIDTH, 256), BF16),
        pltpu.VMEM((WIDTH, 256), BF16),
        pltpu.VMEM((WIDTH, 256), BF16),
        pltpu.VMEM((256, WIDTH), BF16),
        pltpu.VMEM((COLS, EMB), BF16),
        pltpu.VMEM((SIDE, SIDE, DK, HID), BF16),
        pltpu.VMEM((SIDE, SIDE, DK, HID), BF16),
        pltpu.VMEM((SIDE, SIDE, HID, DK), BF16),
        pltpu.VMEM((HEADS, SEQ, SEQ), F32),
        pltpu.VMEM((PPM, ROWS), F32),
        rows,
        rows,
        landed,
        rows,
        rows,
        landed,
        own,
        own,
        own,
        own,
        heads,
        heads,
        heads,
        heads,
        pltpu.VMEM((SEQ, 2 * HID), F32),
        pltpu.VMEM((SEQ, HID), BF16),
        pltpu.VMEM((RINGZ, PPM, COLS), F32),
        pltpu.VMEM((RINGZ, PPM, COLS), F32),
        pltpu.VMEM((RINGZ, PPM, EMB), F32),
        pltpu.VMEM((2 * SHARDS, 8, HALF), F32),
        pltpu.VMEM((SHARDS, 8, HALF), F32),
        dma((5,)),
        dma((3,)),
        dma((3,)),
        dma((1,)),
        dma((1,)),
        dma((GROUPS,)),
        dma((GROUPS,)),
        dma((2, 8, GROUPS)),
        dma((2, 8, GROUPS)),
        dma((2, 16, GROUPS)),
        dma((2, 16, GROUPS)),
        dma((4, 20)),
        dma((4, 20)),
        dma((RINGZ,)),
        dma((RINGZ,)),
        dma((RINGZ,)),
        dma((RINGZ,)),
        dma((2 * SHARDS,)),
        dma((SHARDS,)),
        pltpu.SemaphoreType.REGULAR,
    ]
    vmem_args = (0, 1, 2, 3, 8, 12, 14, 15)
    return pl.pallas_call(
        kernel,
        out_shape=jax.ShapeDtypeStruct((4, EMB), BF16),
        in_specs=[vmem if i in vmem_args else anywhere for i in range(16)],
        out_specs=vmem,
        scratch_shapes=scratch,
        compiler_params=pltpu.CompilerParams(
            collective_id=0, has_side_effects=True, vmem_limit_bytes=58 * 1024 * 1024
        ),
    )(
        embeds,
        segments,
        rel_table,
        attn_gain,
        w_query,
        w_key,
        w_value,
        w_out,
        ffn_gain,
        w_gate,
        w_up,
        w_down,
        final_gain.reshape(1, -1),
        w_proj,
        dest_shard,
        dest_slot,
    )


def solution(mesh):
    in_specs = (
        P("shard", "tensor", None),
        P("shard", None),
        P(None, "tensor"),
        P("section", None),
        P("section", None, "tensor"),
        P("section", None, "tensor"),
        P("section", None, "tensor"),
        P("section", "tensor", None),
        P("section", None),
        P("section", "shard", "tensor"),
        P("section", "shard", "tensor"),
        P("section", "tensor", "shard"),
        P(),
        P("tensor", None),
        P("shard", None),
        P("shard", None),
    )
    out_specs = P(("section", "shard"), None)
    return jax.shard_map(
        on_device, mesh=mesh, in_specs=in_specs, out_specs=out_specs, check_vma=False
    )
```

```python
import jax
import jax.numpy as jnp
from jax import lax
from jax.experimental import pallas as pl
from jax.experimental.pallas import tpu as pltpu
from jax.sharding import PartitionSpec as P

MESH = pl.DeviceIdType.MESH
F32 = jnp.float32
BF16 = jnp.bfloat16
HIGHEST = lax.Precision.HIGHEST

ROWS = 32
CHUNK = 16
RINGZ = 8
SIDE = 4
SHARDS = SIDE * SIDE
WIDTH = 4096
GROUPS = 8
COLS = WIDTH // GROUPS
SEQ = 256
NEAR = 5
HEADS = 4
PPM = 8
DK = 256
HID = 640
EMB = 768
HALF = EMB // 2
EPS = 1e-06

ORDER = (0, 1, 7, 2, 6, 3, 5, 4)
PLACE = tuple(ORDER.index(slot) for slot in range(RINGZ))
lowest = (0, 1, 2, 3, 4, 5, 6, 7, 8, 12, 16, 23, 32, 46, 64, 91)


def copy_to(src, dst, send, recv, device):
    return pltpu.make_async_remote_copy(
        src_ref=src,
        dst_ref=dst,
        send_sem=send,
        recv_sem=recv,
        device_id=device,
        device_id_type=MESH,
    )


def part_rows(half):
    return pl.ds(half * CHUNK, CHUNK)


def group_cols(g):
    return pl.ds(pl.multiple_of(g * COLS, COLS), COLS)


class Spread:
    def __init__(self, z, rows, send, recv):
        self.beside = (lax.rem(z + 1, RINGZ), lax.rem(z + RINGZ - 1, RINGZ))
        self.rows, self.send, self.recv = rows, send, recv

    def move(self, way, hop, g, src=None, section=None):
        source, target = (RINGZ - hop + 1, RINGZ - hop) if way == 0 else (hop - 1, hop)
        rows = pl.ds(0, ROWS) if hop < 4 else part_rows(way)
        if src is None:
            src = self.rows.at[g, PLACE[source % RINGZ], rows]
        device = {"tensor": self.beside[way]}
        if section is not None:
            device["section"] = section
        at = way * 4 + hop - 1
        return copy_to(
            src,
            self.rows.at[g, PLACE[target % RINGZ], rows],
            self.send.at[at],
            self.recv.at[at, 0 if isinstance(g, pl.Slice) else g],
            device,
        )

    def step(self, hop, g):
        for way in (0, 1):
            if hop > 1:
                self.move(way, hop - 1, g).wait_recv()
            self.move(way, hop, g).start()

    def land(self, g):
        for way in (0, 1):
            self.move(way, 4, g).wait_recv()

    def sent(self, src=None):
        for way in (0, 1):
            for hop in (1, 2, 3, 4):
                whole = pl.ds(0, GROUPS)
                self.move(way, hop, whole, src if hop == 1 else None).wait_send()


class Chains:
    def __init__(self, z, parts, landed, send, recv):
        self.beside = (lax.rem(z + 1, RINGZ), lax.rem(z + RINGZ - 1, RINGZ))
        self.parts, self.landed, self.send, self.recv = parts, landed, send, recv

    def move(self, way, hop, g, half):
        ahead = 5 - hop
        place = PLACE[ahead if way == 0 else RINGZ - ahead]
        at = way * 8 + (hop - 1) * 2 + half
        rows = part_rows(half)
        return copy_to(
            self.parts.at[g, place, rows],
            self.landed.at[way, hop - 1, g, rows],
            self.send.at[at],
            self.recv.at[at, 0 if isinstance(g, pl.Slice) else g],
            {"tensor": self.beside[way]},
        )

    def forward(self, hop, g, late):
        for way in (0, 1):
            half = way if late else 1 - way
            if hop > (1 if late else 2):
                self.move(way, hop - 1, g, half).wait_recv()
                place = PLACE[5 - hop if way == 0 else RINGZ - 5 + hop]
                rows = part_rows(half)
                total = self.parts[g, place, rows].astype(F32) + self.landed[
                    way, hop - 2, g, rows
                ].astype(F32)
                self.parts[g, place, rows] = total.astype(BF16)
            self.move(way, hop, g, half).start()

    def total(self, g):
        for way in (0, 1):
            for half in (0, 1):
                self.move(way, 4, g, half).wait_recv()
        own = self.parts[g, 0].astype(F32)
        return own + self.landed[0, 3, g].astype(F32) + self.landed[1, 3, g].astype(F32)

    def sent(self):
        whole = pl.ds(0, GROUPS)
        for way in (0, 1):
            self.move(way, 1, whole, way).wait_send()
            for hop in (2, 3, 4):
                for half in (0, 1):
                    self.move(way, hop, whole, half).wait_send()


class Weights:
    def __init__(self, y, x, gate, up, down, send, recv):
        self.y, self.x = y, x
        self.arrays = ((gate, 0, DK), (up, 0, DK), (down, 0, HID // 2), (down, HID // 2, HID // 2))
        self.send, self.recv = send, recv

    def piece(self, array, first, second, sign):
        ref, start, size = self.arrays[array]
        if sign is not None:
            size = size // 2
            start = start + sign * size
        along_x, along_y = (first, second) if array % 2 == 0 else (second, first)
        at_x, at_y = lax.rem(self.x + along_x, SIDE), lax.rem(self.y + along_y, SIDE)
        return ref.at[at_y, at_x, pl.ds(start, size)]

    def copy(self, array, stage, hop, line, sign, landing):
        step = 1 if sign == 0 else SIDE - 1
        back = SIDE - step
        away = (back if hop == 1 else 0) + (back if landing else 0)
        if stage == 0:
            ref = self.piece(array, away % SIDE, 0, None if hop == 0 else sign)
            at = hop * 2 + sign
        else:
            ref = self.piece(array, line, away % SIDE, None if hop == 0 else sign)
            at = 4 + (line * 2 + hop) * 2 + sign
        on_x = (array % 2 == 0) == (stage == 0)
        if on_x:
            shard = self.y * SIDE + lax.rem(self.x + step, SIDE)
        else:
            shard = lax.rem(self.y + step, SIDE) * SIDE + self.x
        return copy_to(ref, ref, self.send.at[array, at], self.recv.at[array, at], {"shard": shard})

    def go(self, array, stage, hop, line, sign):
        self.copy(array, stage, hop, line, sign, False).start()

    def wait(self, array, stage, hop, line, sign):
        self.copy(array, stage, hop, line, sign, True).wait_recv()

    def run(self, ready):
        both = (0, 1)
        for array in range(4):
            ready(array)
            for sign in both:
                self.go(array, 0, 0, 0, sign)
                self.go(array, 1, 0, 0, sign)
        for array in range(4):
            for sign in both:
                self.wait(array, 0, 0, 0, sign)
                self.go(array, 0, 1, 0, sign)
                line = SIDE - 1 if sign == 0 else 1
                for other in both:
                    self.go(array, 1, 0, line, other)
        for array in range(4):
            for sign in both:
                self.wait(array, 0, 1, 0, sign)
            for sign in both:
                self.go(array, 1, 0, 2, sign)
        for array in range(4):
            for line in (0, 1, 3, 2):
                for sign in both:
                    self.wait(array, 1, 0, line, sign)
                    self.go(array, 1, 1, line, sign)

    def land(self, arrays):
        for array in arrays:
            for line in range(SIDE):
                for sign in (0, 1):
                    self.wait(array, 1, 1, line, sign)

    def sent(self):
        for array in range(4):
            for sign in (0, 1):
                for hop in (0, 1):
                    self.copy(array, 0, hop, 0, sign, False).wait_send()
                    for line in range(SIDE):
                        self.copy(array, 1, hop, line, sign, False).wait_send()


def kernel(
    embeds,
    segments,
    rel_table,
    attn_gain,
    w_query,
    w_key,
    w_value,
    w_out,
    ffn_gain,
    w_gate,
    w_up,
    w_down,
    final_gain,
    w_proj,
    dest_shard,
    dest_slot,
    index,
    segments_v,
    rel_v,
    attn_gain_v,
    ffn_gain_v,
    final_gain_v,
    dest_shard_v,
    dest_slot_v,
    query_w,
    key_w,
    value_w,
    out_w,
    proj_w,
    gate_w,
    up_w,
    down_w,
    bias,
    member_here,
    attn_rows,
    attn_parts,
    attn_landed,
    ffn_rows,
    ffn_parts,
    ffn_landed,
    attn_in,
    handed,
    ffn_in,
    staged,
    queries,
    keys,
    values,
    context,
    sums,
    hidden,
    pooled,
    pooled_in,
    shares,
    placed,
    placed_in,
    load_sem,
    rows_sem,
    swap_send,
    swap_recv,
    hand_send,
    hand_recv,
    near_send,
    near_recv,
    ag_send,
    ag_recv,
    rs_send,
    rs_recv,
    w_send,
    w_recv,
    pool_send,
    pool_recv,
    share_send,
    share_recv,
    place_send,
    place_recv,
    free_sem,
):
    section = lax.axis_index("section")
    z = lax.axis_index("tensor")
    shard = lax.axis_index("shard")
    y, x = shard // SIDE, lax.rem(shard, SIDE)
    other = 1 - section

    barrier = pltpu.get_barrier_semaphore()

    def greet(device):
        pl.semaphore_signal(barrier, inc=1, device_id=device, device_id_type=MESH)

    @pl.loop(1, RINGZ)
    def _(k):
        greet({"tensor": lax.rem(z + k, RINGZ)})

    @pl.loop(0, RINGZ)
    def _(k):
        greet({"section": other, "tensor": lax.rem(z + k, RINGZ)})

    @pl.loop(1, SHARDS)
    def _(k):
        greet({"shard": lax.rem(shard + k, SHARDS)})

    sources = (
        (segments, segments_v),
        (rel_table, rel_v),
        (attn_gain, attn_gain_v),
        (w_query.at[0], query_w),
        (w_key.at[0], key_w),
        (w_value.at[0], value_w),
        (w_out.at[0], out_w),
        (ffn_gain, ffn_gain_v),
        (final_gain, final_gain_v),
        (dest_shard, dest_shard_v),
        (dest_slot, dest_slot_v),
        (w_proj, proj_w),
    )
    loads = [
        pltpu.make_async_copy(src, dst, load_sem.at[i]) for i, (src, dst) in enumerate(sources)
    ]
    first_rows = [
        pltpu.make_async_copy(
            embeds.at[0, :, pl.ds(g * COLS, COLS)], attn_in.at[g], rows_sem.at[g]
        )
        for g in range(GROUPS)
    ]
    for load in loads[:3]:
        load.start()

    @pl.when(section == 0)
    def _():
        for load in first_rows:
            load.start()

    for load in loads[3:]:
        load.start()
    for load in loads[:2]:
        load.wait()

    passage = lax.broadcasted_iota(jnp.int32, (PPM, SEQ), 0)
    counts = jnp.sum((segments_v[...] == passage).astype(F32), axis=-1, keepdims=True)
    first = jnp.sum((segments_v[...] < passage).astype(F32), axis=-1, keepdims=True)

    def members(token):
        at = token.astype(F32)
        return ((at >= first) & (at < first + counts)).astype(F32)

    lane = lax.broadcasted_iota(jnp.int32, (PPM, ROWS), 1)
    member_here[...] = members(lane + z * ROWS)

    def slots(place):
        slot = jnp.full_like(place, ORDER[0])
        for at in range(1, RINGZ):
            slot = jnp.where(place == at, ORDER[at], slot)
        return slot

    def tokens(position):
        return (((slots(position >> 5) + z) & 7) << 5) + (position & 31)

    lane = lax.broadcasted_iota(jnp.int32, (PPM, SEQ), 1)
    member = members(tokens(lane)).astype(BF16)
    bias[0] = lax.dot_general(
        member, member, (((0,), (0,)), ((), ())), preferred_element_type=F32
    )

    @pl.loop(0, RINGZ)
    def _(block):
        rows = pl.ds(pl.multiple_of(block * ROWS, ROWS), ROWS)
        inside = bias[0, rows, :] > 0.5
        i = tokens(lax.broadcasted_iota(jnp.int32, (ROWS, SEQ), 0) + block * ROWS)
        k = tokens(lax.broadcasted_iota(jnp.int32, (ROWS, SEQ), 1))
        ahead = k - i
        distance = jnp.abs(ahead)
        for head in range(HEADS):
            before = jnp.broadcast_to(rel_v[head : head + 1, 0:1], (ROWS, SEQ))
            after = jnp.broadcast_to(rel_v[head : head + 1, 16:17], (ROWS, SEQ))
            for code in range(1, 16):
                reached = distance >= lowest[code]
                before = jnp.where(reached, rel_v[head : head + 1, code : code + 1], before)
                after = jnp.where(
                    reached, rel_v[head : head + 1, 16 + code : 17 + code], after
                )
            value = jnp.where(ahead > 0, after, before)
            bias[head, rows, :] = jnp.where(inside, value, -1e30)

    @pl.when(section == 0)
    def _():
        for load in first_rows:
            load.wait()

    loads[2].wait()
    pl.semaphore_wait(barrier, RINGZ - 1 + RINGZ + SHARDS - 1)

    swaps = [
        copy_to(src, dst, swap_send.at[i], swap_recv.at[i], {"section": other})
        for i, (src, dst) in enumerate(
            (
                (w_gate.at[0], gate_w.at[y, x]),
                (w_up.at[0], up_w.at[y, x]),
                (w_down.at[0], down_w.at[y, x]),
            )
        )
    ]
    for swap in swaps:
        swap.start()

    attn_spread = Spread(z, attn_rows, ag_send.at[0], ag_recv.at[0])
    ffn_spread = Spread(z, ffn_rows, ag_send.at[1], ag_recv.at[1])
    attn_chains = Chains(z, attn_parts, attn_landed, rs_send.at[0], rs_recv.at[0])
    ffn_chains = Chains(z, ffn_parts, ffn_landed, rs_send.at[1], rs_recv.at[1])
    weights = Weights(y, x, gate_w, up_w, down_w, w_send, w_recv)
    hand = copy_to(handed, ffn_in, hand_send.at[0], hand_recv.at[0], {"section": other})

    def near(g):
        at = 0 if isinstance(g, pl.Slice) else g
        return copy_to(
            staged.at[g], ffn_rows.at[g, 0], near_send.at[0], near_recv.at[at], {"section": other}
        )

    def squares(value):
        return jnp.sum(value * value, axis=-1, keepdims=True)

    def scale_of(total):
        return lax.rsqrt(total * (1.0 / WIDTH) + EPS)

    no_squares = jnp.zeros((ROWS, 1), F32)

    def run_spread(spread, multiply):
        @pl.loop(0, GROUPS)
        def _(g):
            spread.step(2, g)

        @pl.loop(0, GROUPS)
        def _(g):
            spread.step(3, g)

        @pl.loop(0, GROUPS // 2)
        def _(pair):
            multiply(pair, 0)
            for g in (2 * pair, 2 * pair + 1):
                spread.step(4, g)

    def run_chains(chains, far, between, close):
        @pl.loop(0, GROUPS)
        def _(g):
            far(g)
            chains.forward(1, g, True)
            chains.forward(2, g, False)

        between()

        @pl.loop(0, GROUPS)
        def _(g):
            close(g)
            chains.forward(2, g, True)
            chains.forward(3, g, False)

        @pl.loop(0, GROUPS)
        def _(g):
            chains.forward(3, g, True)
            chains.forward(4, g, False)

        @pl.loop(0, GROUPS)
        def _(g):
            chains.forward(4, g, True)

    def finish(chains, before, after):
        def add(g, total):
            value = (before[g].astype(F32) + chains.total(g)).astype(BF16)
            after[g] = value
            return total + squares(value.astype(F32))

        return lax.fori_loop(0, GROUPS, add, no_squares)

    def part(place):
        blocks = (0, NEAR) if place == 0 else (NEAR, RINGZ - NEAR)
        return pl.ds(*blocks), pl.ds(blocks[0] * ROWS, blocks[1] * ROWS), blocks[1] * ROWS

    def attention():
        total = lax.fori_loop(
            0, GROUPS, lambda g, t: t + squares(attn_in[g].astype(F32)), no_squares
        )
        scale = scale_of(total)

        @pl.loop(0, GROUPS)
        def _(g):
            value = attn_in[g].astype(F32) * scale * attn_gain_v[:, group_cols(g)]
            attn_rows[g, 0] = value.astype(BF16)
            attn_spread.step(1, g)

        for load in loads[3:6]:
            load.wait()

        def multiply(pair, place):
            blocks, rows, count = part(place)
            for n, weight in enumerate((query_w, key_w, value_w)):
                cols = slice(n * 256, (n + 1) * 256)
                product = jnp.where(pair == 0, 0.0, sums[rows, cols])
                for g in (2 * pair, 2 * pair + 1):
                    product = product + jnp.dot(
                        attn_rows[g, blocks].reshape(count, COLS),
                        weight[group_cols(g), :],
                        preferred_element_type=F32,
                    )
                sums[rows, cols] = product

        run_spread(attn_spread, multiply)

        @pl.loop(0, GROUPS)
        def _(g):
            attn_spread.land(g)

        @pl.loop(0, GROUPS // 2)
        def _(pair):
            multiply(pair, 1)

        queries[...] = sums[:, 0:256].astype(BF16)
        keys[...] = sums[:, 256:512].astype(BF16)
        values[...] = sums[:, 512:768].astype(BF16)

        def attend(place):
            _, rows, count = part(place)
            head_lane = lax.broadcasted_iota(jnp.int32, (count, 128), 1)

            @pl.loop(0, HEADS // 2)
            def _(pair):
                cols = pl.ds(pl.multiple_of(pair * 128, 128), 128)
                query_pair, key_pair, value_pair = queries[rows, cols], keys[:, cols], values[:, cols]
                results = []
                for sub in range(2):
                    mine = (head_lane >= 64) if sub else (head_lane < 64)
                    one = jnp.where(mine, query_pair.astype(F32), 0.0).astype(BF16)
                    scores = lax.dot_general(
                        one, key_pair, (((1,), (1,)), ((), ())), preferred_element_type=F32
                    )
                    scores = scores + bias[pair * 2 + sub, rows, :]
                    powers = jnp.exp(scores - jnp.max(scores, axis=-1, keepdims=True))
                    shares_of = powers / jnp.sum(powers, axis=-1, keepdims=True)
                    results.append(
                        jnp.dot(shares_of.astype(BF16), value_pair, preferred_element_type=F32)
                    )
                context[rows, cols] = jnp.where(head_lane < 64, results[0], results[1]).astype(BF16)

        def project(g, place):
            blocks, rows, count = part(place)
            product = jnp.dot(
                context[rows, :], out_w[:, group_cols(g)], preferred_element_type=F32
            )
            attn_parts[g, blocks] = product.astype(BF16).reshape(
                count // ROWS, ROWS, COLS
            )

        attend(1)
        loads[6].wait()
        run_chains(
            attn_chains, lambda g: project(g, 1), lambda: attend(0), lambda g: project(g, 0)
        )
        loads[7].wait()
        scale = scale_of(finish(attn_chains, attn_in, handed))

        @pl.loop(0, GROUPS)
        def _(g):
            value = handed[g].astype(F32) * scale * ffn_gain_v[:, group_cols(g)]
            staged[g] = value.astype(BF16)
            for way in (0, 1):
                ffn_spread.move(way, 1, g, staged.at[g], other).start()
            near(g).start()

        hand.start()

    def feed():
        def multiply(pair, place):
            blocks, rows, count = part(place)
            for n, weight in enumerate((gate_w, up_w)):
                cols = slice(n * HID, (n + 1) * HID)
                product = jnp.where(pair == 0, 0.0, sums[rows, cols])
                for j in range(2):
                    product = product + jnp.dot(
                        ffn_rows[2 * pair + j, blocks].reshape(count, COLS),
                        weight[pair, 2 * j : 2 * j + 2].reshape(COLS, HID),
                        preferred_element_type=F32,
                    )
                sums[rows, cols] = product

        def activate(place):
            _, rows, count = part(place)
            gate = sums[rows, 0:HID]
            curve = jnp.tanh(0.7978845608 * (gate + 0.044715 * gate * gate * gate))
            hidden[rows, :] = (0.5 * gate * (1.0 + curve) * sums[rows, HID : 2 * HID]).astype(BF16)

        def first_multiply(pair, place):
            @pl.when(pair == 0)
            def _():
                @pl.loop(0, GROUPS)
                def _(g):
                    near(g).wait_recv()

                weights.land((0, 1))

            multiply(pair, place)

        run_spread(ffn_spread, first_multiply)
        activate(0)

        @pl.loop(0, GROUPS)
        def _(g):
            ffn_spread.land(g)

        @pl.loop(0, GROUPS // 2)
        def _(pair):
            multiply(pair, 1)

        activate(1)
        weights.land((2, 3))

        def project(g, place):
            blocks, rows, count = part(place)
            for j in range(2):
                product = jnp.dot(
                    hidden[rows, :],
                    down_w[g // 2, 2 * lax.rem(g, 2) + j],
                    preferred_element_type=F32,
                )
                ffn_parts[g, blocks, :, j * DK : (j + 1) * DK] = product.astype(BF16).reshape(
                    count // ROWS, ROWS, DK
                )

        run_chains(ffn_chains, lambda g: project(g, 1), lambda: None, lambda g: project(g, 0))
        hand.wait_recv()
        finish(ffn_chains, ffn_in, attn_in)

    @pl.loop(0, 3)
    def _(turn):
        role = lax.rem(turn + section, 3)

        @pl.when(role == 0)
        def _():
            attention()

        @pl.when(role == 1)
        def _():
            @pl.when(section == 0)
            def _():
                pl.semaphore_wait(free_sem, 1)

            def ready(array):
                if array < 3:
                    swaps[array].wait_recv()

            weights.run(ready)

            @pl.when(section == 1)
            def _():
                pl.semaphore_signal(
                    free_sem, inc=1, device_id={"section": other}, device_id_type=MESH
                )

        @pl.when(role == 2)
        def _():
            feed()

    def leave():
        for swap in swaps:
            swap.wait_send()
        weights.sent()
        hand.wait_send()
        near(pl.ds(0, GROUPS)).wait_send()
        attn_spread.sent()
        ffn_spread.sent(staged)
        attn_chains.sent()
        ffn_chains.sent()

    for load in loads[8:]:
        load.wait()

    def pool_copy(k):
        to = lax.rem(z + k, RINGZ)
        return copy_to(
            pooled.at[to], pooled_in.at[z], pool_send.at[k], pool_recv.at[k], {"tensor": to}
        )

    def share_copy(k, there):
        device = {"tensor": lax.rem(z + k, RINGZ)}
        at = k
        if there:
            device["section"] = other
            at = RINGZ + k
        return copy_to(shares.at[z], shares.at[z], share_send.at[at], share_recv.at[k], device)

    @pl.when(section == 0)
    def _():
        total = lax.fori_loop(
            0, GROUPS, lambda g, t: t + squares(attn_in[g].astype(F32)), no_squares
        )
        scale = scale_of(total)

        def pool(g):
            finished = attn_in[g].astype(F32) * scale * final_gain_v[:, group_cols(g)]
            return jnp.dot(
                member_here[...], finished, precision=HIGHEST, preferred_element_type=F32
            )

        for k in (4, 3, 5, 2, 6, 1, 7):
            to = lax.rem(z + k, RINGZ)
            pooled[to] = pool(to)
            pool_copy(k).start()
        pooled_in[z] = pool(z)
        leave()
        for k in range(1, RINGZ):
            pool_copy(k).wait_recv()
        means = (jnp.sum(pooled_in[...], axis=0) / counts).astype(BF16)
        shares[z] = jnp.dot(means, proj_w[...], preferred_element_type=F32)
        for k in (4, 3, 5, 2, 6, 1, 7):
            share_copy(k, False).start()
            share_copy(k, True).start()
        share_copy(0, True).start()

    @pl.when(section == 1)
    def _():
        leave()
        share_copy(0, True).wait_recv()

    row = lax.broadcasted_iota(jnp.int32, (SHARDS * 8, PPM), 0)
    chosen = (dest_shard_v[...] == (row >> 3) + section * SHARDS) & (dest_slot_v[...] == (row & 3))
    chosen = chosen.astype(F32)
    for k in range(1, RINGZ):
        share_copy(k, False).wait_recv()
    projected = shares[0]
    for d in range(1, RINGZ):
        projected = projected + shares[d]
    mean_square = jnp.mean(projected * projected, axis=-1, keepdims=True)
    unit = (projected * lax.rsqrt(mean_square + EPS)).astype(BF16).astype(F32)
    lower = jnp.dot(chosen, unit[:, :HALF], preferred_element_type=F32)
    upper = jnp.dot(chosen, unit[:, HALF:], preferred_element_type=F32)
    row = lax.broadcasted_iota(jnp.int32, (SHARDS * 8, HALF), 0)
    placed[...] = jnp.where((row & 7) < 4, lower, upper).reshape(SHARDS, 8, HALF)

    def place_copy(k):
        to = lax.rem(shard + k, SHARDS)
        return copy_to(
            placed.at[to], placed_in.at[shard], place_send.at[k], place_recv.at[k], {"shard": to}
        )

    @pl.loop(1, SHARDS)
    def _(k):
        place_copy(k).start()

    placed_in[shard] = placed[shard]

    @pl.when(section == 0)
    def _():
        for k in range(1, RINGZ):
            pool_copy(k).wait_send()
            share_copy(k, False).wait_send()
        for k in range(RINGZ):
            share_copy(k, True).wait_send()

    @pl.loop(1, SHARDS)
    def _(k):
        place_copy(k).wait_send()

    @pl.loop(1, SHARDS)
    def _(k):
        place_copy(k).wait_recv()

    rows = jnp.sum(placed_in[...], axis=0)
    index[:, 0:HALF] = rows[0:4].astype(BF16)
    index[:, HALF:EMB] = rows[4:8].astype(BF16)


def on_device(
    embeds,
    segments,
    rel_table,
    attn_gain,
    w_query,
    w_key,
    w_value,
    w_out,
    ffn_gain,
    w_gate,
    w_up,
    w_down,
    final_gain,
    w_proj,
    dest_shard,
    dest_slot,
):
    vmem = pl.BlockSpec(memory_space=pltpu.VMEM)
    anywhere = pl.BlockSpec(memory_space=pl.ANY)
    dma = pltpu.SemaphoreType.DMA
    rows = pltpu.VMEM((GROUPS, RINGZ, ROWS, COLS), BF16)
    landed = pltpu.VMEM((2, 4, GROUPS, ROWS, COLS), BF16)
    own = pltpu.VMEM((GROUPS, ROWS, COLS), BF16)
    heads = pltpu.VMEM((SEQ, 256), BF16)
    scratch = [
        pltpu.VMEM((1, SEQ), jnp.int32),
        pltpu.VMEM((HEADS, 32), F32),
        pltpu.VMEM((1, WIDTH), F32),
        pltpu.VMEM((1, WIDTH), F32),
        pltpu.VMEM((1, WIDTH), F32),
        pltpu.VMEM((1, PPM), jnp.int32),
        pltpu.VMEM((1, PPM), jnp.int32),
        pltpu.VMEM((WIDTH, 256), BF16),
        pltpu.VMEM((WIDTH, 256), BF16),
        pltpu.VMEM((WIDTH, 256), BF16),
        pltpu.VMEM((256, WIDTH), BF16),
        pltpu.VMEM((COLS, EMB), BF16),
        pltpu.VMEM((SIDE, SIDE, DK, HID), BF16),
        pltpu.VMEM((SIDE, SIDE, DK, HID), BF16),
        pltpu.VMEM((SIDE, SIDE, HID, DK), BF16),
        pltpu.VMEM((HEADS, SEQ, SEQ), F32),
        pltpu.VMEM((PPM, ROWS), F32),
        rows,
        rows,
        landed,
        rows,
        rows,
        landed,
        own,
        own,
        own,
        own,
        heads,
        heads,
        heads,
        heads,
        pltpu.VMEM((SEQ, 2 * HID), F32),
        pltpu.VMEM((SEQ, HID), BF16),
        pltpu.VMEM((RINGZ, PPM, COLS), F32),
        pltpu.VMEM((RINGZ, PPM, COLS), F32),
        pltpu.VMEM((RINGZ, PPM, EMB), F32),
        pltpu.VMEM((SHARDS, 8, HALF), F32),
        pltpu.VMEM((SHARDS, 8, HALF), F32),
        dma((12,)),
        dma((GROUPS,)),
        dma((3,)),
        dma((3,)),
        dma((1,)),
        dma((1,)),
        dma((1,)),
        dma((GROUPS,)),
        dma((2, 8)),
        dma((2, 8, GROUPS)),
        dma((2, 16)),
        dma((2, 16, GROUPS)),
        dma((4, 20)),
        dma((4, 20)),
        dma((RINGZ,)),
        dma((RINGZ,)),
        dma((2 * RINGZ,)),
        dma((RINGZ,)),
        dma((SHARDS,)),
        dma((SHARDS,)),
        pltpu.SemaphoreType.REGULAR,
    ]
    return pl.pallas_call(
        kernel,
        out_shape=jax.ShapeDtypeStruct((4, EMB), BF16),
        in_specs=[anywhere] * 16,
        out_specs=vmem,
        scratch_shapes=scratch,
        compiler_params=pltpu.CompilerParams(
            collective_id=0, has_side_effects=True, vmem_limit_bytes=58 * 1024 * 1024
        ),
    )(
        embeds,
        segments,
        rel_table.T,
        attn_gain,
        w_query,
        w_key,
        w_value,
        w_out,
        ffn_gain,
        w_gate,
        w_up,
        w_down,
        final_gain.reshape(1, -1),
        w_proj,
        dest_shard,
        dest_slot,
    )


def solution(mesh):
    in_specs = (
        P("shard", "tensor", None),
        P("shard", None),
        P(None, "tensor"),
        P("section", None),
        P("section", None, "tensor"),
        P("section", None, "tensor"),
        P("section", None, "tensor"),
        P("section", "tensor", None),
        P("section", None),
        P("section", "shard", "tensor"),
        P("section", "shard", "tensor"),
        P("section", "tensor", "shard"),
        P(),
        P("tensor", None),
        P("shard", None),
        P("shard", None),
    )
    out_specs = P(("section", "shard"), None)
    return jax.shard_map(
        on_device, mesh=mesh, in_specs=in_specs, out_specs=out_specs, check_vma=False
    )
```

```python
import jax
import jax.numpy as jnp
from jax import lax
from jax.experimental import pallas as pl
from jax.experimental.pallas import tpu as pltpu
from jax.sharding import PartitionSpec as P

MESH = pl.DeviceIdType.MESH
F32 = jnp.float32
BF16 = jnp.bfloat16
HIGHEST = lax.Precision.HIGHEST

ROWS = 32
CHUNK = 16
RINGZ = 8
SIDE = 4
SHARDS = SIDE * SIDE
WIDTH = 4096
GROUPS = 8
COLS = WIDTH // GROUPS
PAIRS = GROUPS // 2
SEQ = 256
NEAR = 5
HEADS = 4
PPM = 8
DK = 256
HID = 640
EMB = 768
HALF = EMB // 2
EPS = 1e-06

ORDER = (0, 1, 7, 2, 6, 3, 5, 4)
PLACE = tuple(ORDER.index(slot) for slot in range(RINGZ))
lowest = (0, 1, 2, 3, 4, 5, 6, 7, 8, 12, 16, 23, 32, 46, 64, 91)


def copy_to(src, dst, send, recv, device):
    return pltpu.make_async_remote_copy(
        src_ref=src,
        dst_ref=dst,
        send_sem=send,
        recv_sem=recv,
        device_id=device,
        device_id_type=MESH,
    )


def part_rows(half):
    return pl.ds(half * CHUNK, CHUNK)


def group_cols(g):
    return pl.ds(pl.multiple_of(g * COLS, COLS), COLS)


class Spread:
    def __init__(self, z, rows, send, recv):
        self.beside = (lax.rem(z + 1, RINGZ), lax.rem(z + RINGZ - 1, RINGZ))
        self.rows, self.send, self.recv = rows, send, recv

    def move(self, way, hop, far, q, src=None, section=None):
        source, target = (RINGZ - hop + 1, RINGZ - hop) if way == 0 else (hop - 1, hop)
        rows = part_rows(way if far else 1 - way)
        groups = pl.ds(0, GROUPS) if q is None else pl.ds(2 * q, 2)
        if src is None:
            src = self.rows.at[groups, PLACE[source % RINGZ], rows]
        else:
            src = src.at[groups, rows]
        device = {"tensor": self.beside[way]}
        if section is not None:
            device["section"] = section
        if hop < 3 or (hop == 3 and far):
            at = (hop - 1) * 8 + (0 if far else 4) + (0 if q is None else q)
        else:
            at = 20 if hop == 3 else 21
        return copy_to(
            src,
            self.rows.at[groups, PLACE[target % RINGZ], rows],
            self.send.at[way, 2 * hop - (2 if far else 1)],
            self.recv.at[way, at],
            device,
        )

    def step(self, hop, far, q):
        for way in (0, 1):
            if hop > 1:
                self.move(way, hop - 1, far, q).wait_recv()
            self.move(way, hop, far, q).start()

    def land(self):
        for way in (0, 1):
            self.move(way, 3, False, None).wait_recv()
        for way in (0, 1):
            self.move(way, 4, True, None).wait_recv()

    def sent(self, src=None):
        for way in (0, 1):
            for hop in (1, 2, 3, 4):
                for far in (True, False)[: 2 if hop < 4 else 1]:
                    self.move(way, hop, far, None, src if hop == 1 else None).wait_send()


class Chains:
    def __init__(self, z, parts, landed, send, recv):
        self.beside = (lax.rem(z + 1, RINGZ), lax.rem(z + RINGZ - 1, RINGZ))
        self.parts, self.landed, self.send, self.recv = parts, landed, send, recv

    def place(self, way, hop):
        return PLACE[5 - hop if way == 0 else RINGZ - 5 + hop]

    def move(self, way, hop, far, q):
        rows = part_rows(way if far else 1 - way)
        groups = pl.ds(0, GROUPS) if q is None else pl.ds(2 * q, 2)
        kind = 2 * hop - (2 if far else 1)
        kind = kind - 1 if hop > 1 else kind
        at = kind * 4 + (0 if q is None or kind == 6 else q)
        return copy_to(
            self.parts.at[groups, self.place(way, hop), rows],
            self.landed.at[way, hop - 1, groups, rows],
            self.send.at[way, kind],
            self.recv.at[way, at],
            {"tensor": self.beside[way]},
        )

    def forward(self, hop, far, q):
        for way in (0, 1):
            if hop > (1 if far else 2):
                self.move(way, hop - 1, far, q).wait_recv()
                place = self.place(way, hop)
                rows = part_rows(way if far else 1 - way)
                groups = pl.ds(2 * q, 2)
                total = self.parts[groups, place, rows].astype(F32) + self.landed[
                    way, hop - 2, groups, rows
                ].astype(F32)
                self.parts[groups, place, rows] = total.astype(BF16)
            self.move(way, hop, far, q).start()

    def total(self, g):
        own = self.parts[g, 0].astype(F32)
        return own + self.landed[0, 3, g].astype(F32) + self.landed[1, 3, g].astype(F32)

    def sent(self):
        for way in (0, 1):
            for hop in (1, 2, 3, 4):
                for far in (True, False)[: 2 if hop > 1 else 1]:
                    self.move(way, hop, far, None).wait_send()


class Weights:
    def __init__(self, y, x, gate, up, down, send, recv):
        self.y, self.x = y, x
        self.arrays = ((gate, 0, DK), (up, 0, DK), (down, 0, HID // 2), (down, HID // 2, HID // 2))
        self.send, self.recv = send, recv

    def piece(self, array, first, second, sign):
        ref, start, size = self.arrays[array]
        if sign is not None:
            size = size // 2
            start = start + sign * size
        along_x, along_y = (first, second) if array % 2 == 0 else (second, first)
        at_x, at_y = lax.rem(self.x + along_x, SIDE), lax.rem(self.y + along_y, SIDE)
        return ref.at[at_y, at_x, pl.ds(start, size)]

    def all_of(self, array, stage, hop):
        ref, start, size = self.arrays[array]
        rows = pl.ds(start, size if hop == 0 else size // 2)
        ref = ref.at[0, pl.ds(0, 2), rows] if stage == 0 else ref.at[pl.ds(0, 2), :, rows]
        return copy_to(
            ref,
            ref,
            self.send.at[array, stage * 2 + hop],
            self.recv.at[array, 2 if stage == 0 else 11],
            {"shard": self.y * SIDE + self.x},
        )

    def copy(self, array, stage, hop, line, sign, landing):
        step = 1 if sign == 0 else SIDE - 1
        back = SIDE - step
        away = (back if hop == 1 else 0) + (back if landing else 0)
        if stage == 0:
            ref = self.piece(array, away % SIDE, 0, None if hop == 0 else sign)
            at = sign if hop == 0 else 2
        else:
            ref = self.piece(array, line, away % SIDE, None if hop == 0 else sign)
            at = 3 + line * 2 + sign if hop == 0 else 11
        on_x = (array % 2 == 0) == (stage == 0)
        if on_x:
            shard = self.y * SIDE + lax.rem(self.x + step, SIDE)
        else:
            shard = lax.rem(self.y + step, SIDE) * SIDE + self.x
        return copy_to(
            ref,
            ref,
            self.send.at[array, stage * 2 + hop],
            self.recv.at[array, at],
            {"shard": shard},
        )

    def go(self, array, stage, hop, line, sign):
        self.copy(array, stage, hop, line, sign, False).start()

    def wait(self, array, stage, hop, line, sign):
        self.copy(array, stage, hop, line, sign, True).wait_recv()

    def run(self, ready):
        both = (0, 1)
        for array in range(4):
            ready(array)
            for sign in both:
                self.go(array, 0, 0, 0, sign)
                self.go(array, 1, 0, 0, sign)
        for array in range(4):
            for sign in both:
                self.wait(array, 0, 0, 0, sign)
                self.go(array, 0, 1, 0, sign)
                line = SIDE - 1 if sign == 0 else 1
                for other in both:
                    self.go(array, 1, 0, line, other)
        for array in range(4):
            self.all_of(array, 0, 1).wait_recv()
            for sign in both:
                self.go(array, 1, 0, 2, sign)
        for array in range(4):
            for line in (0, 1, 3, 2):
                for sign in both:
                    self.wait(array, 1, 0, line, sign)
                    self.go(array, 1, 1, line, sign)

    def land(self, arrays):
        for array in arrays:
            self.all_of(array, 1, 1).wait_recv()

    def sent(self):
        for array in range(4):
            for stage in (0, 1):
                for hop in (0, 1):
                    self.all_of(array, stage, hop).wait_send()


def kernel(
    embeds,
    segments,
    rel_table,
    attn_gain,
    w_query,
    w_key,
    w_value,
    w_out,
    ffn_gain,
    w_gate,
    w_up,
    w_down,
    final_gain,
    w_proj,
    dest_shard,
    dest_slot,
    index,
    segments_v,
    rel_v,
    attn_gain_v,
    ffn_gain_v,
    final_gain_v,
    dest_shard_v,
    dest_slot_v,
    query_w,
    key_w,
    value_w,
    out_w,
    proj_w,
    gate_w,
    up_w,
    down_w,
    bias,
    member_here,
    attn_rows,
    attn_parts,
    attn_landed,
    ffn_rows,
    ffn_parts,
    ffn_landed,
    attn_in,
    handed,
    ffn_in,
    staged,
    queries,
    keys,
    values,
    context,
    sums,
    hidden,
    pooled,
    pooled_in,
    shares,
    units,
    row_squares,
    placed,
    placed_in,
    load_sem,
    rows_sem,
    swap_send,
    swap_recv,
    hand_send,
    hand_recv,
    near_send,
    near_recv,
    ag_send,
    ag_recv,
    rs_send,
    rs_recv,
    w_send,
    w_recv,
    pool_send,
    pool_recv,
    share_send,
    share_recv,
    unit_send,
    unit_recv,
    place_send,
    place_recv,
    free_sem,
):
    section = lax.axis_index("section")
    z = lax.axis_index("tensor")
    shard = lax.axis_index("shard")
    y, x = shard // SIDE, lax.rem(shard, SIDE)
    other = 1 - section

    barrier = pltpu.get_barrier_semaphore()

    def greet(device):
        pl.semaphore_signal(barrier, inc=1, device_id=device, device_id_type=MESH)

    @pl.loop(1, RINGZ)
    def _(k):
        greet({"tensor": lax.rem(z + k, RINGZ)})

    for k in (0, 1, RINGZ - 1):
        greet({"section": other, "tensor": lax.rem(z + k, RINGZ)})

    @pl.loop(1, SHARDS)
    def _(k):
        greet({"shard": lax.rem(shard + k, SHARDS)})

    sources = (
        (segments, segments_v),
        (rel_table, rel_v),
        (attn_gain, attn_gain_v),
        (w_query.at[0], query_w),
        (w_key.at[0], key_w),
        (w_value.at[0], value_w),
        (w_out.at[0], out_w),
        (ffn_gain, ffn_gain_v),
        (final_gain, final_gain_v),
        (dest_shard, dest_shard_v),
        (dest_slot, dest_slot_v),
        (w_proj, proj_w),
    )
    loads = [
        pltpu.make_async_copy(src, dst, load_sem.at[i]) for i, (src, dst) in enumerate(sources)
    ]
    first_rows = [
        pltpu.make_async_copy(
            embeds.at[0, :, pl.ds(g * COLS, COLS)], attn_in.at[g], rows_sem.at[0]
        )
        for g in range(GROUPS)
    ]
    for load in loads[:3]:
        load.start()

    @pl.when(section == 0)
    def _():
        for load in first_rows:
            load.start()

    for load in loads[3:]:
        load.start()
    for load in loads[:2]:
        load.wait()

    def squares(value):
        return jnp.sum(value * value, axis=-1, keepdims=True)

    def row_scale():
        return lax.rsqrt(row_squares[:, 0:1] * (1.0 / WIDTH) + EPS)

    no_squares = jnp.zeros((ROWS, 1), F32)

    passage = lax.broadcasted_iota(jnp.int32, (PPM, SEQ), 0)
    counts = jnp.sum((segments_v[...] == passage).astype(F32), axis=-1, keepdims=True)
    first = jnp.sum((segments_v[...] < passage).astype(F32), axis=-1, keepdims=True)

    def members(token):
        at = token.astype(F32)
        return ((at >= first) & (at < first + counts)).astype(F32)

    lane = lax.broadcasted_iota(jnp.int32, (PPM, ROWS), 1)
    member_here[...] = members(lane + z * ROWS)

    def slots(place):
        slot = jnp.full_like(place, ORDER[0])
        for at in range(1, RINGZ):
            slot = jnp.where(place == at, ORDER[at], slot)
        return slot

    def tokens(position):
        return (((slots(position >> 5) + z) & 7) << 5) + (position & 31)

    lane = lax.broadcasted_iota(jnp.int32, (PPM, SEQ), 1)
    member = members(tokens(lane)).astype(BF16)
    bias[0] = lax.dot_general(
        member, member, (((0,), (0,)), ((), ())), preferred_element_type=F32
    )

    @pl.loop(0, RINGZ)
    def _(block):
        rows = pl.ds(pl.multiple_of(block * ROWS, ROWS), ROWS)
        inside = bias[0, rows, :] > 0.5
        i = tokens(lax.broadcasted_iota(jnp.int32, (ROWS, SEQ), 0) + block * ROWS)
        k = tokens(lax.broadcasted_iota(jnp.int32, (ROWS, SEQ), 1))
        ahead = k - i
        distance = jnp.abs(ahead)
        for head in range(HEADS):
            before = jnp.broadcast_to(rel_v[head : head + 1, 0:1], (ROWS, SEQ))
            after = jnp.broadcast_to(rel_v[head : head + 1, 16:17], (ROWS, SEQ))
            for code in range(1, 16):
                reached = distance >= lowest[code]
                before = jnp.where(reached, rel_v[head : head + 1, code : code + 1], before)
                after = jnp.where(
                    reached, rel_v[head : head + 1, 16 + code : 17 + code], after
                )
            value = jnp.where(ahead > 0, after, before)
            bias[head, rows, :] = jnp.where(inside, value, -1e30)

    @pl.when(section == 0)
    def _():
        pltpu.make_async_copy(attn_in, attn_in, rows_sem.at[0]).wait()
        total = lax.fori_loop(
            0, GROUPS, lambda g, t: t + squares(attn_in[g].astype(F32)), no_squares
        )
        row_squares[...] = jnp.broadcast_to(total, row_squares.shape)

    loads[2].wait()
    pl.semaphore_wait(barrier, RINGZ - 1 + 3 + SHARDS - 1)

    swaps = [
        copy_to(src, dst, swap_send.at[i], swap_recv.at[i], {"section": other})
        for i, (src, dst) in enumerate(
            (
                (w_gate.at[0], gate_w.at[y, x]),
                (w_up.at[0], up_w.at[y, x]),
                (w_down.at[0], down_w.at[y, x]),
            )
        )
    ]
    for swap in swaps:
        swap.start()

    attn_spread = Spread(z, attn_rows, ag_send.at[0], ag_recv.at[0])
    ffn_spread = Spread(z, ffn_rows, ag_send.at[1], ag_recv.at[1])
    attn_chains = Chains(z, attn_parts, attn_landed, rs_send.at[0], rs_recv.at[0])
    ffn_chains = Chains(z, ffn_parts, ffn_landed, rs_send.at[1], rs_recv.at[1])
    weights = Weights(y, x, gate_w, up_w, down_w, w_send, w_recv)
    hand = copy_to(handed, ffn_in, hand_send.at[0], hand_recv.at[0], {"section": other})

    near = copy_to(
        staged, ffn_rows.at[:, 0], near_send.at[0], near_recv.at[0], {"section": other}
    )

    def run_spread(spread, multiply):
        for hop in (2, 3):
            for far in (True, False):

                @pl.loop(0, PAIRS)
                def _(q):
                    spread.step(hop, far, q)

        @pl.loop(0, PAIRS)
        def _(q):
            multiply(q, 0)
            spread.step(4, True, q)

    def run_chains(chains, far, between, close):
        @pl.loop(0, PAIRS)
        def _(q):
            far(2 * q)
            far(2 * q + 1)
            chains.forward(1, True, q)
            chains.forward(2, False, q)

        between()

        @pl.loop(0, PAIRS)
        def _(q):
            close(2 * q)
            close(2 * q + 1)
            chains.forward(2, True, q)

        for hop, is_far in ((3, False), (3, True), (4, False), (4, True)):

            @pl.loop(0, PAIRS)
            def _(q):
                chains.forward(hop, is_far, q)

    def finish(chains, before, after):
        for way in (0, 1):
            chains.move(way, 4, False, None).wait_recv()

        def add(q, total):
            for way in (0, 1):
                chains.move(way, 4, True, q).wait_recv()
            for g in (2 * q, 2 * q + 1):
                value = (before[g].astype(F32) + chains.total(g)).astype(BF16)
                after[g] = value
                total = total + squares(value.astype(F32))
            return total

        total = lax.fori_loop(0, PAIRS, add, no_squares)
        row_squares[...] = jnp.broadcast_to(total, row_squares.shape)

    def part(place):
        blocks = (0, NEAR) if place == 0 else (NEAR, RINGZ - NEAR)
        return pl.ds(*blocks), pl.ds(blocks[0] * ROWS, blocks[1] * ROWS), blocks[1] * ROWS

    def attention():
        scale = row_scale()

        @pl.loop(0, PAIRS)
        def _(q):
            for g in (2 * q, 2 * q + 1):
                value = attn_in[g].astype(F32) * scale * attn_gain_v[:, group_cols(g)]
                attn_rows[g, 0] = value.astype(BF16)
            attn_spread.step(1, True, q)

        @pl.loop(0, PAIRS)
        def _(q):
            attn_spread.step(1, False, q)

        for load in loads[3:6]:
            load.wait()

        def multiply(pair, place):
            blocks, rows, count = part(place)
            for n, weight in enumerate((query_w, key_w, value_w)):
                cols = slice(n * 256, (n + 1) * 256)
                product = jnp.where(pair == 0, 0.0, sums[rows, cols])
                for g in (2 * pair, 2 * pair + 1):
                    product = product + jnp.dot(
                        attn_rows[g, blocks].reshape(count, COLS),
                        weight[group_cols(g), :],
                        preferred_element_type=F32,
                    )
                sums[rows, cols] = product

        run_spread(attn_spread, multiply)

        attn_spread.land()

        @pl.loop(0, GROUPS // 2)
        def _(pair):
            multiply(pair, 1)

        queries[...] = sums[:, 0:256].astype(BF16)
        keys[...] = sums[:, 256:512].astype(BF16)
        values[...] = sums[:, 512:768].astype(BF16)

        def attend(place):
            _, rows, count = part(place)
            head_lane = lax.broadcasted_iota(jnp.int32, (count, 128), 1)

            @pl.loop(0, HEADS // 2)
            def _(pair):
                cols = pl.ds(pl.multiple_of(pair * 128, 128), 128)
                query_pair, key_pair, value_pair = queries[rows, cols], keys[:, cols], values[:, cols]
                results = []
                for sub in range(2):
                    mine = (head_lane >= 64) if sub else (head_lane < 64)
                    one = jnp.where(mine, query_pair.astype(F32), 0.0).astype(BF16)
                    scores = lax.dot_general(
                        one, key_pair, (((1,), (1,)), ((), ())), preferred_element_type=F32
                    )
                    scores = scores + bias[pair * 2 + sub, rows, :]
                    powers = jnp.exp(scores - jnp.max(scores, axis=-1, keepdims=True))
                    shares_of = powers / jnp.sum(powers, axis=-1, keepdims=True)
                    results.append(
                        jnp.dot(shares_of.astype(BF16), value_pair, preferred_element_type=F32)
                    )
                context[rows, cols] = jnp.where(head_lane < 64, results[0], results[1]).astype(BF16)

        def project(g, place):
            blocks, rows, count = part(place)
            product = jnp.dot(
                context[rows, :], out_w[:, group_cols(g)], preferred_element_type=F32
            )
            attn_parts[g, blocks] = product.astype(BF16).reshape(
                count // ROWS, ROWS, COLS
            )

        attend(1)
        loads[6].wait()
        run_chains(
            attn_chains, lambda g: project(g, 1), lambda: attend(0), lambda g: project(g, 0)
        )
        loads[7].wait()
        finish(attn_chains, attn_in, handed)
        scale = row_scale()

        def start(far, q):
            for way in (0, 1):
                ffn_spread.move(way, 1, far, q, staged, other).start()

        @pl.loop(0, PAIRS)
        def _(q):
            for g in (2 * q, 2 * q + 1):
                value = handed[g].astype(F32) * scale * ffn_gain_v[:, group_cols(g)]
                staged[g] = value.astype(BF16)
            start(True, q)

        @pl.loop(0, PAIRS)
        def _(q):
            start(False, q)

        near.start()
        hand.start()

    def feed():
        def multiply(pair, place):
            blocks, rows, count = part(place)
            for n, weight in enumerate((gate_w, up_w)):
                cols = slice(n * HID, (n + 1) * HID)
                product = jnp.where(pair == 0, 0.0, sums[rows, cols])
                for j in range(2):
                    product = product + jnp.dot(
                        ffn_rows[2 * pair + j, blocks].reshape(count, COLS),
                        weight[pair, 2 * j : 2 * j + 2].reshape(COLS, HID),
                        preferred_element_type=F32,
                    )
                sums[rows, cols] = product

        def activate(place):
            _, rows, count = part(place)
            gate = sums[rows, 0:HID]
            curve = jnp.tanh(0.7978845608 * (gate + 0.044715 * gate * gate * gate))
            hidden[rows, :] = (0.5 * gate * (1.0 + curve) * sums[rows, HID : 2 * HID]).astype(BF16)

        def first_multiply(pair, place):
            @pl.when(pair == 0)
            def _():
                near.wait_recv()
                weights.land((0, 1))

            multiply(pair, place)

        run_spread(ffn_spread, first_multiply)
        activate(0)

        ffn_spread.land()

        @pl.loop(0, GROUPS // 2)
        def _(pair):
            multiply(pair, 1)

        activate(1)
        weights.land((2, 3))

        def project(g, place):
            blocks, rows, count = part(place)
            for j in range(2):
                product = jnp.dot(
                    hidden[rows, :],
                    down_w[g // 2, 2 * lax.rem(g, 2) + j],
                    preferred_element_type=F32,
                )
                ffn_parts[g, blocks, :, j * DK : (j + 1) * DK] = product.astype(BF16).reshape(
                    count // ROWS, ROWS, DK
                )

        run_chains(ffn_chains, lambda g: project(g, 1), lambda: None, lambda g: project(g, 0))
        hand.wait_recv()
        finish(ffn_chains, ffn_in, attn_in)

    @pl.loop(0, 3)
    def _(turn):
        role = lax.rem(turn + section, 3)

        @pl.when(role == 0)
        def _():
            attention()

        @pl.when(role == 1)
        def _():
            @pl.when(section == 0)
            def _():
                pl.semaphore_wait(free_sem, 1)

            def ready(array):
                if array < 3:
                    swaps[array].wait_recv()

            weights.run(ready)

            @pl.when(section == 1)
            def _():
                pl.semaphore_signal(
                    free_sem, inc=1, device_id={"section": other}, device_id_type=MESH
                )

        @pl.when(role == 2)
        def _():
            feed()

    def leave():
        for swap in swaps:
            swap.wait_send()
        weights.sent()
        hand.wait_send()
        near.wait_send()
        attn_spread.sent()
        ffn_spread.sent(staged)
        attn_chains.sent()
        ffn_chains.sent()

    for load in loads[8:]:
        load.wait()

    def pool_copy(k):
        to = lax.rem(z + k, RINGZ)
        return copy_to(
            pooled.at[to], pooled_in.at[z], pool_send.at[0], pool_recv.at[0], {"tensor": to}
        )

    def share_copy(k):
        device = {"tensor": lax.rem(z + k, RINGZ)}
        return copy_to(shares.at[z], shares.at[z], share_send.at[0], share_recv.at[0], device)

    def place_copy(k):
        to = lax.rem(shard + k, SHARDS)
        return copy_to(
            placed.at[to], placed_in.at[shard], place_send.at[0], place_recv.at[0], {"shard": to}
        )

    others = pl.ds(0, RINGZ - 1)
    all_pool = copy_to(
        pooled.at[others], pooled_in.at[others], pool_send.at[0], pool_recv.at[0], {"tensor": z}
    )
    all_share = copy_to(
        shares.at[others], shares.at[others], share_send.at[0], share_recv.at[0], {"tensor": z}
    )
    rest = pl.ds(0, SHARDS - 1)
    all_place = copy_to(
        placed.at[rest], placed_in.at[rest], place_send.at[0], place_recv.at[0], {"shard": shard}
    )
    unit_copy = copy_to(units, units, unit_send.at[0], unit_recv.at[0], {"section": other})

    @pl.when(section == 0)
    def _():
        scale = row_scale()

        def pool(g):
            finished = attn_in[g].astype(F32) * scale * final_gain_v[:, group_cols(g)]
            return jnp.dot(
                member_here[...], finished, precision=HIGHEST, preferred_element_type=F32
            )

        for k in (4, 3, 5, 2, 6, 1, 7):
            to = lax.rem(z + k, RINGZ)
            pooled[to] = pool(to)
            pool_copy(k).start()
        pooled_in[z] = pool(z)
        leave()
        all_pool.wait_recv()
        means = (jnp.sum(pooled_in[...], axis=0) / counts).astype(BF16)
        shares[z] = jnp.dot(means, proj_w[...], preferred_element_type=F32)
        for k in (4, 3, 5, 2, 6, 1, 7):
            share_copy(k).start()
        all_pool.wait_send()
        all_share.wait_recv()
        projected = shares[0]
        for d in range(1, RINGZ):
            projected = projected + shares[d]
        mean_square = jnp.mean(projected * projected, axis=-1, keepdims=True)
        units[...] = (projected * lax.rsqrt(mean_square + EPS)).astype(BF16).astype(F32)
        unit_copy.start()

    @pl.when(section == 1)
    def _():
        leave()
        unit_copy.wait_recv()

    row = lax.broadcasted_iota(jnp.int32, (SHARDS * 8, PPM), 0)
    chosen = (dest_shard_v[...] == (row >> 3) + section * SHARDS) & (dest_slot_v[...] == (row & 3))
    chosen = chosen.astype(F32)
    lower = jnp.dot(chosen, units[:, :HALF], preferred_element_type=F32)
    upper = jnp.dot(chosen, units[:, HALF:], preferred_element_type=F32)
    row = lax.broadcasted_iota(jnp.int32, (SHARDS * 8, HALF), 0)
    placed[...] = jnp.where((row & 7) < 4, lower, upper).reshape(SHARDS, 8, HALF)

    @pl.loop(1, SHARDS)
    def _(k):
        place_copy(k).start()

    placed_in[shard] = placed[shard]

    @pl.when(section == 0)
    def _():
        all_share.wait_send()
        unit_copy.wait_send()

    all_place.wait_send()
    all_place.wait_recv()
    rows = jnp.sum(placed_in[...], axis=0)
    index[:, 0:HALF] = rows[0:4].astype(BF16)
    index[:, HALF:EMB] = rows[4:8].astype(BF16)


def on_device(
    embeds,
    segments,
    rel_table,
    attn_gain,
    w_query,
    w_key,
    w_value,
    w_out,
    ffn_gain,
    w_gate,
    w_up,
    w_down,
    final_gain,
    w_proj,
    dest_shard,
    dest_slot,
):
    vmem = pl.BlockSpec(memory_space=pltpu.VMEM)
    anywhere = pl.BlockSpec(memory_space=pl.ANY)
    dma = pltpu.SemaphoreType.DMA
    rows = pltpu.VMEM((GROUPS, RINGZ, ROWS, COLS), BF16)
    landed = pltpu.VMEM((2, 4, GROUPS, ROWS, COLS), BF16)
    own = pltpu.VMEM((GROUPS, ROWS, COLS), BF16)
    heads = pltpu.VMEM((SEQ, 256), BF16)
    scratch = [
        pltpu.VMEM((1, SEQ), jnp.int32),
        pltpu.VMEM((HEADS, 32), F32),
        pltpu.VMEM((1, WIDTH), F32),
        pltpu.VMEM((1, WIDTH), F32),
        pltpu.VMEM((1, WIDTH), F32),
        pltpu.VMEM((1, PPM), jnp.int32),
        pltpu.VMEM((1, PPM), jnp.int32),
        pltpu.VMEM((WIDTH, 256), BF16),
        pltpu.VMEM((WIDTH, 256), BF16),
        pltpu.VMEM((WIDTH, 256), BF16),
        pltpu.VMEM((256, WIDTH), BF16),
        pltpu.VMEM((COLS, EMB), BF16),
        pltpu.VMEM((SIDE, SIDE, DK, HID), BF16),
        pltpu.VMEM((SIDE, SIDE, DK, HID), BF16),
        pltpu.VMEM((SIDE, SIDE, HID, DK), BF16),
        pltpu.VMEM((HEADS, SEQ, SEQ), F32),
        pltpu.VMEM((PPM, ROWS), F32),
        rows,
        rows,
        landed,
        rows,
        rows,
        landed,
        own,
        own,
        own,
        own,
        heads,
        heads,
        heads,
        heads,
        pltpu.VMEM((SEQ, 2 * HID), F32),
        pltpu.VMEM((SEQ, HID), BF16),
        pltpu.VMEM((RINGZ, PPM, COLS), F32),
        pltpu.VMEM((RINGZ, PPM, COLS), F32),
        pltpu.VMEM((RINGZ, PPM, EMB), F32),
        pltpu.VMEM((PPM, EMB), F32),
        pltpu.VMEM((ROWS, 128), F32),
        pltpu.VMEM((SHARDS, 8, HALF), F32),
        pltpu.VMEM((SHARDS, 8, HALF), F32),
        dma((12,)),
        dma((1,)),
        dma((3,)),
        dma((3,)),
        dma((1,)),
        dma((1,)),
        dma((1,)),
        dma((1,)),
        dma((2, 2, 7)),
        dma((2, 2, 22)),
        dma((2, 2, 7)),
        dma((2, 2, 25)),
        dma((4, 4)),
        dma((4, 12)),
        dma((1,)),
        dma((1,)),
        dma((1,)),
        dma((1,)),
        dma((1,)),
        dma((1,)),
        dma((1,)),
        dma((1,)),
        pltpu.SemaphoreType.REGULAR,
    ]
    return pl.pallas_call(
        kernel,
        out_shape=jax.ShapeDtypeStruct((4, EMB), BF16),
        in_specs=[anywhere] * 16,
        out_specs=vmem,
        scratch_shapes=scratch,
        compiler_params=pltpu.CompilerParams(
            collective_id=0, has_side_effects=True, vmem_limit_bytes=58 * 1024 * 1024
        ),
    )(
        embeds,
        segments,
        rel_table.T,
        attn_gain,
        w_query,
        w_key,
        w_value,
        w_out,
        ffn_gain,
        w_gate,
        w_up,
        w_down,
        final_gain.reshape(1, -1),
        w_proj,
        dest_shard,
        dest_slot,
    )


def solution(mesh):
    in_specs = (
        P("shard", "tensor", None),
        P("shard", None),
        P(None, "tensor"),
        P("section", None),
        P("section", None, "tensor"),
        P("section", None, "tensor"),
        P("section", None, "tensor"),
        P("section", "tensor", None),
        P("section", None),
        P("section", "shard", "tensor"),
        P("section", "shard", "tensor"),
        P("section", "tensor", "shard"),
        P(),
        P("tensor", None),
        P("shard", None),
        P("shard", None),
    )
    out_specs = P(("section", "shard"), None)
    return jax.shard_map(
        on_device, mesh=mesh, in_specs=in_specs, out_specs=out_specs, check_vma=False
    )
```

```python
import jax
import jax.numpy as jnp
from jax import lax
from jax.experimental import pallas as pl
from jax.experimental.pallas import tpu as pltpu
from jax.sharding import PartitionSpec as P

MESH = pl.DeviceIdType.MESH
F32 = jnp.float32
BF16 = jnp.bfloat16
HIGHEST = lax.Precision.HIGHEST

ROWS = 32
CHUNK = 16
RINGZ = 8
SIDE = 4
SHARDS = SIDE * SIDE
WIDTH = 4096
GROUPS = 8
COLS = WIDTH // GROUPS
PAIRS = GROUPS // 2
SEQ = 256
NEAR = 5
HEADS = 4
PPM = 8
DK = 256
HID = 640
EMB = 768
HALF = EMB // 2
EPS = 1e-06

ORDER = (0, 1, 7, 2, 6, 3, 5, 4)
PLACE = tuple(ORDER.index(slot) for slot in range(RINGZ))
lowest = (0, 1, 2, 3, 4, 5, 6, 7, 8, 12, 16, 23, 32, 46, 64, 91)


def copy_to(src, dst, send, recv, device):
    return pltpu.make_async_remote_copy(
        src_ref=src,
        dst_ref=dst,
        send_sem=send,
        recv_sem=recv,
        device_id=device,
        device_id_type=MESH,
    )


def part_rows(half):
    return pl.ds(half * CHUNK, CHUNK)


def group_cols(g):
    return pl.ds(pl.multiple_of(g * COLS, COLS), COLS)


class Spread:
    def __init__(self, z, rows, send, recv):
        self.beside = (lax.rem(z + 1, RINGZ), lax.rem(z + RINGZ - 1, RINGZ))
        self.rows, self.send, self.recv = rows, send, recv

    def move(self, way, hop, far, q, src=None, section=None):
        source, target = (RINGZ - hop + 1, RINGZ - hop) if way == 0 else (hop - 1, hop)
        rows = part_rows(way if far else 1 - way)
        groups = pl.ds(0, GROUPS) if q is None else pl.ds(2 * q, 2)
        if src is None:
            src = self.rows.at[groups, PLACE[source % RINGZ], rows]
        else:
            src = src.at[groups, rows]
        device = {"tensor": self.beside[way]}
        if section is not None:
            device["section"] = section
        if hop < 3 or (hop == 3 and far):
            at = (hop - 1) * 8 + (0 if far else 4) + (0 if q is None else q)
        else:
            at = 20 if hop == 3 else 21
        return copy_to(
            src,
            self.rows.at[groups, PLACE[target % RINGZ], rows],
            self.send.at[way, 2 * hop - (2 if far else 1)],
            self.recv.at[way, at],
            device,
        )

    def step(self, hop, far, q):
        for way in (0, 1):
            if hop > 1:
                self.move(way, hop - 1, far, q).wait_recv()
            self.move(way, hop, far, q).start()

    def land(self):
        for way in (0, 1):
            self.move(way, 3, False, None).wait_recv()
        for way in (0, 1):
            self.move(way, 4, True, None).wait_recv()

    def sent(self, src=None):
        for way in (0, 1):
            for hop in (1, 2, 3, 4):
                for far in (True, False)[: 2 if hop < 4 else 1]:
                    self.move(way, hop, far, None, src if hop == 1 else None).wait_send()


class Chains:
    def __init__(self, z, parts, landed, send, recv):
        self.beside = (lax.rem(z + 1, RINGZ), lax.rem(z + RINGZ - 1, RINGZ))
        self.parts, self.landed, self.send, self.recv = parts, landed, send, recv

    def place(self, way, hop):
        return PLACE[5 - hop if way == 0 else RINGZ - 5 + hop]

    def move(self, way, hop, far, q):
        rows = part_rows(way if far else 1 - way)
        groups = pl.ds(0, GROUPS) if q is None else pl.ds(2 * q, 2)
        kind = 2 * hop - (2 if far else 1)
        kind = kind - 1 if hop > 1 else kind
        at = kind * 4 + (0 if q is None or kind == 6 else q)
        return copy_to(
            self.parts.at[groups, self.place(way, hop), rows],
            self.landed.at[way, hop - 1, groups, rows],
            self.send.at[way, kind],
            self.recv.at[way, at],
            {"tensor": self.beside[way]},
        )

    def forward(self, hop, far, q):
        for way in (0, 1):
            if hop > (1 if far else 2):
                self.move(way, hop - 1, far, q).wait_recv()
                place = self.place(way, hop)
                rows = part_rows(way if far else 1 - way)
                groups = pl.ds(2 * q, 2)
                total = self.parts[groups, place, rows].astype(F32) + self.landed[
                    way, hop - 2, groups, rows
                ].astype(F32)
                self.parts[groups, place, rows] = total.astype(BF16)
            self.move(way, hop, far, q).start()

    def total(self, g):
        own = self.parts[g, 0].astype(F32)
        return own + self.landed[0, 3, g].astype(F32) + self.landed[1, 3, g].astype(F32)

    def sent(self):
        for way in (0, 1):
            for hop in (1, 2, 3, 4):
                for far in (True, False)[: 2 if hop > 1 else 1]:
                    self.move(way, hop, far, None).wait_send()


class Weights:
    def __init__(self, y, x, gate, up, down, send, recv):
        self.y, self.x = y, x
        self.arrays = ((gate, 0, DK), (up, 0, DK), (down, 0, HID // 2), (down, HID // 2, HID // 2))
        self.send, self.recv = send, recv

    def piece(self, array, first, second, sign):
        ref, start, size = self.arrays[array]
        if sign is not None:
            size = size // 2
            start = start + sign * size
        along_x, along_y = (first, second) if array % 2 == 0 else (second, first)
        at_x, at_y = lax.rem(self.x + along_x, SIDE), lax.rem(self.y + along_y, SIDE)
        return ref.at[at_y, at_x, pl.ds(start, size)]

    def all_of(self, array, stage, hop):
        ref, start, size = self.arrays[array]
        rows = pl.ds(start, size if hop == 0 else size // 2)
        ref = ref.at[0, pl.ds(0, 2), rows] if stage == 0 else ref.at[pl.ds(0, 2), :, rows]
        return copy_to(
            ref,
            ref,
            self.send.at[array, stage * 2 + hop],
            self.recv.at[array, 2 if stage == 0 else 11],
            {"shard": self.y * SIDE + self.x},
        )

    def copy(self, array, stage, hop, line, sign, landing):
        step = 1 if sign == 0 else SIDE - 1
        back = SIDE - step
        away = (back if hop == 1 else 0) + (back if landing else 0)
        if stage == 0:
            ref = self.piece(array, away % SIDE, 0, None if hop == 0 else sign)
            at = sign if hop == 0 else 2
        else:
            ref = self.piece(array, line, away % SIDE, None if hop == 0 else sign)
            at = 3 + line * 2 + sign if hop == 0 else 11
        on_x = (array % 2 == 0) == (stage == 0)
        if on_x:
            shard = self.y * SIDE + lax.rem(self.x + step, SIDE)
        else:
            shard = lax.rem(self.y + step, SIDE) * SIDE + self.x
        return copy_to(
            ref,
            ref,
            self.send.at[array, stage * 2 + hop],
            self.recv.at[array, at],
            {"shard": shard},
        )

    def go(self, array, stage, hop, line, sign):
        self.copy(array, stage, hop, line, sign, False).start()

    def wait(self, array, stage, hop, line, sign):
        self.copy(array, stage, hop, line, sign, True).wait_recv()

    def second(self, array, line):
        for sign in (0, 1):
            self.go(array, 1, 0, line, sign)
        if array >= 2:
            ref = self.piece(array, line, 0, None)
            if array % 2 == 0:
                shard = lax.rem(self.y + 2, SIDE) * SIDE + self.x
            else:
                shard = self.y * SIDE + lax.rem(self.x + 2, SIDE)
            copy_to(
                ref, ref, self.send.at[array, 3], self.recv.at[array, 11], {"shard": shard}
            ).start()

    def run(self, ready):
        both = (0, 1)
        for array in range(4):
            ready(array)
            for sign in both:
                self.go(array, 0, 0, 0, sign)
            self.second(array, 0)
        for array in range(4):
            for sign in both:
                self.wait(array, 0, 0, 0, sign)
                self.go(array, 0, 1, 0, sign)
                self.second(array, SIDE - 1 if sign == 0 else 1)
        for array in range(4):
            self.all_of(array, 0, 1).wait_recv()
            self.second(array, 2)
        for array in (0, 1):
            for line in (0, 1, 3, 2):
                for sign in both:
                    self.wait(array, 1, 0, line, sign)
                    self.go(array, 1, 1, line, sign)

    def land(self, arrays):
        for array in arrays:
            if array >= 2:
                for line in range(SIDE):
                    for sign in (0, 1):
                        self.wait(array, 1, 0, line, sign)
            self.all_of(array, 1, 1).wait_recv()

    def sent(self):
        for array in range(4):
            for stage in (0, 1):
                for hop in (0, 1):
                    self.all_of(array, stage, hop).wait_send()


def kernel(
    embeds,
    segments,
    rel_table,
    attn_gain,
    w_query,
    w_key,
    w_value,
    w_out,
    ffn_gain,
    w_gate,
    w_up,
    w_down,
    final_gain,
    w_proj,
    dest_shard,
    dest_slot,
    index,
    segments_v,
    rel_v,
    attn_gain_v,
    ffn_gain_v,
    final_gain_v,
    dest_shard_v,
    dest_slot_v,
    query_w,
    key_w,
    value_w,
    out_w,
    proj_w,
    gate_w,
    up_w,
    down_w,
    bias,
    member_here,
    attn_rows,
    attn_parts,
    attn_landed,
    ffn_rows,
    ffn_parts,
    ffn_landed,
    handed,
    last,
    lane_sums,
    queries,
    keys,
    values,
    context,
    sums,
    hidden,
    pooled,
    pooled_in,
    shares,
    units,
    row_squares,
    placed,
    placed_in,
    load_sem,
    rows_sem,
    swap_send,
    swap_recv,
    near_send,
    near_recv,
    ag_send,
    ag_recv,
    rs_send,
    rs_recv,
    w_send,
    w_recv,
    pool_send,
    pool_recv,
    share_send,
    share_recv,
    unit_send,
    unit_recv,
    place_send,
    place_recv,
    free_sem,
):
    section = lax.axis_index("section")
    z = lax.axis_index("tensor")
    shard = lax.axis_index("shard")
    y, x = shard // SIDE, lax.rem(shard, SIDE)
    other = 1 - section

    barrier = pltpu.get_barrier_semaphore()

    def greet(device):
        pl.semaphore_signal(barrier, inc=1, device_id=device, device_id_type=MESH)

    @pl.loop(1, RINGZ)
    def _(k):
        greet({"tensor": lax.rem(z + k, RINGZ)})

    for k in (0, 1, RINGZ - 1):
        greet({"section": other, "tensor": lax.rem(z + k, RINGZ)})

    @pl.loop(1, SHARDS)
    def _(k):
        greet({"shard": lax.rem(shard + k, SHARDS)})

    sources = (
        (segments, segments_v),
        (rel_table, rel_v),
        (attn_gain, attn_gain_v),
        (w_query.at[0], query_w),
        (w_key.at[0], key_w),
        (w_value.at[0], value_w),
        (w_out.at[0], out_w),
        (final_gain, final_gain_v),
        (dest_shard, dest_shard_v),
        (dest_slot, dest_slot_v),
        (w_proj, proj_w),
    )
    loads = [
        pltpu.make_async_copy(src, dst, load_sem.at[i]) for i, (src, dst) in enumerate(sources)
    ]
    first_rows = [
        pltpu.make_async_copy(
            embeds.at[0, :, pl.ds(g * COLS, COLS)], attn_rows.at[g, 0], rows_sem.at[0]
        )
        for g in range(GROUPS)
    ]
    for load in loads[:3]:
        load.start()

    @pl.when(section == 0)
    def _():
        for load in first_rows:
            load.start()

    for load in loads[3:]:
        load.start()
    for load in loads[:2]:
        load.wait()

    def squares(value):
        return jnp.sum(value * value, axis=-1, keepdims=True)

    def row_scale():
        return lax.rsqrt(row_squares[:, 0:1] * (1.0 / WIDTH) + EPS)

    no_squares = jnp.zeros((ROWS, 1), F32)

    passage = lax.broadcasted_iota(jnp.int32, (PPM, SEQ), 0)
    counts = jnp.sum((segments_v[...] == passage).astype(F32), axis=-1, keepdims=True)
    first = jnp.sum((segments_v[...] < passage).astype(F32), axis=-1, keepdims=True)

    def members(token):
        at = token.astype(F32)
        return ((at >= first) & (at < first + counts)).astype(F32)

    lane = lax.broadcasted_iota(jnp.int32, (PPM, ROWS), 1)
    member_here[...] = members(lane + z * ROWS)

    def slots(place):
        slot = jnp.full_like(place, ORDER[0])
        for at in range(1, RINGZ):
            slot = jnp.where(place == at, ORDER[at], slot)
        return slot

    def tokens(position):
        return (((slots(position >> 5) + z) & 7) << 5) + (position & 31)

    lane = lax.broadcasted_iota(jnp.int32, (PPM, SEQ), 1)
    member = members(tokens(lane)).astype(BF16)
    bias[0] = lax.dot_general(
        member, member, (((0,), (0,)), ((), ())), preferred_element_type=F32
    )

    @pl.loop(0, RINGZ)
    def _(block):
        rows = pl.ds(pl.multiple_of(block * ROWS, ROWS), ROWS)
        inside = bias[0, rows, :] > 0.5
        i = tokens(lax.broadcasted_iota(jnp.int32, (ROWS, SEQ), 0) + block * ROWS)
        k = tokens(lax.broadcasted_iota(jnp.int32, (ROWS, SEQ), 1))
        ahead = k - i
        distance = jnp.abs(ahead)
        for head in range(HEADS):
            before = jnp.broadcast_to(rel_v[head : head + 1, 0:1], (ROWS, SEQ))
            after = jnp.broadcast_to(rel_v[head : head + 1, 16:17], (ROWS, SEQ))
            for code in range(1, 16):
                reached = distance >= lowest[code]
                before = jnp.where(reached, rel_v[head : head + 1, code : code + 1], before)
                after = jnp.where(
                    reached, rel_v[head : head + 1, 16 + code : 17 + code], after
                )
            value = jnp.where(ahead > 0, after, before)
            bias[head, rows, :] = jnp.where(inside, value, -1e30)

    loads[2].wait()
    pl.semaphore_wait(barrier, RINGZ - 1 + 3 + SHARDS - 1)

    attn_spread = Spread(z, attn_rows, ag_send.at[0], ag_recv.at[0])
    ffn_spread = Spread(z, ffn_rows, ag_send.at[1], ag_recv.at[1])

    @pl.when(section == 0)
    def _():
        own_rows = attn_rows.at[:, 0]
        pltpu.make_async_copy(own_rows, own_rows, rows_sem.at[0]).wait()
        for far in (True, False):

            @pl.loop(0, PAIRS)
            def _(q):
                attn_spread.step(1, far, q)

    swaps = [
        copy_to(src, dst, swap_send.at[i], swap_recv.at[i], {"section": other})
        for i, (src, dst) in enumerate(
            (
                (w_gate.at[0], gate_w.at[y, x]),
                (w_up.at[0], up_w.at[y, x]),
                (w_down.at[0], down_w.at[y, x]),
            )
        )
    ]
    swaps.append(
        copy_to(ffn_gain, ffn_gain_v, swap_send.at[3], swap_recv.at[3], {"section": other})
    )
    for swap in swaps:
        swap.start()

    attn_chains = Chains(z, attn_parts, attn_landed, rs_send.at[0], rs_recv.at[0])
    ffn_chains = Chains(z, ffn_parts, ffn_landed, rs_send.at[1], rs_recv.at[1])
    weights = Weights(y, x, gate_w, up_w, down_w, w_send, w_recv)

    near = copy_to(
        handed, ffn_rows.at[:, 0], near_send.at[0], near_recv.at[0], {"section": other}
    )

    def run_spread(spread, ready, multiply):
        for hop in (2, 3):
            for far in (True, False):

                @pl.loop(0, PAIRS)
                def _(q):
                    spread.step(hop, far, q)

        ready()

        @pl.loop(0, 1)
        def _(q):
            multiply(q, 0)

        @pl.loop(0, PAIRS)
        def _(q):
            spread.step(4, True, q)

        @pl.loop(1, PAIRS)
        def _(q):
            multiply(q, 0)

    def prepare(rows_ref, gain, pair, place):
        blocks, rows, count = part(place)
        total = jnp.where(pair == 0, 0.0, lane_sums[rows, :])
        prepared = []
        for g in (2 * pair, 2 * pair + 1):
            value = rows_ref[g, blocks].reshape(count, COLS).astype(F32)
            for c in range(0, COLS, 128):
                piece = value[:, c : c + 128]
                total = total + piece * piece
            prepared.append((value * gain[:, group_cols(g)]).astype(BF16))
        lane_sums[rows, :] = total
        return prepared

    def scale_of(sums_of_lanes):
        total = jnp.sum(sums_of_lanes, axis=-1, keepdims=True)
        return lax.rsqrt(total * (1.0 / WIDTH) + EPS)

    def run_chains(chains, far, between, close):
        @pl.loop(0, PAIRS)
        def _(q):
            far(2 * q)
            far(2 * q + 1)
            chains.forward(1, True, q)
            chains.forward(2, False, q)

        between()

        @pl.loop(0, PAIRS)
        def _(q):
            close(2 * q)
            close(2 * q + 1)
            chains.forward(2, True, q)

        for hop, is_far in ((3, False), (3, True), (4, False), (4, True)):

            @pl.loop(0, PAIRS)
            def _(q):
                chains.forward(hop, is_far, q)

    def finish(chains, before, pass_on):
        for way in (0, 1):
            chains.move(way, 4, False, None).wait_recv()

        def add(q, total):
            for way in (0, 1):
                chains.move(way, 4, True, q).wait_recv()
            ready = []
            for g in (2 * q, 2 * q + 1):
                value = (before[g, 0].astype(F32) + chains.total(g)).astype(BF16)
                total = total + squares(value.astype(F32))
                ready.append((g, value))
            pass_on(q, ready)
            return total

        total = lax.fori_loop(0, PAIRS, add, no_squares)
        row_squares[...] = jnp.broadcast_to(total, row_squares.shape)

    def part(place):
        blocks = (0, NEAR) if place == 0 else (NEAR, RINGZ - NEAR)
        return pl.ds(*blocks), pl.ds(blocks[0] * ROWS, blocks[1] * ROWS), blocks[1] * ROWS

    def attention():
        def ready():
            for load in loads[3:6]:
                load.wait()

        def multiply(pair, place):
            prepared = prepare(attn_rows, attn_gain_v, pair, place)
            _, rows, _ = part(place)
            for n, weight in enumerate((query_w, key_w, value_w)):
                cols = slice(n * 256, (n + 1) * 256)
                product = jnp.where(pair == 0, 0.0, sums[rows, cols])
                for j in range(2):
                    product = product + jnp.dot(
                        prepared[j],
                        weight[group_cols(2 * pair + j), :],
                        preferred_element_type=F32,
                    )
                sums[rows, cols] = product

        run_spread(attn_spread, ready, multiply)
        attn_spread.land()

        @pl.loop(0, PAIRS)
        def _(pair):
            multiply(pair, 1)

        scale = scale_of(lane_sums[...])
        queries[...] = (sums[:, 0:256] * scale).astype(BF16)
        keys[...] = (sums[:, 256:512] * scale).astype(BF16)
        values[...] = (sums[:, 512:768] * scale).astype(BF16)

        def attend(place):
            _, rows, count = part(place)
            head_lane = lax.broadcasted_iota(jnp.int32, (count, 128), 1)

            @pl.loop(0, HEADS // 2)
            def _(pair):
                cols = pl.ds(pl.multiple_of(pair * 128, 128), 128)
                query_pair, key_pair, value_pair = queries[rows, cols], keys[:, cols], values[:, cols]
                results = []
                for sub in range(2):
                    mine = (head_lane >= 64) if sub else (head_lane < 64)
                    one = jnp.where(mine, query_pair.astype(F32), 0.0).astype(BF16)
                    scores = lax.dot_general(
                        one, key_pair, (((1,), (1,)), ((), ())), preferred_element_type=F32
                    )
                    scores = scores + bias[pair * 2 + sub, rows, :]
                    powers = jnp.exp(scores - jnp.max(scores, axis=-1, keepdims=True))
                    shares_of = powers / jnp.sum(powers, axis=-1, keepdims=True)
                    results.append(
                        jnp.dot(shares_of.astype(BF16), value_pair, preferred_element_type=F32)
                    )
                context[rows, cols] = jnp.where(head_lane < 64, results[0], results[1]).astype(BF16)

        def project(g, place):
            blocks, rows, count = part(place)
            product = jnp.dot(
                context[rows, :], out_w[:, group_cols(g)], preferred_element_type=F32
            )
            attn_parts[g, blocks] = product.astype(BF16).reshape(
                count // ROWS, ROWS, COLS
            )

        attend(1)
        loads[6].wait()
        run_chains(
            attn_chains, lambda g: project(g, 1), lambda: attend(0), lambda g: project(g, 0)
        )

        def start(far, q):
            for way in (0, 1):
                ffn_spread.move(way, 1, far, q, handed, other).start()

        def pass_on(q, ready):
            for g, value in ready:
                handed[g] = value
            start(True, q)

        finish(attn_chains, attn_rows, pass_on)

        @pl.loop(0, PAIRS)
        def _(q):
            start(False, q)

        near.start()

    def feed():
        def multiply(pair, place):
            prepared = prepare(ffn_rows, ffn_gain_v, pair, place)
            _, rows, _ = part(place)
            for n, weight in enumerate((gate_w, up_w)):
                cols = slice(n * HID, (n + 1) * HID)
                product = jnp.where(pair == 0, 0.0, sums[rows, cols])
                for j in range(2):
                    product = product + jnp.dot(
                        prepared[j],
                        weight[pair, 2 * j : 2 * j + 2].reshape(COLS, HID),
                        preferred_element_type=F32,
                    )
                sums[rows, cols] = product

        def activate(place):
            _, rows, _ = part(place)
            scale = scale_of(lane_sums[rows, :])
            gate = sums[rows, 0:HID] * scale
            up = sums[rows, HID : 2 * HID] * scale
            curve = jnp.tanh(0.7978845608 * (gate + 0.044715 * gate * gate * gate))
            hidden[rows, :] = (0.5 * gate * (1.0 + curve) * up).astype(BF16)

        def ready():
            near.wait_recv()
            swaps[3].wait_recv()
            weights.land((0, 1))

            @pl.when(section == 1)
            def _():
                pl.semaphore_signal(
                    free_sem, inc=1, device_id={"section": other}, device_id_type=MESH
                )

        run_spread(ffn_spread, ready, multiply)
        activate(0)
        ffn_spread.land()

        @pl.loop(0, PAIRS)
        def _(pair):
            multiply(pair, 1)

        activate(1)
        weights.land((2, 3))

        def project(g, place):
            blocks, rows, count = part(place)
            for j in range(2):
                product = jnp.dot(
                    hidden[rows, :],
                    down_w[g // 2, 2 * lax.rem(g, 2) + j],
                    preferred_element_type=F32,
                )
                ffn_parts[g, blocks, :, j * DK : (j + 1) * DK] = product.astype(BF16).reshape(
                    count // ROWS, ROWS, DK
                )

        run_chains(ffn_chains, lambda g: project(g, 1), lambda: None, lambda g: project(g, 0))

        def pass_on(q, ready):
            @pl.when(section == 0)
            def _():
                for g, value in ready:
                    last[g] = value

            @pl.when(section == 1)
            def _():
                for g, value in ready:
                    attn_rows[g, 0] = value
                attn_spread.step(1, True, q)

        finish(ffn_chains, ffn_rows, pass_on)

        @pl.when(section == 1)
        def _():
            @pl.loop(0, PAIRS)
            def _(q):
                attn_spread.step(1, False, q)

    @pl.loop(0, 3)
    def _(turn):
        role = lax.rem(turn + section, 3)

        @pl.when(role == 0)
        def _():
            attention()

        @pl.when(role == 1)
        def _():
            @pl.when(section == 0)
            def _():
                pl.semaphore_wait(free_sem, 1)

            def ready(array):
                if array < 3:
                    swaps[array].wait_recv()

            weights.run(ready)

        @pl.when(role == 2)
        def _():
            feed()

    def leave():
        for swap in swaps:
            swap.wait_send()
        weights.sent()
        near.wait_send()
        attn_spread.sent()
        ffn_spread.sent(handed)
        attn_chains.sent()
        ffn_chains.sent()

    for load in loads[7:]:
        load.wait()

    def pool_copy(k):
        to = lax.rem(z + k, RINGZ)
        return copy_to(
            pooled.at[to], pooled_in.at[z], pool_send.at[0], pool_recv.at[0], {"tensor": to}
        )

    def share_copy(k):
        device = {"tensor": lax.rem(z + k, RINGZ)}
        return copy_to(shares.at[z], shares.at[z], share_send.at[0], share_recv.at[0], device)

    def place_copy(k):
        to = lax.rem(shard + k, SHARDS)
        return copy_to(
            placed.at[to], placed_in.at[shard], place_send.at[0], place_recv.at[0], {"shard": to}
        )

    others = pl.ds(0, RINGZ - 1)
    all_pool = copy_to(
        pooled.at[others], pooled_in.at[others], pool_send.at[0], pool_recv.at[0], {"tensor": z}
    )
    all_share = copy_to(
        shares.at[others], shares.at[others], share_send.at[0], share_recv.at[0], {"tensor": z}
    )
    rest = pl.ds(0, SHARDS - 1)
    all_place = copy_to(
        placed.at[rest], placed_in.at[rest], place_send.at[0], place_recv.at[0], {"shard": shard}
    )
    unit_copy = copy_to(units, units, unit_send.at[0], unit_recv.at[0], {"section": other})

    @pl.when(section == 0)
    def _():
        scale = row_scale()

        def pool(g):
            finished = last[g].astype(F32) * scale * final_gain_v[:, group_cols(g)]
            return jnp.dot(
                member_here[...], finished, precision=HIGHEST, preferred_element_type=F32
            )

        for k in (4, 3, 5, 2, 6, 1, 7):
            to = lax.rem(z + k, RINGZ)
            pooled[to] = pool(to)
            pool_copy(k).start()
        pooled_in[z] = pool(z)
        leave()
        all_pool.wait_recv()
        means = (jnp.sum(pooled_in[...], axis=0) / counts).astype(BF16)
        shares[z] = jnp.dot(means, proj_w[...], preferred_element_type=F32)
        for k in (4, 3, 5, 2, 6, 1, 7):
            share_copy(k).start()
        all_pool.wait_send()
        all_share.wait_recv()
        projected = shares[0]
        for d in range(1, RINGZ):
            projected = projected + shares[d]
        mean_square = jnp.mean(projected * projected, axis=-1, keepdims=True)
        units[...] = (projected * lax.rsqrt(mean_square + EPS)).astype(BF16).astype(F32)
        unit_copy.start()

    @pl.when(section == 1)
    def _():
        leave()
        unit_copy.wait_recv()

    row = lax.broadcasted_iota(jnp.int32, (SHARDS * 8, PPM), 0)
    chosen = (dest_shard_v[...] == (row >> 3) + section * SHARDS) & (dest_slot_v[...] == (row & 3))
    chosen = chosen.astype(F32)
    lower = jnp.dot(chosen, units[:, :HALF], preferred_element_type=F32)
    upper = jnp.dot(chosen, units[:, HALF:], preferred_element_type=F32)
    row = lax.broadcasted_iota(jnp.int32, (SHARDS * 8, HALF), 0)
    placed[...] = jnp.where((row & 7) < 4, lower, upper).reshape(SHARDS, 8, HALF)

    @pl.loop(1, SHARDS)
    def _(k):
        place_copy(k).start()

    placed_in[shard] = placed[shard]

    @pl.when(section == 0)
    def _():
        all_share.wait_send()
        unit_copy.wait_send()

    all_place.wait_send()
    all_place.wait_recv()
    rows = jnp.sum(placed_in[...], axis=0)
    index[:, 0:HALF] = rows[0:4].astype(BF16)
    index[:, HALF:EMB] = rows[4:8].astype(BF16)


def on_device(
    embeds,
    segments,
    rel_table,
    attn_gain,
    w_query,
    w_key,
    w_value,
    w_out,
    ffn_gain,
    w_gate,
    w_up,
    w_down,
    final_gain,
    w_proj,
    dest_shard,
    dest_slot,
):
    vmem = pl.BlockSpec(memory_space=pltpu.VMEM)
    anywhere = pl.BlockSpec(memory_space=pl.ANY)
    dma = pltpu.SemaphoreType.DMA
    rows = pltpu.VMEM((GROUPS, RINGZ, ROWS, COLS), BF16)
    landed = pltpu.VMEM((2, 4, GROUPS, ROWS, COLS), BF16)
    own = pltpu.VMEM((GROUPS, ROWS, COLS), BF16)
    heads = pltpu.VMEM((SEQ, 256), BF16)
    scratch = [
        pltpu.VMEM((1, SEQ), jnp.int32),
        pltpu.VMEM((HEADS, 32), F32),
        pltpu.VMEM((1, WIDTH), F32),
        pltpu.VMEM((1, WIDTH), F32),
        pltpu.VMEM((1, WIDTH), F32),
        pltpu.VMEM((1, PPM), jnp.int32),
        pltpu.VMEM((1, PPM), jnp.int32),
        pltpu.VMEM((WIDTH, 256), BF16),
        pltpu.VMEM((WIDTH, 256), BF16),
        pltpu.VMEM((WIDTH, 256), BF16),
        pltpu.VMEM((256, WIDTH), BF16),
        pltpu.VMEM((COLS, EMB), BF16),
        pltpu.VMEM((SIDE, SIDE, DK, HID), BF16),
        pltpu.VMEM((SIDE, SIDE, DK, HID), BF16),
        pltpu.VMEM((SIDE, SIDE, HID, DK), BF16),
        pltpu.VMEM((HEADS, SEQ, SEQ), F32),
        pltpu.VMEM((PPM, ROWS), F32),
        rows,
        rows,
        landed,
        rows,
        rows,
        landed,
        own,
        own,
        pltpu.VMEM((SEQ, 128), F32),
        heads,
        heads,
        heads,
        heads,
        pltpu.VMEM((SEQ, 2 * HID), F32),
        pltpu.VMEM((SEQ, HID), BF16),
        pltpu.VMEM((RINGZ, PPM, COLS), F32),
        pltpu.VMEM((RINGZ, PPM, COLS), F32),
        pltpu.VMEM((RINGZ, PPM, EMB), F32),
        pltpu.VMEM((PPM, EMB), F32),
        pltpu.VMEM((ROWS, 128), F32),
        pltpu.VMEM((SHARDS, 8, HALF), F32),
        pltpu.VMEM((SHARDS, 8, HALF), F32),
        dma((11,)),
        dma((1,)),
        dma((4,)),
        dma((4,)),
        dma((1,)),
        dma((1,)),
        dma((2, 2, 7)),
        dma((2, 2, 22)),
        dma((2, 2, 7)),
        dma((2, 2, 25)),
        dma((4, 4)),
        dma((4, 12)),
        dma((1,)),
        dma((1,)),
        dma((1,)),
        dma((1,)),
        dma((1,)),
        dma((1,)),
        dma((1,)),
        dma((1,)),
        pltpu.SemaphoreType.REGULAR,
    ]
    return pl.pallas_call(
        kernel,
        out_shape=jax.ShapeDtypeStruct((4, EMB), BF16),
        in_specs=[anywhere] * 16,
        out_specs=vmem,
        scratch_shapes=scratch,
        compiler_params=pltpu.CompilerParams(
            collective_id=0, has_side_effects=True, vmem_limit_bytes=58 * 1024 * 1024
        ),
    )(
        embeds,
        segments,
        rel_table.T,
        attn_gain,
        w_query,
        w_key,
        w_value,
        w_out,
        ffn_gain,
        w_gate,
        w_up,
        w_down,
        final_gain.reshape(1, -1),
        w_proj,
        dest_shard,
        dest_slot,
    )


def solution(mesh):
    in_specs = (
        P("shard", "tensor", None),
        P("shard", None),
        P(None, "tensor"),
        P("section", None),
        P("section", None, "tensor"),
        P("section", None, "tensor"),
        P("section", None, "tensor"),
        P("section", "tensor", None),
        P("section", None),
        P("section", "shard", "tensor"),
        P("section", "shard", "tensor"),
        P("section", "tensor", "shard"),
        P(),
        P("tensor", None),
        P("shard", None),
        P("shard", None),
    )
    out_specs = P(("section", "shard"), None)
    return jax.shard_map(
        on_device, mesh=mesh, in_specs=in_specs, out_specs=out_specs, check_vma=False
    )
```

```python
import jax
import jax.numpy as jnp
from jax import lax
from jax.experimental import pallas as pl
from jax.experimental.pallas import tpu as pltpu
from jax.sharding import PartitionSpec as P

MESH = pl.DeviceIdType.MESH
F32 = jnp.float32
BF16 = jnp.bfloat16
HIGHEST = lax.Precision.HIGHEST

ROWS = 32
CHUNK = 16
RINGZ = 8
SIDE = 4
SHARDS = SIDE * SIDE
WIDTH = 4096
GROUPS = 8
COLS = WIDTH // GROUPS
PAIRS = GROUPS // 2
SEQ = 256
NEAR = 5
HEADS = 4
PPM = 8
DK = 256
HID = 640
EMB = 768
HALF = EMB // 2
EPS = 1e-06

ORDER = (0, 1, 7, 2, 6, 3, 5, 4)
PLACE = tuple(ORDER.index(slot) for slot in range(RINGZ))
lowest = (0, 1, 2, 3, 4, 5, 6, 7, 8, 12, 16, 23, 32, 46, 64, 91)


def copy_to(src, dst, send, recv, device):
    return pltpu.make_async_remote_copy(
        src_ref=src,
        dst_ref=dst,
        send_sem=send,
        recv_sem=recv,
        device_id=device,
        device_id_type=MESH,
    )


def part_rows(half):
    return pl.ds(half * CHUNK, CHUNK)


def group_cols(g):
    return pl.ds(pl.multiple_of(g * COLS, COLS), COLS)


class Spread:
    def __init__(self, z, rows, send, recv):
        self.beside = (lax.rem(z + 1, RINGZ), lax.rem(z + RINGZ - 1, RINGZ))
        self.rows, self.send, self.recv = rows, send, recv

    def move(self, way, hop, far, q, src=None, section=None):
        source, target = (RINGZ - hop + 1, RINGZ - hop) if way == 0 else (hop - 1, hop)
        rows = part_rows(way if far else 1 - way)
        groups = pl.ds(0, GROUPS) if q is None else pl.ds(2 * q, 2)
        if src is None:
            src = self.rows.at[groups, PLACE[source % RINGZ], rows]
        else:
            src = src.at[groups, rows]
        device = {"tensor": self.beside[way]}
        if section is not None:
            device["section"] = section
        if hop < 3 or (hop == 3 and far):
            at = (hop - 1) * 8 + (0 if far else 4) + (0 if q is None else q)
        else:
            at = 20 if hop == 3 else 21
        return copy_to(
            src,
            self.rows.at[groups, PLACE[target % RINGZ], rows],
            self.send.at[way, 2 * hop - (2 if far else 1)],
            self.recv.at[way, at],
            device,
        )

    def step(self, hop, far, q):
        for way in (0, 1):
            if hop > 1:
                self.move(way, hop - 1, far, q).wait_recv()
            self.move(way, hop, far, q).start()

    def land(self):
        for way in (0, 1):
            self.move(way, 3, False, None).wait_recv()
        for way in (0, 1):
            self.move(way, 4, True, None).wait_recv()

    def sent(self, src=None):
        for way in (0, 1):
            for hop in (1, 2, 3, 4):
                for far in (True, False)[: 2 if hop < 4 else 1]:
                    self.move(way, hop, far, None, src if hop == 1 else None).wait_send()


class Chains:
    def __init__(self, z, parts, landed, send, recv):
        self.beside = (lax.rem(z + 1, RINGZ), lax.rem(z + RINGZ - 1, RINGZ))
        self.parts, self.landed, self.send, self.recv = parts, landed, send, recv

    def place(self, way, hop):
        return PLACE[5 - hop if way == 0 else RINGZ - 5 + hop]

    def move(self, way, hop, far, q):
        rows = part_rows(way if far else 1 - way)
        groups = pl.ds(0, GROUPS) if q is None else pl.ds(2 * q, 2)
        kind = 2 * hop - (2 if far else 1)
        kind = kind - 1 if hop > 1 else kind
        at = kind * 4 + (0 if q is None or kind == 6 else q)
        return copy_to(
            self.parts.at[groups, self.place(way, hop), rows],
            self.landed.at[way, hop - 1, groups, rows],
            self.send.at[way, kind],
            self.recv.at[way, at],
            {"tensor": self.beside[way]},
        )

    def forward(self, hop, far, q):
        for way in (0, 1):
            if hop > (1 if far else 2):
                self.move(way, hop - 1, far, q).wait_recv()
                place = self.place(way, hop)
                rows = part_rows(way if far else 1 - way)
                groups = pl.ds(2 * q, 2)
                total = self.parts[groups, place, rows].astype(F32) + self.landed[
                    way, hop - 2, groups, rows
                ].astype(F32)
                self.parts[groups, place, rows] = total.astype(BF16)
            self.move(way, hop, far, q).start()

    def total(self, g):
        own = self.parts[g, 0].astype(F32)
        return own + self.landed[0, 3, g].astype(F32) + self.landed[1, 3, g].astype(F32)

    def sent(self):
        for way in (0, 1):
            for hop in (1, 2, 3, 4):
                for far in (True, False)[: 2 if hop > 1 else 1]:
                    self.move(way, hop, far, None).wait_send()


class Weights:
    def __init__(self, y, x, gate, up, down, send, recv):
        self.y, self.x = y, x
        self.arrays = ((gate, 0, DK), (up, 0, DK), (down, 0, HID // 2), (down, HID // 2, HID // 2))
        self.send, self.recv = send, recv

    def piece(self, array, first, second, sign):
        ref, start, size = self.arrays[array]
        if sign is not None:
            size = size // 2
            start = start + sign * size
        along_x, along_y = (first, second) if array % 2 == 0 else (second, first)
        at_x, at_y = lax.rem(self.x + along_x, SIDE), lax.rem(self.y + along_y, SIDE)
        return ref.at[at_y, at_x, pl.ds(start, size)]

    def all_of(self, array, stage, hop):
        ref, start, size = self.arrays[array]
        rows = pl.ds(start, size if hop == 0 else size // 2)
        ref = ref.at[0, pl.ds(0, 2), rows] if stage == 0 else ref.at[pl.ds(0, 2), :, rows]
        return copy_to(
            ref,
            ref,
            self.send.at[array, stage * 2 + hop],
            self.recv.at[array, 2 if stage == 0 else 11],
            {"shard": self.y * SIDE + self.x},
        )

    def copy(self, array, stage, hop, line, sign, landing):
        step = 1 if sign == 0 else SIDE - 1
        back = SIDE - step
        away = (back if hop == 1 else 0) + (back if landing else 0)
        if stage == 0:
            ref = self.piece(array, away % SIDE, 0, None if hop == 0 else sign)
            at = sign if hop == 0 else 2
        else:
            ref = self.piece(array, line, away % SIDE, None if hop == 0 else sign)
            at = 3 + line * 2 + sign if hop == 0 else 11
        on_x = (array % 2 == 0) == (stage == 0)
        if on_x:
            shard = self.y * SIDE + lax.rem(self.x + step, SIDE)
        else:
            shard = lax.rem(self.y + step, SIDE) * SIDE + self.x
        return copy_to(
            ref,
            ref,
            self.send.at[array, stage * 2 + hop],
            self.recv.at[array, at],
            {"shard": shard},
        )

    def go(self, array, stage, hop, line, sign):
        self.copy(array, stage, hop, line, sign, False).start()

    def wait(self, array, stage, hop, line, sign):
        self.copy(array, stage, hop, line, sign, True).wait_recv()

    def direct(self, array, stage, line):
        ref = self.piece(array, line, 0, None)
        if (array % 2 == 0) == (stage == 0):
            shard = self.y * SIDE + lax.rem(self.x + 2, SIDE)
        else:
            shard = lax.rem(self.y + 2, SIDE) * SIDE + self.x
        return copy_to(
            ref,
            ref,
            self.send.at[array, stage * 2 + 1],
            self.recv.at[array, 2 if stage == 0 else 11],
            {"shard": shard},
        )

    def second(self, array, line):
        for sign in (0, 1):
            self.go(array, 1, 0, line, sign)
        if array >= 2:
            self.direct(array, 1, line).start()

    def run(self, ready):
        def begin(arrays):
            for array in arrays:
                ready(array)
                for sign in (0, 1):
                    self.go(array, 0, 0, 0, sign)
                if array >= 2:
                    self.direct(array, 0, 0).start()
                self.second(array, 0)

        def along(line):
            for array in (0, 1):
                for sign in (0, 1):
                    self.wait(array, 1, 0, line, sign)
                    self.go(array, 1, 1, line, sign)

        begin((0, 1))
        for array in (0, 1):
            for sign in (0, 1):
                self.wait(array, 0, 0, 0, sign)
                self.go(array, 0, 1, 0, sign)
                self.second(array, SIDE - 1 if sign == 0 else 1)
        for array in (0, 1):
            self.all_of(array, 0, 1).wait_recv()
            self.second(array, 2)
        along(0)
        begin((2, 3))
        for line in (1, 3, 2):
            along(line)
        for array in (2, 3):
            for sign in (0, 1):
                self.wait(array, 0, 0, 0, sign)
                self.second(array, SIDE - 1 if sign == 0 else 1)
            self.all_of(array, 0, 1).wait_recv()
            self.second(array, 2)

    def land(self, arrays):
        for array in arrays:
            if array >= 2:
                for line in range(SIDE):
                    for sign in (0, 1):
                        self.wait(array, 1, 0, line, sign)
            self.all_of(array, 1, 1).wait_recv()

    def sent(self):
        for array in range(4):
            for stage in (0, 1):
                for hop in (0, 1):
                    self.all_of(array, stage, hop).wait_send()


def kernel(
    embeds,
    segments,
    rel_table,
    attn_gain,
    w_query,
    w_key,
    w_value,
    w_out,
    ffn_gain,
    w_gate,
    w_up,
    w_down,
    final_gain,
    w_proj,
    dest_shard,
    dest_slot,
    index,
    segments_v,
    rel_v,
    attn_gain_v,
    ffn_gain_v,
    final_gain_v,
    dest_shard_v,
    dest_slot_v,
    query_w,
    key_w,
    value_w,
    out_w,
    proj_w,
    gate_w,
    up_w,
    down_w,
    bias,
    member_here,
    attn_rows,
    attn_parts,
    attn_landed,
    ffn_rows,
    ffn_parts,
    ffn_landed,
    handed,
    last,
    lane_sums,
    queries,
    keys,
    values,
    context,
    sums,
    hidden,
    pooled,
    pooled_in,
    shares,
    units,
    row_squares,
    placed,
    placed_in,
    load_sem,
    rows_sem,
    swap_send,
    swap_recv,
    near_send,
    near_recv,
    ag_send,
    ag_recv,
    rs_send,
    rs_recv,
    w_send,
    w_recv,
    pool_send,
    pool_recv,
    share_send,
    share_recv,
    unit_send,
    unit_recv,
    place_send,
    place_recv,
    free_sem,
):
    section = lax.axis_index("section")
    z = lax.axis_index("tensor")
    shard = lax.axis_index("shard")
    y, x = shard // SIDE, lax.rem(shard, SIDE)
    other = 1 - section

    barrier = pltpu.get_barrier_semaphore()

    def greet(device):
        pl.semaphore_signal(barrier, inc=1, device_id=device, device_id_type=MESH)

    @pl.loop(1, RINGZ)
    def _(k):
        greet({"tensor": lax.rem(z + k, RINGZ)})

    for k in (0, 1, RINGZ - 1):
        greet({"section": other, "tensor": lax.rem(z + k, RINGZ)})

    @pl.loop(1, SHARDS)
    def _(k):
        greet({"shard": lax.rem(shard + k, SHARDS)})

    sources = (
        (segments, segments_v),
        (rel_table, rel_v),
        (attn_gain, attn_gain_v),
        (w_query.at[0], query_w),
        (w_key.at[0], key_w),
        (w_value.at[0], value_w),
        (w_out.at[0], out_w),
        (final_gain, final_gain_v),
        (dest_shard, dest_shard_v),
        (dest_slot, dest_slot_v),
        (w_proj, proj_w),
    )
    loads = [
        pltpu.make_async_copy(src, dst, load_sem.at[i]) for i, (src, dst) in enumerate(sources)
    ]
    first_rows = [
        pltpu.make_async_copy(
            embeds.at[0, :, pl.ds(g * COLS, COLS)], attn_rows.at[g, 0], rows_sem.at[0]
        )
        for g in range(GROUPS)
    ]
    for load in loads[:3]:
        load.start()

    @pl.when(section == 0)
    def _():
        for load in first_rows:
            load.start()

    for load in loads[3:]:
        load.start()
    for load in loads[:2]:
        load.wait()

    def squares(value):
        return jnp.sum(value * value, axis=-1, keepdims=True)

    def row_scale():
        return lax.rsqrt(row_squares[:, 0:1] * (1.0 / WIDTH) + EPS)

    no_squares = jnp.zeros((ROWS, 1), F32)

    passage = lax.broadcasted_iota(jnp.int32, (PPM, SEQ), 0)
    counts = jnp.sum((segments_v[...] == passage).astype(F32), axis=-1, keepdims=True)
    first = jnp.sum((segments_v[...] < passage).astype(F32), axis=-1, keepdims=True)

    def members(token):
        at = token.astype(F32)
        return ((at >= first) & (at < first + counts)).astype(F32)

    lane = lax.broadcasted_iota(jnp.int32, (PPM, ROWS), 1)
    member_here[...] = members(lane + z * ROWS)

    def slots(place):
        slot = jnp.full_like(place, ORDER[0])
        for at in range(1, RINGZ):
            slot = jnp.where(place == at, ORDER[at], slot)
        return slot

    def tokens(position):
        return (((slots(position >> 5) + z) & 7) << 5) + (position & 31)

    lane = lax.broadcasted_iota(jnp.int32, (PPM, SEQ), 1)
    member = members(tokens(lane)).astype(BF16)
    bias[0] = lax.dot_general(
        member, member, (((0,), (0,)), ((), ())), preferred_element_type=F32
    )

    @pl.loop(0, RINGZ)
    def _(block):
        rows = pl.ds(pl.multiple_of(block * ROWS, ROWS), ROWS)
        inside = bias[0, rows, :] > 0.5
        i = tokens(lax.broadcasted_iota(jnp.int32, (ROWS, SEQ), 0) + block * ROWS)
        k = tokens(lax.broadcasted_iota(jnp.int32, (ROWS, SEQ), 1))
        ahead = k - i
        distance = jnp.abs(ahead)
        for head in range(HEADS):
            before = jnp.broadcast_to(rel_v[head : head + 1, 0:1], (ROWS, SEQ))
            after = jnp.broadcast_to(rel_v[head : head + 1, 16:17], (ROWS, SEQ))
            for code in range(1, 16):
                reached = distance >= lowest[code]
                before = jnp.where(reached, rel_v[head : head + 1, code : code + 1], before)
                after = jnp.where(
                    reached, rel_v[head : head + 1, 16 + code : 17 + code], after
                )
            value = jnp.where(ahead > 0, after, before)
            bias[head, rows, :] = jnp.where(inside, value, -1e30)

    loads[2].wait()
    pl.semaphore_wait(barrier, RINGZ - 1 + 3 + SHARDS - 1)

    attn_spread = Spread(z, attn_rows, ag_send.at[0], ag_recv.at[0])
    ffn_spread = Spread(z, ffn_rows, ag_send.at[1], ag_recv.at[1])

    @pl.when(section == 0)
    def _():
        own_rows = attn_rows.at[:, 0]
        pltpu.make_async_copy(own_rows, own_rows, rows_sem.at[0]).wait()
        for far in (True, False):

            @pl.loop(0, PAIRS)
            def _(q):
                attn_spread.step(1, far, q)

    swaps = [
        copy_to(src, dst, swap_send.at[i], swap_recv.at[i], {"section": other})
        for i, (src, dst) in enumerate(
            (
                (w_gate.at[0], gate_w.at[y, x]),
                (w_up.at[0], up_w.at[y, x]),
                (w_down.at[0], down_w.at[y, x]),
            )
        )
    ]
    swaps.append(
        copy_to(ffn_gain, ffn_gain_v, swap_send.at[3], swap_recv.at[3], {"section": other})
    )
    for swap in swaps:
        swap.start()

    attn_chains = Chains(z, attn_parts, attn_landed, rs_send.at[0], rs_recv.at[0])
    ffn_chains = Chains(z, ffn_parts, ffn_landed, rs_send.at[1], rs_recv.at[1])
    weights = Weights(y, x, gate_w, up_w, down_w, w_send, w_recv)

    near = copy_to(
        handed, ffn_rows.at[:, 0], near_send.at[0], near_recv.at[0], {"section": other}
    )

    def run_spread(spread, ready, multiply):
        for hop in (2, 3):
            for far in (True, False):

                @pl.loop(0, PAIRS)
                def _(q):
                    spread.step(hop, far, q)

        ready()

        @pl.loop(0, 1)
        def _(q):
            multiply(q, 0)

        @pl.loop(0, PAIRS)
        def _(q):
            spread.step(4, True, q)

        @pl.loop(1, PAIRS)
        def _(q):
            multiply(q, 0)

    def prepare(rows_ref, gain, pair, place):
        blocks, rows, count = part(place)
        total = jnp.where(pair == 0, 0.0, lane_sums[rows, :])
        prepared = []
        for g in (2 * pair, 2 * pair + 1):
            value = rows_ref[g, blocks].reshape(count, COLS).astype(F32)
            for c in range(0, COLS, 128):
                piece = value[:, c : c + 128]
                total = total + piece * piece
            prepared.append((value * gain[:, group_cols(g)]).astype(BF16))
        lane_sums[rows, :] = total
        return prepared

    def scale_of(sums_of_lanes):
        total = jnp.sum(sums_of_lanes, axis=-1, keepdims=True)
        return lax.rsqrt(total * (1.0 / WIDTH) + EPS)

    def run_chains(chains, far, between, close):
        @pl.loop(0, PAIRS)
        def _(q):
            far(2 * q)
            far(2 * q + 1)
            chains.forward(1, True, q)
            chains.forward(2, False, q)

        between()

        @pl.loop(0, PAIRS)
        def _(q):
            close(2 * q)
            close(2 * q + 1)
            chains.forward(2, True, q)

        for hop, is_far in ((3, False), (3, True), (4, False), (4, True)):

            @pl.loop(0, PAIRS)
            def _(q):
                chains.forward(hop, is_far, q)

    def finish(chains, before, pass_on):
        for way in (0, 1):
            chains.move(way, 4, False, None).wait_recv()

        def add(q, total):
            for way in (0, 1):
                chains.move(way, 4, True, q).wait_recv()
            ready = []
            for g in (2 * q, 2 * q + 1):
                value = (before[g, 0].astype(F32) + chains.total(g)).astype(BF16)
                total = total + squares(value.astype(F32))
                ready.append((g, value))
            pass_on(q, ready)
            return total

        total = lax.fori_loop(0, PAIRS, add, no_squares)
        row_squares[...] = jnp.broadcast_to(total, row_squares.shape)

    def part(place):
        blocks = (0, NEAR) if place == 0 else (NEAR, RINGZ - NEAR)
        return pl.ds(*blocks), pl.ds(blocks[0] * ROWS, blocks[1] * ROWS), blocks[1] * ROWS

    def attention():
        def ready():
            for load in loads[3:6]:
                load.wait()

        def multiply(pair, place):
            prepared = prepare(attn_rows, attn_gain_v, pair, place)
            _, rows, _ = part(place)
            for n, weight in enumerate((query_w, key_w, value_w)):
                cols = slice(n * 256, (n + 1) * 256)
                product = jnp.where(pair == 0, 0.0, sums[rows, cols])
                for j in range(2):
                    product = product + jnp.dot(
                        prepared[j],
                        weight[group_cols(2 * pair + j), :],
                        preferred_element_type=F32,
                    )
                sums[rows, cols] = product

        run_spread(attn_spread, ready, multiply)
        attn_spread.land()

        @pl.loop(0, PAIRS)
        def _(pair):
            multiply(pair, 1)

        scale = scale_of(lane_sums[...])
        queries[...] = (sums[:, 0:256] * scale).astype(BF16)
        keys[...] = (sums[:, 256:512] * scale).astype(BF16)
        values[...] = (sums[:, 512:768] * scale).astype(BF16)

        def attend(place):
            _, rows, count = part(place)
            head_lane = lax.broadcasted_iota(jnp.int32, (count, 128), 1)

            @pl.loop(0, HEADS // 2)
            def _(pair):
                cols = pl.ds(pl.multiple_of(pair * 128, 128), 128)
                query_pair, key_pair, value_pair = queries[rows, cols], keys[:, cols], values[:, cols]
                results = []
                for sub in range(2):
                    mine = (head_lane >= 64) if sub else (head_lane < 64)
                    one = jnp.where(mine, query_pair.astype(F32), 0.0).astype(BF16)
                    scores = lax.dot_general(
                        one, key_pair, (((1,), (1,)), ((), ())), preferred_element_type=F32
                    )
                    scores = scores + bias[pair * 2 + sub, rows, :]
                    powers = jnp.exp(scores - jnp.max(scores, axis=-1, keepdims=True))
                    shares_of = powers / jnp.sum(powers, axis=-1, keepdims=True)
                    results.append(
                        jnp.dot(shares_of.astype(BF16), value_pair, preferred_element_type=F32)
                    )
                context[rows, cols] = jnp.where(head_lane < 64, results[0], results[1]).astype(BF16)

        def project(g, place):
            blocks, rows, count = part(place)
            product = jnp.dot(
                context[rows, :], out_w[:, group_cols(g)], preferred_element_type=F32
            )
            attn_parts[g, blocks] = product.astype(BF16).reshape(
                count // ROWS, ROWS, COLS
            )

        attend(1)
        loads[6].wait()
        run_chains(
            attn_chains, lambda g: project(g, 1), lambda: attend(0), lambda g: project(g, 0)
        )

        def start(far, q):
            for way in (0, 1):
                ffn_spread.move(way, 1, far, q, handed, other).start()

        def pass_on(q, ready):
            for g, value in ready:
                handed[g] = value
            start(True, q)

        finish(attn_chains, attn_rows, pass_on)

        @pl.loop(0, PAIRS)
        def _(q):
            start(False, q)

        near.start()

    def feed():
        def multiply(pair, place):
            prepared = prepare(ffn_rows, ffn_gain_v, pair, place)
            _, rows, _ = part(place)
            for n, weight in enumerate((gate_w, up_w)):
                cols = slice(n * HID, (n + 1) * HID)
                product = jnp.where(pair == 0, 0.0, sums[rows, cols])
                for j in range(2):
                    product = product + jnp.dot(
                        prepared[j],
                        weight[pair, 2 * j : 2 * j + 2].reshape(COLS, HID),
                        preferred_element_type=F32,
                    )
                sums[rows, cols] = product

        def activate(place):
            _, rows, _ = part(place)
            scale = scale_of(lane_sums[rows, :])
            gate = sums[rows, 0:HID] * scale
            up = sums[rows, HID : 2 * HID] * scale
            curve = jnp.tanh(0.7978845608 * (gate + 0.044715 * gate * gate * gate))
            hidden[rows, :] = (0.5 * gate * (1.0 + curve) * up).astype(BF16)

        def ready():
            near.wait_recv()
            swaps[3].wait_recv()
            weights.land((0, 1))

        run_spread(ffn_spread, ready, multiply)
        activate(0)
        ffn_spread.land()

        @pl.loop(0, PAIRS)
        def _(pair):
            multiply(pair, 1)

        activate(1)
        weights.land((2, 3))

        @pl.when(section == 1)
        def _():
            pl.semaphore_signal(free_sem, inc=1, device_id={"section": other}, device_id_type=MESH)

        def project(g, place):
            blocks, rows, count = part(place)
            for j in range(2):
                product = jnp.dot(
                    hidden[rows, :],
                    down_w[g // 2, 2 * lax.rem(g, 2) + j],
                    preferred_element_type=F32,
                )
                ffn_parts[g, blocks, :, j * DK : (j + 1) * DK] = product.astype(BF16).reshape(
                    count // ROWS, ROWS, DK
                )

        run_chains(ffn_chains, lambda g: project(g, 1), lambda: None, lambda g: project(g, 0))

        def pass_on(q, ready):
            @pl.when(section == 0)
            def _():
                for g, value in ready:
                    last[g] = value

            @pl.when(section == 1)
            def _():
                for g, value in ready:
                    attn_rows[g, 0] = value
                attn_spread.step(1, True, q)

        finish(ffn_chains, ffn_rows, pass_on)

        @pl.when(section == 1)
        def _():
            @pl.loop(0, PAIRS)
            def _(q):
                attn_spread.step(1, False, q)

    @pl.loop(0, 3)
    def _(turn):
        role = lax.rem(turn + section, 3)

        @pl.when(role == 0)
        def _():
            attention()

        @pl.when(role == 1)
        def _():
            @pl.when(section == 0)
            def _():
                pl.semaphore_wait(free_sem, 1)

            def ready(array):
                if array < 3:
                    swaps[array].wait_recv()

            weights.run(ready)

        @pl.when(role == 2)
        def _():
            feed()

    def leave():
        for swap in swaps:
            swap.wait_send()
        weights.sent()
        near.wait_send()
        attn_spread.sent()
        ffn_spread.sent(handed)
        attn_chains.sent()
        ffn_chains.sent()

    for load in loads[7:]:
        load.wait()

    def pool_copy(k):
        to = lax.rem(z + k, RINGZ)
        return copy_to(
            pooled.at[to], pooled_in.at[z], pool_send.at[0], pool_recv.at[0], {"tensor": to}
        )

    def share_copy(k):
        device = {"tensor": lax.rem(z + k, RINGZ)}
        return copy_to(shares.at[z], shares.at[z], share_send.at[0], share_recv.at[0], device)

    def place_copy(k):
        to = lax.rem(shard + k, SHARDS)
        return copy_to(
            placed.at[to], placed_in.at[shard], place_send.at[0], place_recv.at[0], {"shard": to}
        )

    others = pl.ds(0, RINGZ - 1)
    all_pool = copy_to(
        pooled.at[others], pooled_in.at[others], pool_send.at[0], pool_recv.at[0], {"tensor": z}
    )
    all_share = copy_to(
        shares.at[others], shares.at[others], share_send.at[0], share_recv.at[0], {"tensor": z}
    )
    rest = pl.ds(0, SHARDS - 1)
    all_place = copy_to(
        placed.at[rest], placed_in.at[rest], place_send.at[0], place_recv.at[0], {"shard": shard}
    )
    unit_copy = copy_to(units, units, unit_send.at[0], unit_recv.at[0], {"section": other})

    @pl.when(section == 0)
    def _():
        scale = row_scale()

        def pool(g):
            finished = last[g].astype(F32) * scale * final_gain_v[:, group_cols(g)]
            return jnp.dot(
                member_here[...], finished, precision=HIGHEST, preferred_element_type=F32
            )

        for k in (4, 3, 5, 2, 6, 1, 7):
            to = lax.rem(z + k, RINGZ)
            pooled[to] = pool(to)
            pool_copy(k).start()
        pooled_in[z] = pool(z)
        leave()
        all_pool.wait_recv()
        means = (jnp.sum(pooled_in[...], axis=0) / counts).astype(BF16)
        shares[z] = jnp.dot(means, proj_w[...], preferred_element_type=F32)
        for k in (4, 3, 5, 2, 6, 1, 7):
            share_copy(k).start()
        all_pool.wait_send()
        all_share.wait_recv()
        projected = shares[0]
        for d in range(1, RINGZ):
            projected = projected + shares[d]
        mean_square = jnp.mean(projected * projected, axis=-1, keepdims=True)
        units[...] = (projected * lax.rsqrt(mean_square + EPS)).astype(BF16).astype(F32)
        unit_copy.start()

    @pl.when(section == 1)
    def _():
        leave()
        unit_copy.wait_recv()

    row = lax.broadcasted_iota(jnp.int32, (SHARDS * 8, PPM), 0)
    chosen = (dest_shard_v[...] == (row >> 3) + section * SHARDS) & (dest_slot_v[...] == (row & 3))
    chosen = chosen.astype(F32)
    lower = jnp.dot(chosen, units[:, :HALF], preferred_element_type=F32)
    upper = jnp.dot(chosen, units[:, HALF:], preferred_element_type=F32)
    row = lax.broadcasted_iota(jnp.int32, (SHARDS * 8, HALF), 0)
    placed[...] = jnp.where((row & 7) < 4, lower, upper).reshape(SHARDS, 8, HALF)

    @pl.loop(1, SHARDS)
    def _(k):
        place_copy(k).start()

    placed_in[shard] = placed[shard]

    @pl.when(section == 0)
    def _():
        all_share.wait_send()
        unit_copy.wait_send()

    all_place.wait_send()
    all_place.wait_recv()
    rows = jnp.sum(placed_in[...], axis=0)
    index[:, 0:HALF] = rows[0:4].astype(BF16)
    index[:, HALF:EMB] = rows[4:8].astype(BF16)


def on_device(
    embeds,
    segments,
    rel_table,
    attn_gain,
    w_query,
    w_key,
    w_value,
    w_out,
    ffn_gain,
    w_gate,
    w_up,
    w_down,
    final_gain,
    w_proj,
    dest_shard,
    dest_slot,
):
    vmem = pl.BlockSpec(memory_space=pltpu.VMEM)
    anywhere = pl.BlockSpec(memory_space=pl.ANY)
    dma = pltpu.SemaphoreType.DMA
    rows = pltpu.VMEM((GROUPS, RINGZ, ROWS, COLS), BF16)
    landed = pltpu.VMEM((2, 4, GROUPS, ROWS, COLS), BF16)
    own = pltpu.VMEM((GROUPS, ROWS, COLS), BF16)
    heads = pltpu.VMEM((SEQ, 256), BF16)
    scratch = [
        pltpu.VMEM((1, SEQ), jnp.int32),
        pltpu.VMEM((HEADS, 32), F32),
        pltpu.VMEM((1, WIDTH), F32),
        pltpu.VMEM((1, WIDTH), F32),
        pltpu.VMEM((1, WIDTH), F32),
        pltpu.VMEM((1, PPM), jnp.int32),
        pltpu.VMEM((1, PPM), jnp.int32),
        pltpu.VMEM((WIDTH, 256), BF16),
        pltpu.VMEM((WIDTH, 256), BF16),
        pltpu.VMEM((WIDTH, 256), BF16),
        pltpu.VMEM((256, WIDTH), BF16),
        pltpu.VMEM((COLS, EMB), BF16),
        pltpu.VMEM((SIDE, SIDE, DK, HID), BF16),
        pltpu.VMEM((SIDE, SIDE, DK, HID), BF16),
        pltpu.VMEM((SIDE, SIDE, HID, DK), BF16),
        pltpu.VMEM((HEADS, SEQ, SEQ), F32),
        pltpu.VMEM((PPM, ROWS), F32),
        rows,
        rows,
        landed,
        rows,
        rows,
        landed,
        own,
        own,
        pltpu.VMEM((SEQ, 128), F32),
        heads,
        heads,
        heads,
        heads,
        pltpu.VMEM((SEQ, 2 * HID), F32),
        pltpu.VMEM((SEQ, HID), BF16),
        pltpu.VMEM((RINGZ, PPM, COLS), F32),
        pltpu.VMEM((RINGZ, PPM, COLS), F32),
        pltpu.VMEM((RINGZ, PPM, EMB), F32),
        pltpu.VMEM((PPM, EMB), F32),
        pltpu.VMEM((ROWS, 128), F32),
        pltpu.VMEM((SHARDS, 8, HALF), F32),
        pltpu.VMEM((SHARDS, 8, HALF), F32),
        dma((11,)),
        dma((1,)),
        dma((4,)),
        dma((4,)),
        dma((1,)),
        dma((1,)),
        dma((2, 2, 7)),
        dma((2, 2, 22)),
        dma((2, 2, 7)),
        dma((2, 2, 25)),
        dma((4, 4)),
        dma((4, 12)),
        dma((1,)),
        dma((1,)),
        dma((1,)),
        dma((1,)),
        dma((1,)),
        dma((1,)),
        dma((1,)),
        dma((1,)),
        pltpu.SemaphoreType.REGULAR,
    ]
    return pl.pallas_call(
        kernel,
        out_shape=jax.ShapeDtypeStruct((4, EMB), BF16),
        in_specs=[anywhere] * 16,
        out_specs=vmem,
        scratch_shapes=scratch,
        compiler_params=pltpu.CompilerParams(
            collective_id=0, has_side_effects=True, vmem_limit_bytes=58 * 1024 * 1024
        ),
    )(
        embeds,
        segments,
        rel_table.T,
        attn_gain,
        w_query,
        w_key,
        w_value,
        w_out,
        ffn_gain,
        w_gate,
        w_up,
        w_down,
        final_gain.reshape(1, -1),
        w_proj,
        dest_shard,
        dest_slot,
    )


def solution(mesh):
    in_specs = (
        P("shard", "tensor", None),
        P("shard", None),
        P(None, "tensor"),
        P("section", None),
        P("section", None, "tensor"),
        P("section", None, "tensor"),
        P("section", None, "tensor"),
        P("section", "tensor", None),
        P("section", None),
        P("section", "shard", "tensor"),
        P("section", "shard", "tensor"),
        P("section", "tensor", "shard"),
        P(),
        P("tensor", None),
        P("shard", None),
        P("shard", None),
    )
    out_specs = P(("section", "shard"), None)
    return jax.shard_map(
        on_device, mesh=mesh, in_specs=in_specs, out_specs=out_specs, check_vma=False
    )
```

```python
import jax
import jax.numpy as jnp
from jax import lax
from jax.experimental import pallas as pl
from jax.experimental.pallas import tpu as pltpu
from jax.sharding import PartitionSpec as P

MESH = pl.DeviceIdType.MESH
F32 = jnp.float32
BF16 = jnp.bfloat16
HIGHEST = lax.Precision.HIGHEST

ROWS = 32
CHUNK = 16
RINGZ = 8
SIDE = 4
SHARDS = SIDE * SIDE
WIDTH = 4096
GROUPS = 8
COLS = WIDTH // GROUPS
PAIRS = GROUPS // 2
SEQ = 256
NEAR = 5
HEADS = 4
PPM = 8
DK = 256
HID = 640
EMB = 768
HALF = EMB // 2
EPS = 1e-06

ORDER = (0, 1, 7, 2, 6, 3, 5, 4)
PLACE = tuple(ORDER.index(slot) for slot in range(RINGZ))
lowest = (0, 1, 2, 3, 4, 5, 6, 7, 8, 12, 16, 23, 32, 46, 64, 91)


def copy_to(src, dst, send, recv, device):
    return pltpu.make_async_remote_copy(
        src_ref=src,
        dst_ref=dst,
        send_sem=send,
        recv_sem=recv,
        device_id=device,
        device_id_type=MESH,
    )


def part_rows(half):
    return pl.ds(half * CHUNK, CHUNK)


def group_cols(g):
    return pl.ds(pl.multiple_of(g * COLS, COLS), COLS)


class Spread:
    def __init__(self, z, rows, send, recv):
        self.beside = (lax.rem(z + 1, RINGZ), lax.rem(z + RINGZ - 1, RINGZ))
        self.rows, self.send, self.recv = rows, send, recv

    def move(self, way, hop, far, q, src=None, section=None):
        source, target = (RINGZ - hop + 1, RINGZ - hop) if way == 0 else (hop - 1, hop)
        rows = part_rows(way if far else 1 - way)
        groups = pl.ds(0, GROUPS) if q is None else pl.ds(2 * q, 2)
        if src is None:
            src = self.rows.at[groups, PLACE[source % RINGZ], rows]
        else:
            src = src.at[groups, rows]
        device = {"tensor": self.beside[way]}
        if section is not None:
            device["section"] = section
        if hop < 3 or (hop == 3 and far):
            at = (hop - 1) * 8 + (0 if far else 4) + (0 if q is None else q)
        else:
            at = 20 if hop == 3 else 21
        return copy_to(
            src,
            self.rows.at[groups, PLACE[target % RINGZ], rows],
            self.send.at[way, 2 * hop - (2 if far else 1)],
            self.recv.at[way, at],
            device,
        )

    def step(self, hop, far, q):
        for way in (0, 1):
            if hop > 1:
                self.move(way, hop - 1, far, q).wait_recv()
            self.move(way, hop, far, q).start()

    def land(self):
        for way in (0, 1):
            self.move(way, 3, False, None).wait_recv()
        for way in (0, 1):
            self.move(way, 4, True, None).wait_recv()

    def sent(self, src=None):
        for way in (0, 1):
            for hop in (1, 2, 3, 4):
                for far in (True, False)[: 2 if hop < 4 else 1]:
                    self.move(way, hop, far, None, src if hop == 1 else None).wait_send()


class Chains:
    def __init__(self, z, parts, landed, send, recv):
        self.beside = (lax.rem(z + 1, RINGZ), lax.rem(z + RINGZ - 1, RINGZ))
        self.parts, self.landed, self.send, self.recv = parts, landed, send, recv

    def place(self, way, hop):
        return PLACE[5 - hop if way == 0 else RINGZ - 5 + hop]

    def move(self, way, hop, far, q):
        rows = part_rows(way if far else 1 - way)
        groups = pl.ds(0, GROUPS) if q is None else pl.ds(2 * q, 2)
        kind = 2 * hop - (2 if far else 1)
        kind = kind - 1 if hop > 1 else kind
        at = kind * 4 + (0 if q is None or kind == 6 else q)
        return copy_to(
            self.parts.at[groups, self.place(way, hop), rows],
            self.landed.at[way, hop - 1, groups, rows],
            self.send.at[way, kind],
            self.recv.at[way, at],
            {"tensor": self.beside[way]},
        )

    def forward(self, hop, far, q):
        for way in (0, 1):
            if hop > (1 if far else 2):
                self.move(way, hop - 1, far, q).wait_recv()
                place = self.place(way, hop)
                rows = part_rows(way if far else 1 - way)
                groups = pl.ds(2 * q, 2)
                total = self.parts[groups, place, rows].astype(F32) + self.landed[
                    way, hop - 2, groups, rows
                ].astype(F32)
                self.parts[groups, place, rows] = total.astype(BF16)
            self.move(way, hop, far, q).start()

    def total(self, g):
        own = self.parts[g, 0].astype(F32)
        return own + self.landed[0, 3, g].astype(F32) + self.landed[1, 3, g].astype(F32)

    def sent(self):
        for way in (0, 1):
            for hop in (1, 2, 3, 4):
                for far in (True, False)[: 2 if hop > 1 else 1]:
                    self.move(way, hop, far, None).wait_send()


class Weights:
    def __init__(self, y, x, gate, up, down, send, recv):
        self.y, self.x = y, x
        self.arrays = ((gate, 0, DK), (up, 0, DK), (down, 0, HID // 2), (down, HID // 2, HID // 2))
        self.send, self.recv = send, recv

    def piece(self, array, first, second, sign):
        ref, start, size = self.arrays[array]
        if sign is not None:
            size = size // 2
            start = start + sign * size
        along_x, along_y = (first, second) if array % 2 == 0 else (second, first)
        at_x, at_y = lax.rem(self.x + along_x, SIDE), lax.rem(self.y + along_y, SIDE)
        return ref.at[at_y, at_x, pl.ds(start, size)]

    def all_of(self, array, stage, hop):
        ref, start, size = self.arrays[array]
        rows = pl.ds(start, size if hop == 0 else size // 2)
        ref = ref.at[0, pl.ds(0, 2), rows] if stage == 0 else ref.at[pl.ds(0, 2), :, rows]
        return copy_to(
            ref,
            ref,
            self.send.at[array, stage * 2 + hop],
            self.recv.at[array, 2 if stage == 0 else 11],
            {"shard": self.y * SIDE + self.x},
        )

    def copy(self, array, stage, hop, line, sign, landing):
        step = 1 if sign == 0 else SIDE - 1
        back = SIDE - step
        away = (back if hop == 1 else 0) + (back if landing else 0)
        if stage == 0:
            ref = self.piece(array, away % SIDE, 0, None if hop == 0 else sign)
            at = sign if hop == 0 else 2
        else:
            ref = self.piece(array, line, away % SIDE, None if hop == 0 else sign)
            at = 3 + line * 2 + sign if hop == 0 and array < 2 else 11
        on_x = (array % 2 == 0) == (stage == 0)
        if on_x:
            shard = self.y * SIDE + lax.rem(self.x + step, SIDE)
        else:
            shard = lax.rem(self.y + step, SIDE) * SIDE + self.x
        return copy_to(
            ref,
            ref,
            self.send.at[array, stage * 2 + hop],
            self.recv.at[array, at],
            {"shard": shard},
        )

    def go(self, array, stage, hop, line, sign):
        self.copy(array, stage, hop, line, sign, False).start()

    def wait(self, array, stage, hop, line, sign):
        self.copy(array, stage, hop, line, sign, True).wait_recv()

    def direct(self, array, stage, line):
        ref = self.piece(array, line, 0, None)
        if (array % 2 == 0) == (stage == 0):
            shard = self.y * SIDE + lax.rem(self.x + 2, SIDE)
        else:
            shard = lax.rem(self.y + 2, SIDE) * SIDE + self.x
        return copy_to(
            ref,
            ref,
            self.send.at[array, stage * 2 + 1],
            self.recv.at[array, 2 if stage == 0 else 11],
            {"shard": shard},
        )

    def second(self, array, line):
        for sign in (0, 1):
            self.go(array, 1, 0, line, sign)
        if array >= 2:
            self.direct(array, 1, line).start()

    def run(self, ready):
        def begin(arrays):
            for array in arrays:
                ready(array)
                for sign in (0, 1):
                    self.go(array, 0, 0, 0, sign)
                if array >= 2:
                    self.direct(array, 0, 0).start()
                self.second(array, 0)

        def along(line):
            for array in (0, 1):
                for sign in (0, 1):
                    self.wait(array, 1, 0, line, sign)
                    self.go(array, 1, 1, line, sign)

        begin((0, 1))
        for array in (0, 1):
            for sign in (0, 1):
                self.wait(array, 0, 0, 0, sign)
                self.go(array, 0, 1, 0, sign)
                self.second(array, SIDE - 1 if sign == 0 else 1)
        for array in (0, 1):
            self.all_of(array, 0, 1).wait_recv()
            self.second(array, 2)
        along(0)
        begin((2, 3))
        for line in (1, 3, 2):
            along(line)
        for array in (2, 3):
            for sign in (0, 1):
                self.wait(array, 0, 0, 0, sign)
                self.second(array, SIDE - 1 if sign == 0 else 1)
            self.all_of(array, 0, 1).wait_recv()
            self.second(array, 2)

    def land(self, arrays):
        for array in arrays:
            if array < 2:
                self.all_of(array, 1, 1).wait_recv()
            else:
                ref, start, size = self.arrays[array]
                ref = ref.at[pl.ds(0, 3), :, pl.ds(start, size)]
                copy_to(
                    ref,
                    ref,
                    self.send.at[array, 2],
                    self.recv.at[array, 11],
                    {"shard": self.y * SIDE + self.x},
                ).wait_recv()

    def sent(self):
        for array in range(4):
            for stage in (0, 1):
                for hop in (0, 1):
                    self.all_of(array, stage, hop).wait_send()


def kernel(
    embeds,
    segments,
    rel_table,
    attn_gain,
    w_query,
    w_key,
    w_value,
    w_out,
    ffn_gain,
    w_gate,
    w_up,
    w_down,
    final_gain,
    w_proj,
    dest_shard,
    dest_slot,
    index,
    segments_v,
    rel_v,
    attn_gain_v,
    ffn_gain_v,
    final_gain_v,
    dest_shard_v,
    dest_slot_v,
    query_w,
    key_w,
    value_w,
    out_w,
    proj_w,
    gate_w,
    up_w,
    down_w,
    bias,
    member_here,
    attn_rows,
    attn_parts,
    attn_landed,
    ffn_rows,
    ffn_parts,
    ffn_landed,
    handed,
    last,
    lane_sums,
    queries,
    keys,
    values,
    context,
    sums,
    hidden,
    pooled,
    pooled_in,
    shares,
    units,
    row_squares,
    placed,
    placed_in,
    load_sem,
    rows_sem,
    swap_send,
    swap_recv,
    near_send,
    near_recv,
    ag_send,
    ag_recv,
    rs_send,
    rs_recv,
    w_send,
    w_recv,
    pool_send,
    pool_recv,
    share_send,
    share_recv,
    unit_send,
    unit_recv,
    place_send,
    place_recv,
    free_sem,
):
    section = lax.axis_index("section")
    z = lax.axis_index("tensor")
    shard = lax.axis_index("shard")
    y, x = shard // SIDE, lax.rem(shard, SIDE)
    other = 1 - section

    barrier = pltpu.get_barrier_semaphore()

    def greet(device):
        pl.semaphore_signal(barrier, inc=1, device_id=device, device_id_type=MESH)

    @pl.loop(1, RINGZ)
    def _(k):
        greet({"tensor": lax.rem(z + k, RINGZ)})

    for k in (0, 1, RINGZ - 1):
        greet({"section": other, "tensor": lax.rem(z + k, RINGZ)})

    @pl.loop(1, SHARDS)
    def _(k):
        greet({"shard": lax.rem(shard + k, SHARDS)})

    sources = (
        (segments, segments_v),
        (rel_table, rel_v),
        (attn_gain, attn_gain_v),
        (w_query.at[0], query_w),
        (w_key.at[0], key_w),
        (w_value.at[0], value_w),
        (w_out.at[0], out_w),
        (final_gain, final_gain_v),
        (dest_shard, dest_shard_v),
        (dest_slot, dest_slot_v),
        (w_proj, proj_w),
    )
    loads = [
        pltpu.make_async_copy(src, dst, load_sem.at[i]) for i, (src, dst) in enumerate(sources)
    ]
    first_rows = [
        pltpu.make_async_copy(
            embeds.at[0, :, pl.ds(g * COLS, COLS)], attn_rows.at[g, 0], rows_sem.at[0]
        )
        for g in range(GROUPS)
    ]
    for load in loads[:3]:
        load.start()

    @pl.when(section == 0)
    def _():
        for load in first_rows:
            load.start()

    for load in loads[3:]:
        load.start()
    for load in loads[:2]:
        load.wait()

    def squares(value):
        return jnp.sum(value * value, axis=-1, keepdims=True)

    def row_scale():
        return lax.rsqrt(row_squares[:, 0:1] * (1.0 / WIDTH) + EPS)

    no_squares = jnp.zeros((ROWS, 1), F32)

    passage = lax.broadcasted_iota(jnp.int32, (PPM, SEQ), 0)
    counts = jnp.sum((segments_v[...] == passage).astype(F32), axis=-1, keepdims=True)
    first = jnp.sum((segments_v[...] < passage).astype(F32), axis=-1, keepdims=True)

    def members(token):
        at = token.astype(F32)
        return ((at >= first) & (at < first + counts)).astype(F32)

    lane = lax.broadcasted_iota(jnp.int32, (PPM, ROWS), 1)
    member_here[...] = members(lane + z * ROWS)

    def slots(place):
        slot = jnp.full_like(place, ORDER[0])
        for at in range(1, RINGZ):
            slot = jnp.where(place == at, ORDER[at], slot)
        return slot

    def tokens(position):
        return (((slots(position >> 5) + z) & 7) << 5) + (position & 31)

    lane = lax.broadcasted_iota(jnp.int32, (PPM, SEQ), 1)
    member = members(tokens(lane)).astype(BF16)
    bias[0] = lax.dot_general(
        member, member, (((0,), (0,)), ((), ())), preferred_element_type=F32
    )

    @pl.loop(0, RINGZ)
    def _(block):
        rows = pl.ds(pl.multiple_of(block * ROWS, ROWS), ROWS)
        inside = bias[0, rows, :] > 0.5
        i = tokens(lax.broadcasted_iota(jnp.int32, (ROWS, SEQ), 0) + block * ROWS)
        k = tokens(lax.broadcasted_iota(jnp.int32, (ROWS, SEQ), 1))
        ahead = k - i
        distance = jnp.abs(ahead)
        for head in range(HEADS):
            before = jnp.broadcast_to(rel_v[head : head + 1, 0:1], (ROWS, SEQ))
            after = jnp.broadcast_to(rel_v[head : head + 1, 16:17], (ROWS, SEQ))
            for code in range(1, 16):
                reached = distance >= lowest[code]
                before = jnp.where(reached, rel_v[head : head + 1, code : code + 1], before)
                after = jnp.where(
                    reached, rel_v[head : head + 1, 16 + code : 17 + code], after
                )
            value = jnp.where(ahead > 0, after, before)
            bias[head, rows, :] = jnp.where(inside, value, -1e30)

    loads[2].wait()
    pl.semaphore_wait(barrier, RINGZ - 1 + 3 + SHARDS - 1)

    attn_spread = Spread(z, attn_rows, ag_send.at[0], ag_recv.at[0])
    ffn_spread = Spread(z, ffn_rows, ag_send.at[1], ag_recv.at[1])

    @pl.when(section == 0)
    def _():
        own_rows = attn_rows.at[:, 0]
        pltpu.make_async_copy(own_rows, own_rows, rows_sem.at[0]).wait()
        for far in (True, False):

            @pl.loop(0, PAIRS)
            def _(q):
                attn_spread.step(1, far, q)

    swaps = [
        copy_to(src, dst, swap_send.at[i], swap_recv.at[i], {"section": other})
        for i, (src, dst) in enumerate(
            (
                (w_gate.at[0], gate_w.at[y, x]),
                (w_up.at[0], up_w.at[y, x]),
                (w_down.at[0], down_w.at[y, x]),
            )
        )
    ]
    swaps.append(
        copy_to(ffn_gain, ffn_gain_v, swap_send.at[3], swap_recv.at[3], {"section": other})
    )
    for swap in swaps:
        swap.start()

    attn_chains = Chains(z, attn_parts, attn_landed, rs_send.at[0], rs_recv.at[0])
    ffn_chains = Chains(z, ffn_parts, ffn_landed, rs_send.at[1], rs_recv.at[1])
    weights = Weights(y, x, gate_w, up_w, down_w, w_send, w_recv)

    near = copy_to(
        handed, ffn_rows.at[:, 0], near_send.at[0], near_recv.at[0], {"section": other}
    )

    def run_spread(spread, ready, multiply):
        for hop in (2, 3):
            for far in (True, False):

                @pl.loop(0, PAIRS)
                def _(q):
                    spread.step(hop, far, q)

        ready()

        @pl.loop(0, 1)
        def _(q):
            multiply(q, 0)

        @pl.loop(0, PAIRS)
        def _(q):
            spread.step(4, True, q)

        @pl.loop(1, PAIRS)
        def _(q):
            multiply(q, 0)

    def prepare(rows_ref, gain, pair, place):
        blocks, rows, count = part(place)
        total = jnp.where(pair == 0, 0.0, lane_sums[rows, :])
        prepared = []
        for g in (2 * pair, 2 * pair + 1):
            value = rows_ref[g, blocks].reshape(count, COLS).astype(F32)
            for c in range(0, COLS, 128):
                piece = value[:, c : c + 128]
                total = total + piece * piece
            prepared.append((value * gain[:, group_cols(g)]).astype(BF16))
        lane_sums[rows, :] = total
        return prepared

    def scale_of(sums_of_lanes):
        total = jnp.sum(sums_of_lanes, axis=-1, keepdims=True)
        return lax.rsqrt(total * (1.0 / WIDTH) + EPS)

    def run_chains(chains, far, between, close):
        @pl.loop(0, PAIRS)
        def _(q):
            far(2 * q)
            far(2 * q + 1)
            chains.forward(1, True, q)
            chains.forward(2, False, q)

        between()

        @pl.loop(0, PAIRS)
        def _(q):
            close(2 * q)
            close(2 * q + 1)
            chains.forward(2, True, q)

        for hop, is_far in ((3, False), (3, True), (4, False), (4, True)):

            @pl.loop(0, PAIRS)
            def _(q):
                chains.forward(hop, is_far, q)

    def finish(chains, before, pass_on):
        for way in (0, 1):
            chains.move(way, 4, False, None).wait_recv()

        def add(q, total):
            for way in (0, 1):
                chains.move(way, 4, True, q).wait_recv()
            ready = []
            for g in (2 * q, 2 * q + 1):
                value = (before[g, 0].astype(F32) + chains.total(g)).astype(BF16)
                total = total + squares(value.astype(F32))
                ready.append((g, value))
            pass_on(q, ready)
            return total

        total = lax.fori_loop(0, PAIRS, add, no_squares)
        row_squares[...] = jnp.broadcast_to(total, row_squares.shape)

    def part(place):
        blocks = (0, NEAR) if place == 0 else (NEAR, RINGZ - NEAR)
        return pl.ds(*blocks), pl.ds(blocks[0] * ROWS, blocks[1] * ROWS), blocks[1] * ROWS

    def attention():
        def ready():
            for load in loads[3:6]:
                load.wait()

        def multiply(pair, place):
            prepared = prepare(attn_rows, attn_gain_v, pair, place)
            _, rows, _ = part(place)
            for n, weight in enumerate((query_w, key_w, value_w)):
                cols = slice(n * 256, (n + 1) * 256)
                product = jnp.where(pair == 0, 0.0, sums[rows, cols])
                for j in range(2):
                    product = product + jnp.dot(
                        prepared[j],
                        weight[group_cols(2 * pair + j), :],
                        preferred_element_type=F32,
                    )
                sums[rows, cols] = product

        run_spread(attn_spread, ready, multiply)
        attn_spread.land()

        @pl.loop(0, PAIRS)
        def _(pair):
            multiply(pair, 1)

        scale = scale_of(lane_sums[...])
        queries[...] = (sums[:, 0:256] * scale).astype(BF16)
        keys[...] = (sums[:, 256:512] * scale).astype(BF16)
        values[...] = (sums[:, 512:768] * scale).astype(BF16)

        def attend(place):
            _, rows, count = part(place)
            head_lane = lax.broadcasted_iota(jnp.int32, (count, 128), 1)

            @pl.loop(0, HEADS // 2)
            def _(pair):
                cols = pl.ds(pl.multiple_of(pair * 128, 128), 128)
                query_pair, key_pair, value_pair = queries[rows, cols], keys[:, cols], values[:, cols]
                results = []
                for sub in range(2):
                    mine = (head_lane >= 64) if sub else (head_lane < 64)
                    one = jnp.where(mine, query_pair.astype(F32), 0.0).astype(BF16)
                    scores = lax.dot_general(
                        one, key_pair, (((1,), (1,)), ((), ())), preferred_element_type=F32
                    )
                    scores = scores + bias[pair * 2 + sub, rows, :]
                    powers = jnp.exp(scores - jnp.max(scores, axis=-1, keepdims=True))
                    shares_of = powers / jnp.sum(powers, axis=-1, keepdims=True)
                    results.append(
                        jnp.dot(shares_of.astype(BF16), value_pair, preferred_element_type=F32)
                    )
                context[rows, cols] = jnp.where(head_lane < 64, results[0], results[1]).astype(BF16)

        def project(g, place):
            blocks, rows, count = part(place)
            product = jnp.dot(
                context[rows, :], out_w[:, group_cols(g)], preferred_element_type=F32
            )
            attn_parts[g, blocks] = product.astype(BF16).reshape(
                count // ROWS, ROWS, COLS
            )

        attend(1)
        loads[6].wait()
        run_chains(
            attn_chains, lambda g: project(g, 1), lambda: attend(0), lambda g: project(g, 0)
        )

        def start(far, q):
            for way in (0, 1):
                ffn_spread.move(way, 1, far, q, handed, other).start()

        def pass_on(q, ready):
            for g, value in ready:
                handed[g] = value
            start(True, q)

        finish(attn_chains, attn_rows, pass_on)

        @pl.loop(0, PAIRS)
        def _(q):
            start(False, q)

        near.start()

    def feed():
        def multiply(pair, place):
            prepared = prepare(ffn_rows, ffn_gain_v, pair, place)
            _, rows, _ = part(place)
            for n, weight in enumerate((gate_w, up_w)):
                cols = slice(n * HID, (n + 1) * HID)
                product = jnp.where(pair == 0, 0.0, sums[rows, cols])
                for j in range(2):
                    product = product + jnp.dot(
                        prepared[j],
                        weight[pair, 2 * j : 2 * j + 2].reshape(COLS, HID),
                        preferred_element_type=F32,
                    )
                sums[rows, cols] = product

        def activate(place):
            _, rows, _ = part(place)
            scale = scale_of(lane_sums[rows, :])
            gate = sums[rows, 0:HID] * scale
            up = sums[rows, HID : 2 * HID] * scale
            curve = jnp.tanh(0.7978845608 * (gate + 0.044715 * gate * gate * gate))
            hidden[rows, :] = (0.5 * gate * (1.0 + curve) * up).astype(BF16)

        def ready():
            near.wait_recv()
            swaps[3].wait_recv()
            weights.land((0, 1))

        run_spread(ffn_spread, ready, multiply)
        activate(0)
        ffn_spread.land()

        @pl.loop(0, PAIRS)
        def _(pair):
            multiply(pair, 1)

        activate(1)
        weights.land((2, 3))

        @pl.when(section == 1)
        def _():
            pl.semaphore_signal(free_sem, inc=1, device_id={"section": other}, device_id_type=MESH)

        def project(g, place):
            blocks, rows, count = part(place)
            for j in range(2):
                product = jnp.dot(
                    hidden[rows, :],
                    down_w[g // 2, 2 * lax.rem(g, 2) + j],
                    preferred_element_type=F32,
                )
                ffn_parts[g, blocks, :, j * DK : (j + 1) * DK] = product.astype(BF16).reshape(
                    count // ROWS, ROWS, DK
                )

        run_chains(ffn_chains, lambda g: project(g, 1), lambda: None, lambda g: project(g, 0))

        def pass_on(q, ready):
            @pl.when(section == 0)
            def _():
                for g, value in ready:
                    last[g] = value

            @pl.when(section == 1)
            def _():
                for g, value in ready:
                    attn_rows[g, 0] = value
                attn_spread.step(1, True, q)

        finish(ffn_chains, ffn_rows, pass_on)

        @pl.when(section == 1)
        def _():
            @pl.loop(0, PAIRS)
            def _(q):
                attn_spread.step(1, False, q)

    @pl.loop(0, 3)
    def _(turn):
        role = lax.rem(turn + section, 3)

        @pl.when(role == 0)
        def _():
            attention()

        @pl.when(role == 1)
        def _():
            @pl.when(section == 0)
            def _():
                pl.semaphore_wait(free_sem, 1)

            def ready(array):
                if array < 3:
                    swaps[array].wait_recv()

            weights.run(ready)

        @pl.when(role == 2)
        def _():
            feed()

    def leave():
        for swap in swaps:
            swap.wait_send()
        weights.sent()
        near.wait_send()
        attn_spread.sent()
        ffn_spread.sent(handed)
        attn_chains.sent()
        ffn_chains.sent()

    for load in loads[7:]:
        load.wait()

    def pool_copy(k):
        to = lax.rem(z + k, RINGZ)
        return copy_to(
            pooled.at[to], pooled_in.at[z], pool_send.at[0], pool_recv.at[0], {"tensor": to}
        )

    def share_copy(k):
        device = {"tensor": lax.rem(z + k, RINGZ)}
        return copy_to(shares.at[z], shares.at[z], share_send.at[0], share_recv.at[0], device)

    def place_copy(k):
        to = lax.rem(shard + k, SHARDS)
        return copy_to(
            placed.at[to], placed_in.at[shard], place_send.at[0], place_recv.at[0], {"shard": to}
        )

    others = pl.ds(0, RINGZ - 1)
    all_pool = copy_to(
        pooled.at[others], pooled_in.at[others], pool_send.at[0], pool_recv.at[0], {"tensor": z}
    )
    all_share = copy_to(
        shares.at[others], shares.at[others], share_send.at[0], share_recv.at[0], {"tensor": z}
    )
    rest = pl.ds(0, SHARDS - 1)
    all_place = copy_to(
        placed.at[rest], placed_in.at[rest], place_send.at[0], place_recv.at[0], {"shard": shard}
    )
    unit_copy = copy_to(units, units, unit_send.at[0], unit_recv.at[0], {"section": other})

    @pl.when(section == 0)
    def _():
        scale = row_scale()

        def pool(g):
            finished = last[g].astype(F32) * scale * final_gain_v[:, group_cols(g)]
            return jnp.dot(
                member_here[...], finished, precision=HIGHEST, preferred_element_type=F32
            )

        def stacked(value):
            cut = value.shape[1] // 2
            return jnp.concatenate([value[:, :cut], value[:, cut:]], axis=0).astype(BF16)

        for k in (4, 3, 5, 2, 6, 1, 7):
            to = lax.rem(z + k, RINGZ)
            pooled[to] = stacked(pool(to))
            pool_copy(k).start()
        pooled_in[z] = stacked(pool(z))
        leave()
        all_pool.wait_recv()
        whole = jnp.sum(pooled_in[...].astype(F32), axis=0)
        whole = jnp.concatenate([whole[:PPM], whole[PPM:]], axis=1)
        means = (whole / counts).astype(BF16)
        shares[z] = stacked(jnp.dot(means, proj_w[...], preferred_element_type=F32))
        for k in (4, 3, 5, 2, 6, 1, 7):
            share_copy(k).start()
        all_pool.wait_send()
        all_share.wait_recv()
        projected = jnp.sum(shares[...].astype(F32), axis=0)
        projected = jnp.concatenate([projected[:PPM], projected[PPM:]], axis=1)
        mean_square = jnp.mean(projected * projected, axis=-1, keepdims=True)
        units[...] = (projected * lax.rsqrt(mean_square + EPS)).astype(BF16).astype(F32)
        unit_copy.start()

    @pl.when(section == 1)
    def _():
        leave()
        unit_copy.wait_recv()

    row = lax.broadcasted_iota(jnp.int32, (SHARDS * 8, PPM), 0)
    chosen = (dest_shard_v[...] == (row >> 3) + section * SHARDS) & (dest_slot_v[...] == (row & 3))
    chosen = chosen.astype(F32)
    lower = jnp.dot(chosen, units[:, :HALF], preferred_element_type=F32)
    upper = jnp.dot(chosen, units[:, HALF:], preferred_element_type=F32)
    row = lax.broadcasted_iota(jnp.int32, (SHARDS * 8, HALF), 0)
    placed[...] = jnp.where((row & 7) < 4, lower, upper).reshape(SHARDS, 8, HALF)

    @pl.loop(1, SHARDS)
    def _(k):
        place_copy(k).start()

    placed_in[shard] = placed[shard]

    @pl.when(section == 0)
    def _():
        all_share.wait_send()
        unit_copy.wait_send()

    all_place.wait_send()
    all_place.wait_recv()
    rows = jnp.sum(placed_in[...], axis=0)
    index[:, 0:HALF] = rows[0:4].astype(BF16)
    index[:, HALF:EMB] = rows[4:8].astype(BF16)


def on_device(
    embeds,
    segments,
    rel_table,
    attn_gain,
    w_query,
    w_key,
    w_value,
    w_out,
    ffn_gain,
    w_gate,
    w_up,
    w_down,
    final_gain,
    w_proj,
    dest_shard,
    dest_slot,
):
    vmem = pl.BlockSpec(memory_space=pltpu.VMEM)
    anywhere = pl.BlockSpec(memory_space=pl.ANY)
    dma = pltpu.SemaphoreType.DMA
    rows = pltpu.VMEM((GROUPS, RINGZ, ROWS, COLS), BF16)
    landed = pltpu.VMEM((2, 4, GROUPS, ROWS, COLS), BF16)
    own = pltpu.VMEM((GROUPS, ROWS, COLS), BF16)
    heads = pltpu.VMEM((SEQ, 256), BF16)
    scratch = [
        pltpu.VMEM((1, SEQ), jnp.int32),
        pltpu.VMEM((HEADS, 32), F32),
        pltpu.VMEM((1, WIDTH), F32),
        pltpu.VMEM((1, WIDTH), F32),
        pltpu.VMEM((1, WIDTH), F32),
        pltpu.VMEM((1, PPM), jnp.int32),
        pltpu.VMEM((1, PPM), jnp.int32),
        pltpu.VMEM((WIDTH, 256), BF16),
        pltpu.VMEM((WIDTH, 256), BF16),
        pltpu.VMEM((WIDTH, 256), BF16),
        pltpu.VMEM((256, WIDTH), BF16),
        pltpu.VMEM((COLS, EMB), BF16),
        pltpu.VMEM((SIDE, SIDE, DK, HID), BF16),
        pltpu.VMEM((SIDE, SIDE, DK, HID), BF16),
        pltpu.VMEM((SIDE, SIDE, HID, DK), BF16),
        pltpu.VMEM((HEADS, SEQ, SEQ), F32),
        pltpu.VMEM((PPM, ROWS), F32),
        rows,
        rows,
        landed,
        rows,
        rows,
        landed,
        own,
        own,
        pltpu.VMEM((SEQ, 128), F32),
        heads,
        heads,
        heads,
        heads,
        pltpu.VMEM((SEQ, 2 * HID), F32),
        pltpu.VMEM((SEQ, HID), BF16),
        pltpu.VMEM((RINGZ, 2 * PPM, COLS // 2), BF16),
        pltpu.VMEM((RINGZ, 2 * PPM, COLS // 2), BF16),
        pltpu.VMEM((RINGZ, 2 * PPM, HALF), BF16),
        pltpu.VMEM((PPM, EMB), F32),
        pltpu.VMEM((ROWS, 128), F32),
        pltpu.VMEM((SHARDS, 8, HALF), F32),
        pltpu.VMEM((SHARDS, 8, HALF), F32),
        dma((11,)),
        dma((1,)),
        dma((4,)),
        dma((4,)),
        dma((1,)),
        dma((1,)),
        dma((2, 2, 7)),
        dma((2, 2, 22)),
        dma((2, 2, 7)),
        dma((2, 2, 25)),
        dma((4, 4)),
        dma((4, 12)),
        dma((1,)),
        dma((1,)),
        dma((1,)),
        dma((1,)),
        dma((1,)),
        dma((1,)),
        dma((1,)),
        dma((1,)),
        pltpu.SemaphoreType.REGULAR,
    ]
    return pl.pallas_call(
        kernel,
        out_shape=jax.ShapeDtypeStruct((4, EMB), BF16),
        in_specs=[anywhere] * 16,
        out_specs=vmem,
        scratch_shapes=scratch,
        compiler_params=pltpu.CompilerParams(
            collective_id=0, has_side_effects=True, vmem_limit_bytes=58 * 1024 * 1024
        ),
    )(
        embeds,
        segments,
        rel_table.T,
        attn_gain,
        w_query,
        w_key,
        w_value,
        w_out,
        ffn_gain,
        w_gate,
        w_up,
        w_down,
        final_gain.reshape(1, -1),
        w_proj,
        dest_shard,
        dest_slot,
    )


def solution(mesh):
    in_specs = (
        P("shard", "tensor", None),
        P("shard", None),
        P(None, "tensor"),
        P("section", None),
        P("section", None, "tensor"),
        P("section", None, "tensor"),
        P("section", None, "tensor"),
        P("section", "tensor", None),
        P("section", None),
        P("section", "shard", "tensor"),
        P("section", "shard", "tensor"),
        P("section", "tensor", "shard"),
        P(),
        P("tensor", None),
        P("shard", None),
        P("shard", None),
    )
    out_specs = P(("section", "shard"), None)
    return jax.shard_map(
        on_device, mesh=mesh, in_specs=in_specs, out_specs=out_specs, check_vma=False
    )
```

```python
import jax
import jax.numpy as jnp
from jax import lax
from jax.experimental import pallas as pl
from jax.experimental.pallas import tpu as pltpu
from jax.sharding import PartitionSpec as P

MESH = pl.DeviceIdType.MESH
F32 = jnp.float32
BF16 = jnp.bfloat16
HIGHEST = lax.Precision.HIGHEST

ROWS = 32
CHUNK = 16
RINGZ = 8
SIDE = 4
SHARDS = SIDE * SIDE
WIDTH = 4096
GROUPS = 8
COLS = WIDTH // GROUPS
PAIRS = GROUPS // 2
SEQ = 256
NEAR = 5
HEADS = 4
PPM = 8
DK = 256
HID = 640
EMB = 768
HALF = EMB // 2
EPS = 1e-06

ORDER = (0, 1, 7, 2, 6, 3, 5, 4)
PLACE = tuple(ORDER.index(slot) for slot in range(RINGZ))
lowest = (0, 1, 2, 3, 4, 5, 6, 7, 8, 12, 16, 23, 32, 46, 64, 91)


def copy_to(src, dst, send, recv, device):
    return pltpu.make_async_remote_copy(
        src_ref=src,
        dst_ref=dst,
        send_sem=send,
        recv_sem=recv,
        device_id=device,
        device_id_type=MESH,
    )


def part_rows(half):
    return pl.ds(half * CHUNK, CHUNK)


def group_cols(g):
    return pl.ds(pl.multiple_of(g * COLS, COLS), COLS)


class Spread:
    def __init__(self, z, rows, send, recv):
        self.beside = (lax.rem(z + 1, RINGZ), lax.rem(z + RINGZ - 1, RINGZ))
        self.rows, self.send, self.recv = rows, send, recv

    def move(self, way, hop, far, q, src=None, section=None):
        source, target = (RINGZ - hop + 1, RINGZ - hop) if way == 0 else (hop - 1, hop)
        rows = part_rows(way if far else 1 - way)
        groups = pl.ds(0, GROUPS) if q is None else pl.ds(2 * q, 2)
        if src is None:
            src = self.rows.at[groups, PLACE[source % RINGZ], rows]
        else:
            src = src.at[groups, rows]
        device = {"tensor": self.beside[way]}
        if section is not None:
            device["section"] = section
        if hop < 3 or (hop == 3 and far):
            at = (hop - 1) * 8 + (0 if far else 4) + (0 if q is None else q)
        else:
            at = 20 if hop == 3 else 21
        return copy_to(
            src,
            self.rows.at[groups, PLACE[target % RINGZ], rows],
            self.send.at[way, 2 * hop - (2 if far else 1)],
            self.recv.at[way, at],
            device,
        )

    def step(self, hop, far, q):
        for way in (0, 1):
            if hop > 1:
                self.move(way, hop - 1, far, q).wait_recv()
            self.move(way, hop, far, q).start()

    def land(self):
        for way in (0, 1):
            self.move(way, 3, False, None).wait_recv()
        for way in (0, 1):
            self.move(way, 4, True, None).wait_recv()

    def sent(self, src=None):
        for way in (0, 1):
            for hop in (1, 2, 3, 4):
                for far in (True, False)[: 2 if hop < 4 else 1]:
                    self.move(way, hop, far, None, src if hop == 1 else None).wait_send()


class Chains:
    def __init__(self, z, parts, landed, send, recv):
        self.beside = (lax.rem(z + 1, RINGZ), lax.rem(z + RINGZ - 1, RINGZ))
        self.parts, self.landed, self.send, self.recv = parts, landed, send, recv

    def place(self, way, hop):
        return PLACE[5 - hop if way == 0 else RINGZ - 5 + hop]

    def move(self, way, hop, far, q):
        rows = part_rows(way if far else 1 - way)
        groups = pl.ds(0, GROUPS) if q is None else pl.ds(2 * q, 2)
        kind = 2 * hop - (2 if far else 1)
        kind = kind - 1 if hop > 1 else kind
        at = kind * 4 + (0 if q is None or kind == 6 else q)
        return copy_to(
            self.parts.at[groups, self.place(way, hop), rows],
            self.landed.at[way, hop - 1, groups, rows],
            self.send.at[way, kind],
            self.recv.at[way, at],
            {"tensor": self.beside[way]},
        )

    def forward(self, hop, far, q):
        for way in (0, 1):
            if hop > (1 if far else 2):
                self.move(way, hop - 1, far, q).wait_recv()
                place = self.place(way, hop)
                rows = part_rows(way if far else 1 - way)
                groups = pl.ds(2 * q, 2)
                total = self.parts[groups, place, rows].astype(F32) + self.landed[
                    way, hop - 2, groups, rows
                ].astype(F32)
                self.parts[groups, place, rows] = total.astype(BF16)
            self.move(way, hop, far, q).start()

    def total(self, g):
        own = self.parts[g, 0].astype(F32)
        return own + self.landed[0, 3, g].astype(F32) + self.landed[1, 3, g].astype(F32)

    def sent(self):
        for way in (0, 1):
            for hop in (1, 2, 3, 4):
                for far in (True, False)[: 2 if hop > 1 else 1]:
                    self.move(way, hop, far, None).wait_send()


class Weights:
    def __init__(self, y, x, gate, up, down, send, recv):
        self.y, self.x = y, x
        self.arrays = ((gate, 0, DK), (up, 0, DK), (down, 0, HID // 2), (down, HID // 2, HID // 2))
        self.send, self.recv = send, recv

    def piece(self, array, first, second, sign):
        ref, start, size = self.arrays[array]
        if sign is not None:
            size = size // 2
            start = start + sign * size
        along_x, along_y = (first, second) if array % 2 == 0 else (second, first)
        at_x, at_y = lax.rem(self.x + along_x, SIDE), lax.rem(self.y + along_y, SIDE)
        return ref.at[at_y, at_x, pl.ds(start, size)]

    def all_of(self, array, stage, hop):
        ref, start, size = self.arrays[array]
        rows = pl.ds(start, size if hop == 0 else size // 2)
        ref = ref.at[0, pl.ds(0, 2), rows] if stage == 0 else ref.at[pl.ds(0, 2), :, rows]
        return copy_to(
            ref,
            ref,
            self.send.at[array, stage * 2 + hop],
            self.recv.at[array, 2 if stage == 0 else 11],
            {"shard": self.y * SIDE + self.x},
        )

    def copy(self, array, stage, hop, line, sign, landing):
        step = 1 if sign == 0 else SIDE - 1
        back = SIDE - step
        away = (back if hop == 1 else 0) + (back if landing else 0)
        if stage == 0:
            ref = self.piece(array, away % SIDE, 0, None if hop == 0 else sign)
            at = sign if hop == 0 else 2
        else:
            ref = self.piece(array, line, away % SIDE, None if hop == 0 else sign)
            at = 3 + line * 2 + sign if hop == 0 and array < 2 else 11
        on_x = (array % 2 == 0) == (stage == 0)
        if on_x:
            shard = self.y * SIDE + lax.rem(self.x + step, SIDE)
        else:
            shard = lax.rem(self.y + step, SIDE) * SIDE + self.x
        return copy_to(
            ref,
            ref,
            self.send.at[array, stage * 2 + hop],
            self.recv.at[array, at],
            {"shard": shard},
        )

    def go(self, array, stage, hop, line, sign):
        self.copy(array, stage, hop, line, sign, False).start()

    def wait(self, array, stage, hop, line, sign):
        self.copy(array, stage, hop, line, sign, True).wait_recv()

    def direct(self, array, stage, line):
        ref = self.piece(array, line, 0, None)
        if (array % 2 == 0) == (stage == 0):
            shard = self.y * SIDE + lax.rem(self.x + 2, SIDE)
        else:
            shard = lax.rem(self.y + 2, SIDE) * SIDE + self.x
        return copy_to(
            ref,
            ref,
            self.send.at[array, stage * 2 + 1],
            self.recv.at[array, 2 if stage == 0 else 11],
            {"shard": shard},
        )

    def second(self, array, line):
        for sign in (0, 1):
            self.go(array, 1, 0, line, sign)
        if array >= 2:
            self.direct(array, 1, line).start()

    def run(self, ready):
        def begin(arrays):
            for array in arrays:
                ready(array)
                for sign in (0, 1):
                    self.go(array, 0, 0, 0, sign)
                if array >= 2:
                    self.direct(array, 0, 0).start()
                self.second(array, 0)

        def along(line):
            for array in (0, 1):
                for sign in (0, 1):
                    self.wait(array, 1, 0, line, sign)
                    self.go(array, 1, 1, line, sign)

        begin((0, 1))
        for array in (0, 1):
            for sign in (0, 1):
                self.wait(array, 0, 0, 0, sign)
                self.go(array, 0, 1, 0, sign)
                self.second(array, SIDE - 1 if sign == 0 else 1)
        for array in (0, 1):
            self.all_of(array, 0, 1).wait_recv()
            self.second(array, 2)
        along(0)
        begin((2, 3))
        for line in (1, 3, 2):
            along(line)
        for array in (2, 3):
            for sign in (0, 1):
                self.wait(array, 0, 0, 0, sign)
                self.second(array, SIDE - 1 if sign == 0 else 1)
            self.all_of(array, 0, 1).wait_recv()
            self.second(array, 2)

    def land(self, arrays):
        for array in arrays:
            if array < 2:
                self.all_of(array, 1, 1).wait_recv()
            else:
                ref, start, size = self.arrays[array]
                ref = ref.at[pl.ds(0, 3), :, pl.ds(start, size)]
                copy_to(
                    ref,
                    ref,
                    self.send.at[array, 2],
                    self.recv.at[array, 11],
                    {"shard": self.y * SIDE + self.x},
                ).wait_recv()

    def sent(self):
        for array in range(4):
            for stage in (0, 1):
                for hop in (0, 1):
                    self.all_of(array, stage, hop).wait_send()


def kernel(
    embeds,
    segments,
    rel_table,
    attn_gain,
    w_query,
    w_key,
    w_value,
    w_out,
    ffn_gain,
    w_gate,
    w_up,
    w_down,
    final_gain,
    w_proj,
    dest_shard,
    dest_slot,
    index,
    segments_v,
    rel_v,
    attn_gain_v,
    ffn_gain_v,
    final_gain_v,
    dest_shard_v,
    dest_slot_v,
    query_w,
    key_w,
    value_w,
    out_w,
    proj_w,
    gate_w,
    up_w,
    down_w,
    bias,
    member_here,
    attn_rows,
    attn_parts,
    attn_landed,
    ffn_rows,
    ffn_parts,
    ffn_landed,
    handed,
    last,
    lane_sums,
    queries,
    keys,
    values,
    context,
    sums,
    hidden,
    pooled,
    pooled_in,
    shares,
    units,
    row_squares,
    placed,
    placed_in,
    load_sem,
    rows_sem,
    swap_send,
    swap_recv,
    near_send,
    near_recv,
    ag_send,
    ag_recv,
    rs_send,
    rs_recv,
    w_send,
    w_recv,
    pool_send,
    pool_recv,
    share_send,
    share_recv,
    unit_send,
    unit_recv,
    place_send,
    place_recv,
    free_sem,
):
    section = lax.axis_index("section")
    z = lax.axis_index("tensor")
    shard = lax.axis_index("shard")
    y, x = shard // SIDE, lax.rem(shard, SIDE)
    other = 1 - section

    barrier = pltpu.get_barrier_semaphore()

    def greet(device):
        pl.semaphore_signal(barrier, inc=1, device_id=device, device_id_type=MESH)

    @pl.loop(1, RINGZ)
    def _(k):
        greet({"tensor": lax.rem(z + k, RINGZ)})

    for k in (0, 1, RINGZ - 1):
        greet({"section": other, "tensor": lax.rem(z + k, RINGZ)})

    @pl.loop(1, SHARDS)
    def _(k):
        greet({"shard": lax.rem(shard + k, SHARDS)})

    sources = (
        (segments, segments_v),
        (rel_table, rel_v),
        (attn_gain, attn_gain_v),
        (w_query.at[0], query_w),
        (w_key.at[0], key_w),
        (w_value.at[0], value_w),
        (w_out.at[0], out_w),
        (final_gain, final_gain_v),
        (dest_shard, dest_shard_v),
        (dest_slot, dest_slot_v),
        (w_proj, proj_w),
    )
    loads = [
        pltpu.make_async_copy(src, dst, load_sem.at[i]) for i, (src, dst) in enumerate(sources)
    ]
    first_rows = [
        pltpu.make_async_copy(
            embeds.at[0, :, pl.ds(g * COLS, COLS)], attn_rows.at[g, 0], rows_sem.at[0]
        )
        for g in range(GROUPS)
    ]
    for load in loads[:3]:
        load.start()

    @pl.when(section == 0)
    def _():
        for load in first_rows:
            load.start()

    for load in loads[3:]:
        load.start()
    for load in loads[:2]:
        load.wait()

    def squares(value):
        return jnp.sum(value * value, axis=-1, keepdims=True)

    def row_scale():
        return lax.rsqrt(row_squares[:, 0:1] * (1.0 / WIDTH) + EPS)

    no_squares = jnp.zeros((ROWS, 1), F32)

    passage = lax.broadcasted_iota(jnp.int32, (PPM, SEQ), 0)
    counts = jnp.sum((segments_v[...] == passage).astype(F32), axis=-1, keepdims=True)
    first = jnp.sum((segments_v[...] < passage).astype(F32), axis=-1, keepdims=True)

    def members(token):
        at = token.astype(F32)
        return ((at >= first) & (at < first + counts)).astype(F32)

    lane = lax.broadcasted_iota(jnp.int32, (PPM, ROWS), 1)
    member_here[...] = members(lane + z * ROWS)

    def slots(place):
        slot = jnp.full_like(place, ORDER[0])
        for at in range(1, RINGZ):
            slot = jnp.where(place == at, ORDER[at], slot)
        return slot

    def tokens(position):
        return (((slots(position >> 5) + z) & 7) << 5) + (position & 31)

    lane = lax.broadcasted_iota(jnp.int32, (PPM, SEQ), 1)
    member = members(tokens(lane)).astype(BF16)
    bias[0] = lax.dot_general(
        member, member, (((0,), (0,)), ((), ())), preferred_element_type=F32
    )

    @pl.loop(0, RINGZ)
    def _(block):
        rows = pl.ds(pl.multiple_of(block * ROWS, ROWS), ROWS)
        inside = bias[0, rows, :] > 0.5
        i = tokens(lax.broadcasted_iota(jnp.int32, (ROWS, SEQ), 0) + block * ROWS)
        k = tokens(lax.broadcasted_iota(jnp.int32, (ROWS, SEQ), 1))
        ahead = k - i
        distance = jnp.abs(ahead)
        for head in range(HEADS):
            before = jnp.broadcast_to(rel_v[head : head + 1, 0:1], (ROWS, SEQ))
            after = jnp.broadcast_to(rel_v[head : head + 1, 16:17], (ROWS, SEQ))
            for code in range(1, 16):
                reached = distance >= lowest[code]
                before = jnp.where(reached, rel_v[head : head + 1, code : code + 1], before)
                after = jnp.where(
                    reached, rel_v[head : head + 1, 16 + code : 17 + code], after
                )
            value = jnp.where(ahead > 0, after, before)
            bias[head, rows, :] = jnp.where(inside, value, -1e30)

    loads[2].wait()
    pl.semaphore_wait(barrier, RINGZ - 1 + 3 + SHARDS - 1)

    attn_spread = Spread(z, attn_rows, ag_send.at[0], ag_recv.at[0])
    ffn_spread = Spread(z, ffn_rows, ag_send.at[1], ag_recv.at[0])

    @pl.when(section == 0)
    def _():
        own_rows = attn_rows.at[:, 0]
        pltpu.make_async_copy(own_rows, own_rows, rows_sem.at[0]).wait()
        for far in (True, False):

            @pl.loop(0, PAIRS)
            def _(q):
                attn_spread.step(1, far, q)

    swaps = [
        copy_to(src, dst, swap_send.at[i], swap_recv.at[i], {"section": other})
        for i, (src, dst) in enumerate(
            (
                (w_gate.at[0], gate_w.at[y, x]),
                (w_up.at[0], up_w.at[y, x]),
                (w_down.at[0], down_w.at[y, x]),
            )
        )
    ]
    swaps.append(
        copy_to(ffn_gain, ffn_gain_v, swap_send.at[3], swap_recv.at[3], {"section": other})
    )
    for swap in swaps:
        swap.start()

    attn_chains = Chains(z, attn_parts, attn_landed, rs_send.at[0], rs_recv.at[0])
    ffn_chains = Chains(z, ffn_parts, ffn_landed, rs_send.at[1], rs_recv.at[0])
    weights = Weights(y, x, gate_w, up_w, down_w, w_send, w_recv)

    near = copy_to(
        handed, ffn_rows.at[:, 0], near_send.at[0], near_recv.at[0], {"section": other}
    )

    def run_spread(spread, ready, multiply):
        for hop in (2, 3):
            for far in (True, False):

                @pl.loop(0, PAIRS)
                def _(q):
                    spread.step(hop, far, q)

        ready()

        @pl.loop(0, 1)
        def _(q):
            multiply(q, 0)

        @pl.loop(0, PAIRS)
        def _(q):
            spread.step(4, True, q)

        @pl.loop(1, PAIRS)
        def _(q):
            multiply(q, 0)

    def prepare(rows_ref, gain, pair, place):
        blocks, rows, count = part(place)
        total = jnp.where(pair == 0, 0.0, lane_sums[rows, :])
        prepared = []
        for g in (2 * pair, 2 * pair + 1):
            value = rows_ref[g, blocks].reshape(count, COLS).astype(F32)
            for c in range(0, COLS, 128):
                piece = value[:, c : c + 128]
                total = total + piece * piece
            prepared.append((value * gain[:, group_cols(g)]).astype(BF16))
        lane_sums[rows, :] = total
        return prepared

    def scale_of(sums_of_lanes):
        total = jnp.sum(sums_of_lanes, axis=-1, keepdims=True)
        return lax.rsqrt(total * (1.0 / WIDTH) + EPS)

    def run_chains(chains, far, between, close):
        @pl.loop(0, PAIRS)
        def _(q):
            far(2 * q)
            far(2 * q + 1)
            chains.forward(1, True, q)
            chains.forward(2, False, q)

        between()

        @pl.loop(0, PAIRS)
        def _(q):
            close(2 * q)
            close(2 * q + 1)
            chains.forward(2, True, q)

        for hop, is_far in ((3, False), (3, True), (4, False), (4, True)):

            @pl.loop(0, PAIRS)
            def _(q):
                chains.forward(hop, is_far, q)

    def finish(chains, before, pass_on):
        for way in (0, 1):
            chains.move(way, 4, False, None).wait_recv()

        def add(q, total):
            for way in (0, 1):
                chains.move(way, 4, True, q).wait_recv()
            ready = []
            for g in (2 * q, 2 * q + 1):
                value = (before[g, 0].astype(F32) + chains.total(g)).astype(BF16)
                total = total + squares(value.astype(F32))
                ready.append((g, value))
            pass_on(q, ready)
            return total

        total = lax.fori_loop(0, PAIRS, add, no_squares)
        row_squares[...] = jnp.broadcast_to(total, row_squares.shape)

    def part(place):
        blocks = (0, NEAR) if place == 0 else (NEAR, RINGZ - NEAR)
        return pl.ds(*blocks), pl.ds(blocks[0] * ROWS, blocks[1] * ROWS), blocks[1] * ROWS

    def attention():
        def ready():
            for load in loads[3:6]:
                load.wait()

        def multiply(pair, place):
            prepared = prepare(attn_rows, attn_gain_v, pair, place)
            _, rows, _ = part(place)
            for n, weight in enumerate((query_w, key_w, value_w)):
                cols = slice(n * 256, (n + 1) * 256)
                product = jnp.where(pair == 0, 0.0, sums[rows, cols])
                for j in range(2):
                    product = product + jnp.dot(
                        prepared[j],
                        weight[group_cols(2 * pair + j), :],
                        preferred_element_type=F32,
                    )
                sums[rows, cols] = product

        run_spread(attn_spread, ready, multiply)
        attn_spread.land()

        @pl.loop(0, PAIRS)
        def _(pair):
            multiply(pair, 1)

        scale = scale_of(lane_sums[...])
        queries[...] = (sums[:, 0:256] * scale).astype(BF16)
        keys[...] = (sums[:, 256:512] * scale).astype(BF16)
        values[...] = (sums[:, 512:768] * scale).astype(BF16)

        def attend(place):
            _, rows, count = part(place)
            head_lane = lax.broadcasted_iota(jnp.int32, (count, 128), 1)

            @pl.loop(0, HEADS // 2)
            def _(pair):
                cols = pl.ds(pl.multiple_of(pair * 128, 128), 128)
                query_pair, key_pair, value_pair = queries[rows, cols], keys[:, cols], values[:, cols]
                results = []
                for sub in range(2):
                    mine = (head_lane >= 64) if sub else (head_lane < 64)
                    one = jnp.where(mine, query_pair.astype(F32), 0.0).astype(BF16)
                    scores = lax.dot_general(
                        one, key_pair, (((1,), (1,)), ((), ())), preferred_element_type=F32
                    )
                    scores = scores + bias[pair * 2 + sub, rows, :]
                    powers = jnp.exp(scores - jnp.max(scores, axis=-1, keepdims=True))
                    shares_of = powers / jnp.sum(powers, axis=-1, keepdims=True)
                    results.append(
                        jnp.dot(shares_of.astype(BF16), value_pair, preferred_element_type=F32)
                    )
                context[rows, cols] = jnp.where(head_lane < 64, results[0], results[1]).astype(BF16)

        def project(g, place):
            blocks, rows, count = part(place)
            product = jnp.dot(
                context[rows, :], out_w[:, group_cols(g)], preferred_element_type=F32
            )
            attn_parts[g, blocks] = product.astype(BF16).reshape(
                count // ROWS, ROWS, COLS
            )

        attend(1)
        loads[6].wait()
        run_chains(
            attn_chains, lambda g: project(g, 1), lambda: attend(0), lambda g: project(g, 0)
        )

        def start(far, q):
            for way in (0, 1):
                ffn_spread.move(way, 1, far, q, handed, other).start()

        def pass_on(q, ready):
            for g, value in ready:
                handed[g] = value
            start(True, q)

        finish(attn_chains, attn_rows, pass_on)

        @pl.loop(0, PAIRS)
        def _(q):
            start(False, q)

        near.start()

    def feed():
        def multiply(pair, place):
            prepared = prepare(ffn_rows, ffn_gain_v, pair, place)
            _, rows, _ = part(place)
            for n, weight in enumerate((gate_w, up_w)):
                cols = slice(n * HID, (n + 1) * HID)
                product = jnp.where(pair == 0, 0.0, sums[rows, cols])
                for j in range(2):
                    product = product + jnp.dot(
                        prepared[j],
                        weight[pair, 2 * j : 2 * j + 2].reshape(COLS, HID),
                        preferred_element_type=F32,
                    )
                sums[rows, cols] = product

        def activate(place):
            _, rows, _ = part(place)
            scale = scale_of(lane_sums[rows, :])
            gate = sums[rows, 0:HID] * scale
            up = sums[rows, HID : 2 * HID] * scale
            curve = jnp.tanh(0.7978845608 * (gate + 0.044715 * gate * gate * gate))
            hidden[rows, :] = (0.5 * gate * (1.0 + curve) * up).astype(BF16)

        def ready():
            near.wait_recv()
            swaps[3].wait_recv()
            weights.land((0, 1))

        run_spread(ffn_spread, ready, multiply)
        activate(0)
        ffn_spread.land()

        @pl.loop(0, PAIRS)
        def _(pair):
            multiply(pair, 1)

        activate(1)
        weights.land((2, 3))

        @pl.when(section == 1)
        def _():
            pl.semaphore_signal(free_sem, inc=1, device_id={"section": other}, device_id_type=MESH)

        def project(g, place):
            blocks, rows, count = part(place)
            for j in range(2):
                product = jnp.dot(
                    hidden[rows, :],
                    down_w[g // 2, 2 * lax.rem(g, 2) + j],
                    preferred_element_type=F32,
                )
                ffn_parts[g, blocks, :, j * DK : (j + 1) * DK] = product.astype(BF16).reshape(
                    count // ROWS, ROWS, DK
                )

        run_chains(ffn_chains, lambda g: project(g, 1), lambda: None, lambda g: project(g, 0))

        def pass_on(q, ready):
            @pl.when(section == 0)
            def _():
                for g, value in ready:
                    last[g] = value

            @pl.when(section == 1)
            def _():
                for g, value in ready:
                    attn_rows[g, 0] = value
                attn_spread.step(1, True, q)

        finish(ffn_chains, ffn_rows, pass_on)

        @pl.when(section == 1)
        def _():
            @pl.loop(0, PAIRS)
            def _(q):
                attn_spread.step(1, False, q)

    @pl.loop(0, 3)
    def _(turn):
        role = lax.rem(turn + section, 3)

        @pl.when(role == 0)
        def _():
            attention()

        @pl.when(role == 1)
        def _():
            @pl.when(section == 0)
            def _():
                pl.semaphore_wait(free_sem, 1)

            def ready(array):
                if array < 3:
                    swaps[array].wait_recv()

            weights.run(ready)

        @pl.when(role == 2)
        def _():
            feed()

    def leave():
        for swap in swaps:
            swap.wait_send()
        weights.sent()
        near.wait_send()
        attn_spread.sent()
        ffn_spread.sent(handed)
        attn_chains.sent()
        ffn_chains.sent()

    for load in loads[7:]:
        load.wait()

    def pool_copy(k):
        to = lax.rem(z + k, RINGZ)
        return copy_to(
            pooled.at[to], pooled_in.at[z], pool_send.at[0], pool_recv.at[0], {"tensor": to}
        )

    def share_copy(k):
        device = {"tensor": lax.rem(z + k, RINGZ)}
        return copy_to(shares.at[z], shares.at[z], share_send.at[0], share_recv.at[0], device)

    def place_copy(k):
        to = lax.rem(shard + k, SHARDS)
        return copy_to(
            placed.at[to], placed_in.at[shard], place_send.at[0], place_recv.at[0], {"shard": to}
        )

    others = pl.ds(0, RINGZ - 1)
    all_pool = copy_to(
        pooled.at[others], pooled_in.at[others], pool_send.at[0], pool_recv.at[0], {"tensor": z}
    )
    all_share = copy_to(
        shares.at[others], shares.at[others], share_send.at[0], share_recv.at[0], {"tensor": z}
    )
    rest = pl.ds(0, SHARDS - 1)
    all_place = copy_to(
        placed.at[rest], placed_in.at[rest], place_send.at[0], place_recv.at[0], {"shard": shard}
    )
    unit_copy = copy_to(units, units, unit_send.at[0], unit_recv.at[0], {"section": other})

    @pl.when(section == 0)
    def _():
        scale = row_scale()

        def pool(g):
            finished = last[g].astype(F32) * scale * final_gain_v[:, group_cols(g)]
            return jnp.dot(
                member_here[...], finished, precision=HIGHEST, preferred_element_type=F32
            )

        def stacked(value):
            cut = value.shape[1] // 2
            return jnp.concatenate([value[:, :cut], value[:, cut:]], axis=0).astype(BF16)

        for k in (4, 3, 5, 2, 6, 1, 7):
            to = lax.rem(z + k, RINGZ)
            pooled[to] = stacked(pool(to))
            pool_copy(k).start()
        pooled_in[z] = stacked(pool(z))
        leave()
        all_pool.wait_recv()
        whole = jnp.sum(pooled_in[...].astype(F32), axis=0)
        whole = jnp.concatenate([whole[:PPM], whole[PPM:]], axis=1)
        means = (whole / counts).astype(BF16)
        shares[z] = stacked(jnp.dot(means, proj_w[...], preferred_element_type=F32))
        for k in (4, 3, 5, 2, 6, 1, 7):
            share_copy(k).start()
        all_pool.wait_send()
        all_share.wait_recv()
        projected = jnp.sum(shares[...].astype(F32), axis=0)
        projected = jnp.concatenate([projected[:PPM], projected[PPM:]], axis=1)
        mean_square = jnp.mean(projected * projected, axis=-1, keepdims=True)
        units[...] = (projected * lax.rsqrt(mean_square + EPS)).astype(BF16).astype(F32)
        unit_copy.start()

    @pl.when(section == 1)
    def _():
        leave()
        unit_copy.wait_recv()

    row = lax.broadcasted_iota(jnp.int32, (SHARDS * 8, PPM), 0)
    chosen = (dest_shard_v[...] == (row >> 3) + section * SHARDS) & (dest_slot_v[...] == (row & 3))
    chosen = chosen.astype(F32)
    lower = jnp.dot(chosen, units[:, :HALF], preferred_element_type=F32)
    upper = jnp.dot(chosen, units[:, HALF:], preferred_element_type=F32)
    row = lax.broadcasted_iota(jnp.int32, (SHARDS * 8, HALF), 0)
    placed[...] = jnp.where((row & 7) < 4, lower, upper).reshape(SHARDS, 8, HALF)

    @pl.loop(1, SHARDS)
    def _(k):
        place_copy(k).start()

    placed_in[shard] = placed[shard]

    @pl.when(section == 0)
    def _():
        all_share.wait_send()
        unit_copy.wait_send()

    all_place.wait_send()
    all_place.wait_recv()
    rows = jnp.sum(placed_in[...], axis=0)
    index[:, 0:HALF] = rows[0:4].astype(BF16)
    index[:, HALF:EMB] = rows[4:8].astype(BF16)


def on_device(
    embeds,
    segments,
    rel_table,
    attn_gain,
    w_query,
    w_key,
    w_value,
    w_out,
    ffn_gain,
    w_gate,
    w_up,
    w_down,
    final_gain,
    w_proj,
    dest_shard,
    dest_slot,
):
    vmem = pl.BlockSpec(memory_space=pltpu.VMEM)
    anywhere = pl.BlockSpec(memory_space=pl.ANY)
    dma = pltpu.SemaphoreType.DMA
    rows = pltpu.VMEM((GROUPS, RINGZ, ROWS, COLS), BF16)
    landed = pltpu.VMEM((2, 4, GROUPS, ROWS, COLS), BF16)
    own = pltpu.VMEM((GROUPS, ROWS, COLS), BF16)
    heads = pltpu.VMEM((SEQ, 256), BF16)
    scratch = [
        pltpu.VMEM((1, SEQ), jnp.int32),
        pltpu.VMEM((HEADS, 32), F32),
        pltpu.VMEM((1, WIDTH), F32),
        pltpu.VMEM((1, WIDTH), F32),
        pltpu.VMEM((1, WIDTH), F32),
        pltpu.VMEM((1, PPM), jnp.int32),
        pltpu.VMEM((1, PPM), jnp.int32),
        pltpu.VMEM((WIDTH, 256), BF16),
        pltpu.VMEM((WIDTH, 256), BF16),
        pltpu.VMEM((WIDTH, 256), BF16),
        pltpu.VMEM((256, WIDTH), BF16),
        pltpu.VMEM((COLS, EMB), BF16),
        pltpu.VMEM((SIDE, SIDE, DK, HID), BF16),
        pltpu.VMEM((SIDE, SIDE, DK, HID), BF16),
        pltpu.VMEM((SIDE, SIDE, HID, DK), BF16),
        pltpu.VMEM((HEADS, SEQ, SEQ), F32),
        pltpu.VMEM((PPM, ROWS), F32),
        rows,
        rows,
        landed,
        rows,
        rows,
        landed,
        own,
        own,
        pltpu.VMEM((SEQ, 128), F32),
        heads,
        heads,
        heads,
        heads,
        pltpu.VMEM((SEQ, 2 * HID), F32),
        pltpu.VMEM((SEQ, HID), BF16),
        pltpu.VMEM((RINGZ, 2 * PPM, COLS // 2), BF16),
        pltpu.VMEM((RINGZ, 2 * PPM, COLS // 2), BF16),
        pltpu.VMEM((RINGZ, 2 * PPM, HALF), BF16),
        pltpu.VMEM((PPM, EMB), F32),
        pltpu.VMEM((ROWS, 128), F32),
        pltpu.VMEM((SHARDS, 8, HALF), F32),
        pltpu.VMEM((SHARDS, 8, HALF), F32),
        dma((11,)),
        dma((1,)),
        dma((4,)),
        dma((4,)),
        dma((1,)),
        dma((1,)),
        dma((2, 2, 7)),
        dma((1, 2, 22)),
        dma((2, 2, 7)),
        dma((1, 2, 25)),
        dma((4, 4)),
        dma((4, 12)),
        dma((1,)),
        dma((1,)),
        dma((1,)),
        dma((1,)),
        dma((1,)),
        dma((1,)),
        dma((1,)),
        dma((1,)),
        pltpu.SemaphoreType.REGULAR,
    ]
    return pl.pallas_call(
        kernel,
        out_shape=jax.ShapeDtypeStruct((4, EMB), BF16),
        in_specs=[anywhere] * 16,
        out_specs=vmem,
        scratch_shapes=scratch,
        compiler_params=pltpu.CompilerParams(
            collective_id=0, has_side_effects=True, vmem_limit_bytes=58 * 1024 * 1024
        ),
    )(
        embeds,
        segments,
        rel_table.T,
        attn_gain,
        w_query,
        w_key,
        w_value,
        w_out,
        ffn_gain,
        w_gate,
        w_up,
        w_down,
        final_gain.reshape(1, -1),
        w_proj,
        dest_shard,
        dest_slot,
    )


def solution(mesh):
    in_specs = (
        P("shard", "tensor", None),
        P("shard", None),
        P(None, "tensor"),
        P("section", None),
        P("section", None, "tensor"),
        P("section", None, "tensor"),
        P("section", None, "tensor"),
        P("section", "tensor", None),
        P("section", None),
        P("section", "shard", "tensor"),
        P("section", "shard", "tensor"),
        P("section", "tensor", "shard"),
        P(),
        P("tensor", None),
        P("shard", None),
        P("shard", None),
    )
    out_specs = P(("section", "shard"), None)
    return jax.shard_map(
        on_device, mesh=mesh, in_specs=in_specs, out_specs=out_specs, check_vma=False
    )
```
